32 devices in a mesh: seq: 8 (over z, x), mp: 4 (over y, core).
Axes of the slice: x: 2, y: 2, z: 4, core: 2. Of those that a mesh axis runs over, the one named last changes fastest.
Arguments:
- tokens: bfloat16 [2048, 2048], P('seq'), may hold values from -6 to 6
- gate_weight: bfloat16 [2048, 64, 64], P('seq', 'mp'), may hold values from -0.125 to 0.125
- input_weight: bfloat16 [2048, 64, 64], P('seq', 'mp'), may hold values from -0.125 to 0.125
- group_weight: bfloat16 [2048, 4, 2, 128], P('seq', 'mp'), may hold values from -0.125 to 0.125
- step_weight: bfloat16 [2048, 64], P('seq', 'mp'), may hold values from -0.0625 to 0.0625
- step_bias: float32 [64], P('mp'), may hold values from -3.91 to -1.5
- bucket_table: float32 [4, 64], P(None, 'mp'), may hold values from -1.2 to 2.5
- bucket_ids: int32 [2048], P('seq'), may hold values from 0 to 3, as said below
- decay_rate: float32 [64], P('mp'), may hold values from 0.00072753906 to 2.001
- conv_input: float32 [4, 64, 64], P(None, 'mp'), may hold values from -3 to 3
- conv_input_bias: float32 [64, 64], P('mp'), may hold values from -2 to 2
- conv_group: float32 [4, 4, 2, 128], P(None, 'mp'), may hold values from -3 to 3
- conv_group_bias: float32 [4, 2, 128], P('mp'), may hold values from -2 to 2
- skip_gain: float32 [64], P('mp'), may hold values from 0.5 to 1.5
- norm_gain: float32 [64, 64], P('mp'), may hold values from 0.1 to 1.9
- out_weight: bfloat16 [64, 64, 2048], P('mp'), may hold values from -0.09375 to 0.09375
Outputs:
- layer_out: bfloat16 [2048, 2048], P(('seq', 'mp'))
The draws below stay inside these ranges and needn't reach their ends.
Inputs may be any that keep to these rules, and one draw needn't show every extreme that they name: `bucket_ids`: exactly 3 tokens of the sequence have a bucket other than 0.
All inputs are finite; a program needn't handle non-finite values.
Results may differ from the reference program's by a relative error of at most 0.02.
Values may be sent and summed in bfloat16 or wider, within the bound.
No kernel may reach another device: no remote copies, remote signals or barrier semaphores. Data moves between devices by JAX's collectives and lax.ppermute only.
A program may use at most 128 MiB of HBM per device.

```python
import jax
import jax.numpy as jnp
from jax import lax

D = 2048
HEAD_DIM = 64
STATE = 128
GROUPS = 4
SHARD_ATTENDERS = 64
KCONV = 4
SPAN = 256
PLACE_BINS = 4
CLUSTER_ENTRIES = 3
CONTEXT_SPAN = 2048


def head_rates(key):
    share_key = jax.random.fold_in(key, 101)
    mask_key, step_key, fast_key, slow_key = jax.random.split(share_key, 4)
    fast_share = 0.5
    is_fast = jax.random.uniform(mask_key, (SHARD_ATTENDERS,), jnp.float32) < fast_share
    step_target = jnp.exp(jax.random.uniform(step_key, (SHARD_ATTENDERS,), jnp.float32, jnp.log(0.0201), jnp.log(0.199)))
    fast_rate = jnp.exp(jax.random.uniform(fast_key, (SHARD_ATTENDERS,), jnp.float32, jnp.log(1.0 / 40.0), jnp.log(1.0 / 25.0)))
    slow_rate = jnp.exp(jax.random.uniform(slow_key, (SHARD_ATTENDERS,), jnp.float32, jnp.log(0.3), jnp.log(1.5))) / CONTEXT_SPAN
    return (step_target, jnp.where(is_fast, fast_rate, slow_rate) / step_target)


def draw_decay_rate(key, part):
    return head_rates(key)[1]


def draw_step_bias(key, part):
    step_target = head_rates(key)[0]
    return jnp.log(jnp.expm1(step_target))


def draw_bucket_table(key, part):
    drawn_seed_handle, cluster_seed_handle = jax.random.split(jax.random.fold_in(key, 7))
    default_word_vector = jnp.clip(0.3 * jax.random.normal(drawn_seed_handle, (1, SHARD_ATTENDERS), jnp.float32), -1.2, 1.2)
    cluster_word_vectors = jax.random.uniform(cluster_seed_handle, (PLACE_BINS - 1, SHARD_ATTENDERS), jnp.float32, 1.0, 2.5)
    return jnp.concatenate([default_word_vector, cluster_word_vectors], axis=0)


def draw_bucket_ids(key, part):
    sampled_seed_handle, kind_key = jax.random.split(jax.random.fold_in(key, 13))
    sampled_indices = jax.random.permutation(sampled_seed_handle, CONTEXT_SPAN)[:CLUSTER_ENTRIES]
    entry_categories = 1 + jnp.arange(CLUSTER_ENTRIES, dtype=jnp.int32) % (PLACE_BINS - 1)
    entry_categories = jax.random.permutation(kind_key, entry_categories)
    return jnp.zeros((CONTEXT_SPAN,), jnp.int32).at[sampled_indices].set(entry_categories.astype(jnp.int32))


def block_scale(rng, shape, cuts, least, largest):
    level, own = 1.0, jax.random.fold_in(rng, 6)
    for position, blocks in cuts:
        draws = jnp.exp(jax.random.uniform(jax.random.fold_in(own, position), (blocks,), jnp.float32, least / len(cuts), largest / len(cuts)))
        level = level * jnp.repeat(draws, shape[position] // blocks).reshape([-1 if axis == position else 1 for axis in range(len(shape))])
    return level


def noise(stream_key, shape, scale, bound, pieces=(), kind=jnp.bfloat16):
    values = jax.random.normal(stream_key, shape, jnp.float32) * scale
    if len(pieces) > 0:
        values = block_scale(stream_key, shape, pieces, -0.22, 0.18) * values
    return jnp.clip(values, min=-bound, max=bound).astype(kind)


def setup_inputs(seed: int = 0) -> dict:
    keys = jax.random.split(jax.random.key(seed), 17)
    return {
        "tokens": noise(keys[0], (CONTEXT_SPAN, D), 1.0, 6.0, ((0, 8),)),
        "gate_weight": noise(keys[1], (D, SHARD_ATTENDERS, HEAD_DIM), D ** -0.5, 0.125, ((0, 8), (1, 4))),
        "input_weight": noise(keys[2], (D, SHARD_ATTENDERS, HEAD_DIM), D ** -0.5, 0.125, ((0, 8), (1, 4))),
        "group_weight": noise(keys[3], (D, GROUPS, 2, STATE), D ** -0.5, 0.125, ((0, 8), (1, 4))),
        "step_weight": noise(keys[4], (D, SHARD_ATTENDERS), (4 * D) ** -0.5, 0.0625, ((0, 8), (1, 4))),
        "step_bias": draw_step_bias(jax.random.fold_in(keys[16], 71), 0),
        "bucket_table": draw_bucket_table(jax.random.fold_in(keys[16], 71), 0),
        "bucket_ids": draw_bucket_ids(jax.random.fold_in(keys[16], 71), 0),
        "decay_rate": draw_decay_rate(jax.random.fold_in(keys[16], 71), 0),
        "conv_input": noise(keys[9], (KCONV, SHARD_ATTENDERS, HEAD_DIM), 0.5, 3.0, ((1, 4),), jnp.float32),
        "conv_input_bias": noise(keys[10], (SHARD_ATTENDERS, HEAD_DIM), 0.3, 2.0, ((0, 4),), jnp.float32),
        "conv_group": noise(keys[11], (KCONV, GROUPS, 2, STATE), 0.5, 3.0, ((1, 4),), jnp.float32),
        "conv_group_bias": noise(keys[12], (GROUPS, 2, STATE), 0.3, 2.0, ((0, 4),), jnp.float32),
        "skip_gain": jnp.clip(0.5 + 1.0 * jax.random.uniform(keys[13], (SHARD_ATTENDERS,), jnp.float32) ** block_scale(keys[13], (SHARD_ATTENDERS,), ((0, 4),), -0.2, 0.2), 0.5, 1.5),
        "norm_gain": jnp.clip(1.0 + 0.18 * jax.random.normal(keys[14], (SHARD_ATTENDERS, HEAD_DIM), jnp.float32), 0.1, 1.9),
        "out_weight": noise(keys[15], (SHARD_ATTENDERS, HEAD_DIM, D), (SHARD_ATTENDERS * HEAD_DIM) ** -0.5, 0.09375, ((0, 4),)),
    }


norm_epsilon = 1e-05
highest = lax.Precision.HIGHEST

def causal_conv(raw_rows, rim_rows, tap_weights, tap_bias):
    extended = jnp.concatenate([rim_rows, raw_rows], axis=0).astype(jnp.float32)
    row_count = raw_rows.shape[0]
    tap_count = tap_weights.shape[0]
    running = tap_bias[None, :] + tap_weights[tap_count - 1][None, :] * extended[tap_count - 1:tap_count - 1 + row_count]
    for tap_index in range(tap_count - 1):
        running = running + tap_weights[tap_index][None, :] * extended[tap_index:tap_index + row_count]
    return jax.nn.silu(running).astype(jnp.bfloat16)

def ssd_block(carried_state, block_inputs, decay_neg):
    block_values, block_b, block_c, block_steps = block_inputs
    step_rates = block_steps.astype(jnp.float32) * decay_neg[None, :]
    cumulative = jnp.cumsum(step_rates, axis=0)
    scores = jnp.dot(block_c, jnp.transpose(block_b), preferred_element_type=jnp.float32)
    by_head = jnp.transpose(cumulative)
    spread = by_head[:, :, None] - by_head[:, None, :]
    block_rows = block_values.shape[0]
    causal = (jnp.arange(block_rows)[:, None] >= jnp.arange(block_rows)[None, :])[None]
    decays = jnp.where(causal, jnp.exp(jnp.where(causal, spread, 0.0)), 0.0)
    mixing = scores[None] * decays
    driven = block_steps.astype(jnp.float32)[:, :, None] * block_values.astype(jnp.float32)
    within = jnp.einsum('rts,srp->trp', mixing, driven, precision=highest)
    readout = jnp.einsum('tn,rpn->trp', block_c.astype(jnp.float32), carried_state, precision=highest)
    outputs = within + jnp.exp(cumulative)[:, :, None] * readout
    remaining = jnp.exp(cumulative[-1][None, :] - cumulative)
    injected = jnp.einsum('srp,sn->rpn', driven * remaining[:, :, None], block_b.astype(jnp.float32), precision=highest)
    next_state = jnp.exp(cumulative[-1])[:, None, None] * carried_state + injected
    return (next_state, outputs)

def ssd_group(start_state, group_values, group_b, group_c, group_steps, decay_neg):
    row_total = group_values.shape[0]
    block_count = row_total // SPAN

    def advance(carried_state, block_inputs):
        return ssd_block(carried_state, block_inputs, decay_neg)
    blocked = (group_values.reshape((block_count, SPAN) + group_values.shape[1:]), group_b.reshape(block_count, SPAN, -1), group_c.reshape(block_count, SPAN, -1), group_steps.reshape(block_count, SPAN, -1))
    final_state, outputs = lax.scan(advance, start_state, blocked)
    return (final_state, outputs.reshape((row_total,) + outputs.shape[2:]))

def reference(tokens, gate_weight, input_weight, group_weight, step_weight, step_bias, bucket_table, bucket_ids, decay_rate, conv_input, conv_input_bias, conv_group, conv_group_bias, skip_gain, norm_gain, out_weight):
    seq_total = tokens.shape[0]
    model_width = tokens.shape[1]
    head_count = step_bias.shape[0]
    per_group = head_count // GROUPS
    head_size = gate_weight.shape[2]
    state_size = group_weight.shape[3]
    tap_count = conv_input.shape[0]
    gate_act = jnp.dot(tokens, gate_weight.reshape(model_width, -1), preferred_element_type=jnp.float32).astype(jnp.bfloat16)
    input_raw = jnp.dot(tokens, input_weight.reshape(model_width, -1), preferred_element_type=jnp.float32).astype(jnp.bfloat16)
    group_raw = jnp.dot(tokens, group_weight.reshape(model_width, -1), preferred_element_type=jnp.float32).astype(jnp.bfloat16)
    onehot = (bucket_ids[:, None] == jnp.arange(PLACE_BINS, dtype=jnp.int32)[None, :]).astype(jnp.float32)
    offsets = jnp.dot(onehot, bucket_table, precision=highest)
    step_sum = jnp.dot(tokens, step_weight, preferred_element_type=jnp.float32)
    steps_tok = jax.nn.softplus(step_sum + step_bias[None, :] + offsets).astype(jnp.bfloat16)
    conv_values = causal_conv(input_raw, jnp.zeros((tap_count - 1, input_raw.shape[1]), jnp.bfloat16), conv_input.reshape(tap_count, -1), conv_input_bias.reshape(-1))
    conv_groups = causal_conv(group_raw, jnp.zeros((tap_count - 1, group_raw.shape[1]), jnp.bfloat16), conv_group.reshape(tap_count, -1), conv_group_bias.reshape(-1))
    values_groups = jnp.moveaxis(conv_values.reshape(seq_total, GROUPS, per_group, head_size), 1, 0)
    paired = conv_groups.reshape(seq_total, GROUPS, 2, state_size)
    b_groups = jnp.moveaxis(paired[:, :, 0], 1, 0)
    c_groups = jnp.moveaxis(paired[:, :, 1], 1, 0)
    steps_groups = jnp.moveaxis(steps_tok.reshape(seq_total, GROUPS, per_group), 1, 0)
    decay_groups = (-decay_rate).reshape(GROUPS, per_group)

    def run_group(member):
        start_state = jnp.zeros((per_group, head_size, state_size), jnp.float32)
        return ssd_group(start_state, member[0], member[1], member[2], member[3], member[4])[1]
    scanned = jnp.moveaxis(lax.map(run_group, (values_groups, b_groups, c_groups, steps_groups, decay_groups)), 0, 1)
    scanned = scanned + skip_gain.reshape(GROUPS, per_group)[None, :, :, None] * conv_values.reshape(seq_total, GROUPS, per_group, head_size).astype(jnp.float32)
    scanned = scanned.reshape(seq_total, -1).astype(jnp.bfloat16)
    gated_out = scanned.astype(jnp.float32) * jax.nn.silu(gate_act.astype(jnp.float32))
    grouped = gated_out.reshape(seq_total, GROUPS, -1)
    mean_square = lax.optimization_barrier(jnp.mean(grouped * grouped, axis=2))
    normed = ((grouped * lax.rsqrt(mean_square + norm_epsilon)[:, :, None]).reshape(seq_total, -1) * norm_gain.reshape(-1)[None, :]).astype(jnp.bfloat16)
    return jnp.dot(normed, out_weight.reshape(-1, model_width), preferred_element_type=jnp.float32).astype(jnp.bfloat16)
```

```python
import functools

import jax
import jax.numpy as jnp
from jax import lax
from jax.experimental import pallas as pl
from jax.experimental.pallas import tpu as pltpu
from jax.sharding import PartitionSpec as P

SPAN = 256
PLACE_BINS = 4


norm_epsilon = 1e-05
highest = lax.Precision.HIGHEST


def causal_conv(raw_rows, rim_rows, tap_weights, tap_bias):
    extended = jnp.concatenate([rim_rows, raw_rows], axis=0).astype(jnp.float32)
    row_count = raw_rows.shape[0]
    tap_count = tap_weights.shape[0]
    running = (
        tap_bias[None, :]
        + tap_weights[tap_count - 1][None, :] * extended[tap_count - 1 : tap_count - 1 + row_count]
    )
    for tap_index in range(tap_count - 1):
        running = (
            running + tap_weights[tap_index][None, :] * extended[tap_index : tap_index + row_count]
        )
    return jax.nn.silu(running).astype(jnp.bfloat16)


def ssd_block(carried_state, block_inputs, decay_neg):
    block_values, block_b, block_c, block_steps = block_inputs
    step_rates = block_steps.astype(jnp.float32) * decay_neg[None, :]
    cumulative = jnp.cumsum(step_rates, axis=0)
    scores = jnp.einsum("tn,sn->ts", block_c, block_b, preferred_element_type=jnp.float32)
    by_head = jnp.transpose(cumulative)
    spread = by_head[:, :, None] - by_head[:, None, :]
    block_rows = block_values.shape[0]
    causal = (jnp.arange(block_rows)[:, None] >= jnp.arange(block_rows)[None, :])[None]
    decays = jnp.where(causal, jnp.exp(jnp.where(causal, spread, 0.0)), 0.0)
    mixing = scores[None] * decays
    driven = block_steps.astype(jnp.float32)[:, :, None] * block_values.astype(jnp.float32)
    within = jnp.einsum("rts,srp->trp", mixing, driven, precision=highest)
    readout = jnp.einsum(
        "tn,rpn->trp", block_c.astype(jnp.float32), carried_state, precision=highest
    )
    outputs = within + jnp.exp(cumulative)[:, :, None] * readout
    remaining = jnp.exp(cumulative[-1][None, :] - cumulative)
    injected = jnp.einsum(
        "srp,sn->rpn",
        driven * remaining[:, :, None],
        block_b.astype(jnp.float32),
        precision=highest,
    )
    next_state = jnp.exp(cumulative[-1])[:, None, None] * carried_state + injected
    return (next_state, outputs)


def ssd_group(start_state, group_values, group_b, group_c, group_steps, decay_neg):
    row_total = group_values.shape[0]
    block_count = row_total // SPAN

    def advance(carried_state, block_inputs):
        return ssd_block(carried_state, block_inputs, decay_neg)

    blocked = (
        group_values.reshape((block_count, SPAN) + group_values.shape[1:]),
        group_b.reshape(block_count, SPAN, -1),
        group_c.reshape(block_count, SPAN, -1),
        group_steps.reshape(block_count, SPAN, -1),
    )
    final_state, outputs = lax.scan(advance, start_state, blocked)
    return (final_state, outputs.reshape((row_total,) + outputs.shape[2:]))


def weights_travel(
    tokens,
    gate_weight,
    input_weight,
    group_weight,
    step_weight,
    step_bias,
    bucket_table,
    bucket_ids,
    decay_rate,
    conv_input,
    conv_input_bias,
    conv_group,
    conv_group_bias,
    skip_gain,
    norm_gain,
    out_weight,
):
    tok_rows = tokens.shape[0]
    heads_here = step_bias.shape[0]
    groups_here = group_weight.shape[1]
    per_group = heads_here // groups_here
    head_size = gate_weight.shape[2]
    state_size = group_weight.shape[3]
    tap_count = conv_input.shape[0]
    channel_width = heads_here * head_size
    group_width = groups_here * 2 * state_size
    pieces = (
        lax.all_gather(gate_weight, "seq", axis=0, tiled=True),
        lax.all_gather(input_weight, "seq", axis=0, tiled=True),
        lax.all_gather(group_weight, "seq", axis=0, tiled=True),
        lax.all_gather(step_weight, "seq", axis=0, tiled=True),
    )
    rows_here = pieces[0].shape[0]
    gate_sum, input_sum, group_sum, step_sum = tuple(
        (
            jnp.dot(tokens, piece.reshape(rows_here, -1), preferred_element_type=jnp.float32)
            for piece in pieces
        )
    )
    gate_act = gate_sum.astype(jnp.bfloat16)
    input_raw = input_sum.astype(jnp.bfloat16)
    group_raw = group_sum.astype(jnp.bfloat16)
    onehot = (bucket_ids[:, None] == jnp.arange(PLACE_BINS, dtype=jnp.int32)[None, :]).astype(
        jnp.float32
    )
    offsets = jnp.dot(onehot, bucket_table, precision=highest)
    steps_tok = jax.nn.softplus(step_sum + step_bias[None, :] + offsets).astype(jnp.bfloat16)
    decay_neg = -decay_rate
    seq_count = lax.axis_size("seq")
    piece_width = channel_width // seq_count
    sub_width = min(piece_width, head_size)
    sub_count = piece_width // sub_width
    subs_per_head = head_size // sub_width
    steps_sub = jnp.repeat(steps_tok, subs_per_head, axis=1)
    wide_groups = jnp.broadcast_to(
        group_raw[:, None, :], (tok_rows, seq_count, group_width)
    ).reshape(tok_rows, seq_count * group_width)
    head_inputs, head_steps, head_groups = (
        lax.all_to_all(input_raw, "seq", split_axis=1, concat_axis=0, tiled=True),
        lax.all_to_all(steps_sub, "seq", split_axis=1, concat_axis=0, tiled=True),
        lax.all_to_all(wide_groups, "seq", split_axis=1, concat_axis=0, tiled=True),
    )
    seq_total = head_inputs.shape[0]
    first_channel = lax.axis_index("seq") * piece_width
    input_taps = lax.dynamic_slice_in_dim(
        conv_input.reshape(tap_count, -1), first_channel, piece_width, 1
    )
    input_shift = lax.dynamic_slice_in_dim(
        conv_input_bias.reshape(-1), first_channel, piece_width, 0
    )
    conv_values = causal_conv(
        head_inputs, jnp.zeros((tap_count - 1, piece_width), jnp.bfloat16), input_taps, input_shift
    )
    conv_groups = causal_conv(
        head_groups,
        jnp.zeros((tap_count - 1, group_width), jnp.bfloat16),
        conv_group.reshape(tap_count, -1),
        conv_group_bias.reshape(-1),
    )
    conv_groups = conv_groups.reshape(seq_total, groups_here, 2, state_size)
    sub_heads = (first_channel + jnp.arange(sub_count, dtype=jnp.int32) * sub_width) // head_size
    sub_groups = sub_heads // per_group
    sub_decay = jnp.take(decay_neg, sub_heads)[:, None]
    sub_skip = jnp.take(skip_gain, sub_heads)
    values_sub = jnp.moveaxis(conv_values.reshape(seq_total, sub_count, 1, sub_width), 1, 0)
    steps_heads = jnp.moveaxis(head_steps, 1, 0)[:, :, None]

    def run_sub(member):
        chosen = lax.dynamic_index_in_dim(conv_groups, member[3], 1, False)
        start_state = jnp.zeros((1, sub_width, state_size), jnp.float32)
        return ssd_group(start_state, member[0], chosen[:, 0], chosen[:, 1], member[1], member[2])[
            1
        ]

    scanned = jnp.moveaxis(
        lax.map(run_sub, (values_sub, steps_heads, sub_decay, sub_groups)), 0, 1
    ).reshape(seq_total, sub_count, sub_width)
    head_out = (
        scanned
        + sub_skip[None, :, None]
        * conv_values.reshape(seq_total, sub_count, sub_width).astype(jnp.float32)
    ).astype(jnp.bfloat16)
    ssd_out = lax.all_to_all(
        head_out.reshape(seq_total, piece_width), "seq", split_axis=0, concat_axis=1, tiled=True
    )
    gated_out = ssd_out.astype(jnp.float32) * jax.nn.silu(gate_act.astype(jnp.float32))
    grouped = gated_out.reshape(tok_rows, groups_here, -1)
    mean_square = jnp.mean(grouped * grouped, axis=2)
    scales = lax.rsqrt(mean_square + norm_epsilon)
    normed = (
        (grouped * scales[:, :, None]).reshape(tok_rows, -1) * norm_gain.reshape(-1)[None, :]
    ).astype(jnp.bfloat16)
    flat_out = out_weight.reshape(-1, out_weight.shape[2])
    layer_out = lax.psum_scatter(
        jnp.dot(normed, flat_out, preferred_element_type=jnp.float32).astype(jnp.bfloat16),
        "mp",
        scatter_dimension=0,
        tiled=True,
    )
    return layer_out


bf16 = jnp.bfloat16
f32 = jnp.float32
ROW_PAD = 16


def matmul(left, right, dims=((1,), (0,))):
    return lax.dot_general(left, right, (dims, ((), ())), preferred_element_type=f32)


def softplus(value):
    return jnp.maximum(value, 0.0) + jnp.log1p(jnp.exp(-jnp.abs(value)))


def silu(value):
    return value / (1.0 + jnp.exp(-value))


def project_kernel(place, first, second, weight, raw_in, step_in, raw, step):
    del place, raw_in, step_in
    raw_width = raw.shape[1]

    def emit(tok):
        total = matmul(tok, weight[...])
        raw[...] = total[:, :raw_width].astype(bf16)
        step[...] = total[:, raw_width:]

    @pl.when(pl.program_id(0) == 0)
    def _():
        emit(first[...])

    @pl.when(pl.program_id(0) == 1)
    def _():
        emit(second[...])


def project(place, first, second, weight, raw, step):
    rows, depth = first.shape
    whole = lambda i, place: (0, 0)
    spot = lambda i, place: (place[i], 0)
    width = raw.shape[1]
    extra = step.shape[1]
    return pl.pallas_call(
        project_kernel,
        grid_spec=pltpu.PrefetchScalarGridSpec(
            num_scalar_prefetch=1,
            grid=(2,),
            in_specs=[
                pl.BlockSpec((rows, depth), whole),
                pl.BlockSpec((rows, depth), whole),
                pl.BlockSpec(weight.shape, whole),
                pl.BlockSpec(memory_space=pl.ANY),
                pl.BlockSpec(memory_space=pl.ANY),
            ],
            out_specs=[pl.BlockSpec((rows, width), spot), pl.BlockSpec((rows, extra), spot)],
        ),
        out_shape=[
            jax.ShapeDtypeStruct(raw.shape, raw.dtype),
            jax.ShapeDtypeStruct(step.shape, step.dtype),
        ],
        input_output_aliases={4: 0, 5: 1},
        compiler_params=pltpu.CompilerParams(vmem_limit_bytes=32 * 1024 * 1024),
        cost_estimate=pl.CostEstimate(
            flops=4 * rows * depth * (width + extra),
            bytes_accessed=4 * rows * depth + 2 * weight.size,
            transcendentals=0,
        ),
        name="project",
    )(place, first, second, weight, raw, step)


def scan_kernel(
    head_size, raw, step, ids, table, bias, decay, skip, x_taps, x_shift, g_taps, g_shift,
    out, state, x_ext, g_ext,
):
    rows, channels = step.shape
    states = state.shape[1]
    heads = channels // head_size
    tap_count = x_taps.shape[0]
    rim = x_ext.shape[0] - rows

    @pl.when(pl.program_id(0) == 0)
    def _():
        state[...] = jnp.zeros_like(state)
        x_ext[:rim] = jnp.zeros((rim, channels), f32)
        g_ext[:rim] = jnp.zeros((rim, g_ext.shape[1]), f32)

    @pl.when(pl.program_id(0) > 0)
    def _():
        x_ext[:rim] = x_ext[rows:]
        g_ext[:rim] = g_ext[rows:]

    x_ext[rim:] = raw[:, :channels].astype(f32)
    g_ext[rim:] = raw[:, 2 * channels :].astype(f32)

    def conv(ext, taps, shift):
        first = rim - tap_count + 1
        running = shift[...]
        for tap in range(tap_count):
            running = running + taps[tap : tap + 1] * ext[first + tap : first + tap + rows]
        return silu(running).astype(bf16)

    values = conv(x_ext, x_taps, x_shift).astype(f32)
    groups = conv(g_ext, g_taps, g_shift)
    b_rows, c_rows = groups[:, :states], groups[:, states:]

    bucket = lax.broadcasted_iota(jnp.int32, (table.shape[0], rows), 0).astype(f32)
    onehot = (bucket == ids[0]).astype(f32)
    offsets = lax.dot_general(
        onehot, table[...], (((0,), (0,)), ((), ())),
        precision=highest, preferred_element_type=f32,
    )
    sizes = softplus(step[...] + bias[...] + offsets).astype(bf16).astype(f32)
    rates = -decay[...] * sizes
    row_at = lax.broadcasted_iota(jnp.int32, (rows, rows), 0)
    col_at = lax.broadcasted_iota(jnp.int32, (rows, rows), 1)
    causal = row_at >= col_at
    lower = jnp.where(causal, 1.0, 0.0).astype(bf16)
    coarse = rates.astype(bf16)
    left = rates - coarse.astype(f32)
    middle = left.astype(bf16)
    fine = (left - middle.astype(f32)).astype(bf16)
    cumulative = matmul(lower, coarse) + (matmul(lower, middle) + matmul(lower, fine))
    across = jnp.transpose(cumulative)

    scores = matmul(c_rows, b_rows, ((1,), (1,)))
    driven = sizes * values
    driven_low = driven.astype(bf16)
    lane = lax.broadcasted_iota(jnp.int32, (rows, channels), 1)
    within = jnp.zeros((rows, channels), f32)
    for head in range(heads):
        at = head * head_size
        spread = cumulative[:, at : at + 1] - across[at : at + 1, :]
        decays = jnp.exp(jnp.where(causal, spread, -1e30))
        part = matmul((scores * decays).astype(bf16), driven_low)
        within = jnp.where(lane >= at, part, within)
    readout = matmul(c_rows, state[...].astype(bf16), ((1,), (1,)))
    scanned = within + jnp.exp(cumulative) * readout + skip[...] * values
    scanned = scanned.astype(bf16).astype(f32)
    out[...] = (scanned * silu(raw[:, channels : 2 * channels].astype(f32))).astype(bf16)
    last = cumulative[rows - 1 : rows, :]
    remaining = jnp.exp(last - cumulative)
    injected = matmul((driven * remaining).astype(bf16), b_rows, ((0,), (0,)))
    state[...] = jnp.exp(across[:, rows - 1 : rows]) * state[...] + injected


def scan(head_size, state_size, raw, step, ids, table, *params):
    total, channels = step.shape
    rows = ids.shape[2]
    width = raw.shape[1]
    rim = 8
    block = lambda i: (i, 0)
    whole = lambda i: (0, 0)
    return pl.pallas_call(
        functools.partial(scan_kernel, head_size),
        grid=(total // rows,),
        in_specs=[
            pl.BlockSpec((rows, width), block),
            pl.BlockSpec((rows, channels), block),
            pl.BlockSpec((1, 1, rows), lambda i: (i, 0, 0)),
            pl.BlockSpec(table.shape, whole),
        ]
        + [pl.BlockSpec(param.shape, whole) for param in params],
        out_specs=pl.BlockSpec((rows, channels), block),
        out_shape=jax.ShapeDtypeStruct((total, channels), bf16),
        scratch_shapes=[
            pltpu.VMEM((channels, state_size), f32),
            pltpu.VMEM((rim + rows, channels), f32),
            pltpu.VMEM((rim + rows, 2 * state_size), f32),
        ],
        compiler_params=pltpu.CompilerParams(vmem_limit_bytes=32 * 1024 * 1024),
        cost_estimate=pl.CostEstimate(
            flops=2 * total * rows * (state_size + 2 * channels),
            bytes_accessed=4 * total * width,
            transcendentals=4 * total * rows,
        ),
        name="scan",
    )(raw, step, ids, table, *params)


def close_kernel(gated, gain, weight, out):
    pieces, _, width = gated.shape
    square = jnp.zeros(gated.shape[1:], f32)
    total = jnp.zeros(out.shape, f32)
    parts = []
    for piece in range(pieces):
        part = gated[piece].astype(f32)
        square = square + part * part
        parts.append((part * gain[:, piece * width : (piece + 1) * width]).astype(bf16))
    total = matmul(jnp.concatenate(parts, axis=1), weight[...])
    mean = jnp.sum(square, axis=1, keepdims=True) * (1.0 / (pieces * width))
    out[...] = (total * lax.rsqrt(mean + norm_epsilon)).astype(bf16)


def close(gated, gain, weight):
    pieces, rows, width = gated.shape
    columns = 512
    return pl.pallas_call(
        close_kernel,
        grid=(weight.shape[1] // columns,),
        in_specs=[
            pl.BlockSpec(gated.shape, lambda i: (0, 0, 0)),
            pl.BlockSpec(gain.shape, lambda i: (0, 0)),
            pl.BlockSpec((weight.shape[0], columns), lambda i: (0, i)),
        ],
        out_specs=pl.BlockSpec((rows, columns), lambda i: (0, i)),
        out_shape=jax.ShapeDtypeStruct((rows, weight.shape[1]), bf16),
        compiler_params=pltpu.CompilerParams(vmem_limit_bytes=32 * 1024 * 1024),
        cost_estimate=pl.CostEstimate(
            flops=2 * rows * weight.size, bytes_accessed=2 * weight.size, transcendentals=0
        ),
        name="close",
    )(gated, gain, weight)


def tokens_travel(
    tokens,
    gate_weight,
    input_weight,
    group_weight,
    step_weight,
    step_bias,
    bucket_table,
    bucket_ids,
    decay_rate,
    conv_input,
    conv_input_bias,
    conv_group,
    conv_group_bias,
    skip_gain,
    norm_gain,
    out_weight,
):
    rows, depth = tokens.shape
    slab = gate_weight.shape[0]
    heads_here = step_bias.shape[0]
    head_size = gate_weight.shape[2]
    state_size = group_weight.shape[3]
    tap_count = conv_input.shape[0]
    ring = lax.axis_size("seq")
    seats = lax.axis_size("mp")
    me = lax.axis_index("seq")
    seat = lax.axis_index("mp")
    core = seat % 2
    channels = heads_here * head_size // ring
    heads = channels // head_size
    half = rows // 2
    order = list(range(0, ring, 2)) + list(range(ring - 1, 0, -2))
    onward = [(order[i], order[(i + 1) % ring]) for i in range(ring)]
    backward = [(b, a) for a, b in onward]
    swap_core = [(i, i ^ 1) for i in range(seats)]
    position = [order.index(i) for i in range(ring)]
    place_of = jnp.asarray(position, jnp.int32)[me]
    source = lambda distance: jnp.asarray(order, jnp.int32)[(place_of + ring - distance) % ring]

    pair = jnp.stack(
        [input_weight.reshape(slab, ring, channels), gate_weight.reshape(slab, ring, channels)],
        axis=2,
    ).reshape(slab, ring, 2 * channels)
    pair = lax.all_to_all(pair, "seq", split_axis=1, concat_axis=0, tiled=True)
    pair = pair.reshape(ring * slab, 2 * channels)

    lanes = 2 * state_size
    step_rows = step_weight.size // lanes
    id_rows = rows // lanes
    pad_rows = -(step_rows + id_rows) % ROW_PAD
    shared = jnp.concatenate(
        [
            group_weight.reshape(slab, lanes),
            step_weight.reshape(step_rows, lanes),
            bucket_ids.astype(bf16).reshape(id_rows, lanes),
            jnp.zeros((pad_rows, lanes), bf16),
        ],
        axis=0,
    )
    mine = lax.dynamic_slice_in_dim(tokens, core * half, half, 0)
    other = lax.dynamic_slice_in_dim(tokens, (1 - core) * half, half, 0)

    gathered = jnp.zeros((ring,) + shared.shape, bf16)
    gathered = lax.dynamic_update_slice_in_dim(gathered, shared[None], me, 0)
    ahead = behind = shared
    for distance in range(1, ring // 2 + 1):
        ahead = lax.ppermute(ahead, "seq", onward)
        gathered = lax.dynamic_update_slice_in_dim(gathered, ahead[None], source(distance), 0)
        if distance < ring - distance:
            behind = lax.ppermute(behind, "seq", backward)
            gathered = lax.dynamic_update_slice_in_dim(
                gathered, behind[None], source(ring - distance), 0
            )
    group_all = gathered[:, :slab].reshape(ring * slab, lanes)
    step_all = gathered[:, slab : slab + step_rows].reshape(ring * slab, heads_here)
    step_mine = lax.dynamic_slice_in_dim(step_all, me * heads, heads, 1)
    step_wide = jnp.repeat(step_mine, head_size, axis=1)
    ids = gathered[:, slab + step_rows : slab + step_rows + id_rows].reshape(ring, 1, rows)
    weight = jnp.concatenate([pair, group_all, step_wide], axis=1)

    raw = jnp.zeros((ring * rows, 2 * channels + lanes), bf16)
    step = jnp.zeros((ring * rows, channels), f32)

    def put(block, near, far, raw, step):
        place = jnp.stack([2 * block + core, 2 * block + 1 - core]).astype(jnp.int32)
        return project(place, near, far, weight, raw, step)

    raw, step = put(me, mine, other, raw, step)
    ahead = behind = mine
    for distance in range(1, ring // 2 + 1):
        ahead = lax.ppermute(ahead, "seq", onward)
        far = lax.ppermute(ahead, "mp", swap_core)
        raw, step = put(source(distance), ahead, far, raw, step)
        if distance < ring - distance:
            behind = lax.ppermute(behind, "seq", backward)
            far = lax.ppermute(behind, "mp", swap_core)
            raw, step = put(source(ring - distance), behind, far, raw, step)

    def wide(per_head):
        own = lax.dynamic_slice_in_dim(per_head, me * heads, heads, per_head.ndim - 1)
        return jnp.repeat(own, head_size, axis=-1).reshape(-1, channels)

    def own(per_channel):
        flat = per_channel.reshape(-1, heads_here * head_size)
        return lax.dynamic_slice_in_dim(flat, me * channels, channels, 1)

    table = jnp.pad(wide(bucket_table), ((0, 8 - bucket_table.shape[0]), (0, 0)))
    gated = scan(
        head_size,
        state_size,
        raw,
        step,
        ids.astype(f32),
        table,
        wide(step_bias),
        wide(decay_rate),
        wide(skip_gain),
        own(conv_input),
        own(conv_input_bias),
        conv_group.reshape(tap_count, lanes),
        conv_group_bias.reshape(1, lanes),
    )
    gated = lax.all_to_all(
        gated.reshape(ring, rows, channels), "seq", split_axis=0, concat_axis=0, tiled=True
    )
    partial = close(
        gated, norm_gain.reshape(1, -1), out_weight.reshape(-1, out_weight.shape[2])
    )
    swap_chip = [(i, (i + 2) % seats) for i in range(seats)]
    quarters = partial.reshape(seats // 2, 2, rows // seats, -1)
    keep = lax.dynamic_index_in_dim(quarters, core, 1, False)
    give = lax.dynamic_index_in_dim(quarters, 1 - core, 1, False)
    both = (keep.astype(f32) + lax.ppermute(give, "mp", swap_core).astype(f32)).astype(bf16)
    chip = seat // 2
    keep = lax.dynamic_index_in_dim(both, chip, 0, False)
    give = lax.dynamic_index_in_dim(both, 1 - chip, 0, False)
    return (keep.astype(f32) + lax.ppermute(give, "mp", swap_chip).astype(f32)).astype(bf16)


def on_device(*arrays):
    tokens, gate_weight, group_weight = arrays[0], arrays[1], arrays[3]
    ring = lax.axis_size("seq")
    channels = gate_weight.shape[1] * gate_weight.shape[2] // ring
    weights = 2 * gate_weight.size + group_weight.size + arrays[4].size
    fits = (
        tokens.size <= weights
        and channels % 128 == 0
        and channels % gate_weight.shape[2] == 0
        and group_weight.shape[1] == 1
        and lax.axis_size("mp") == 4
        and ring % 2 == 0
    )
    return (tokens_travel if fits else weights_travel)(*arrays)


def solution(mesh):
    placed = (
        P("seq", None),
        P("seq", "mp", None),
        P("seq", "mp", None),
        P("seq", "mp", None, None),
        P("seq", "mp"),
        P("mp"),
        P(None, "mp"),
        P("seq"),
        P("mp"),
        P(None, "mp", None),
        P("mp", None),
        P(None, "mp", None, None),
        P("mp", None, None),
        P("mp"),
        P("mp", None),
        P("mp", None, None),
    )
    return jax.shard_map(
        on_device, mesh=mesh, in_specs=placed, out_specs=P(("seq", "mp"), None), check_vma=False
    )
```

```python
import functools

import jax
import jax.numpy as jnp
from jax import lax
from jax.experimental import pallas as pl
from jax.experimental.pallas import tpu as pltpu
from jax.sharding import PartitionSpec as P

SPAN = 256
PLACE_BINS = 4


norm_epsilon = 1e-05
highest = lax.Precision.HIGHEST


def causal_conv(raw_rows, rim_rows, tap_weights, tap_bias):
    extended = jnp.concatenate([rim_rows, raw_rows], axis=0).astype(jnp.float32)
    row_count = raw_rows.shape[0]
    tap_count = tap_weights.shape[0]
    running = (
        tap_bias[None, :]
        + tap_weights[tap_count - 1][None, :] * extended[tap_count - 1 : tap_count - 1 + row_count]
    )
    for tap_index in range(tap_count - 1):
        running = (
            running + tap_weights[tap_index][None, :] * extended[tap_index : tap_index + row_count]
        )
    return jax.nn.silu(running).astype(jnp.bfloat16)


def ssd_block(carried_state, block_inputs, decay_neg):
    block_values, block_b, block_c, block_steps = block_inputs
    step_rates = block_steps.astype(jnp.float32) * decay_neg[None, :]
    cumulative = jnp.cumsum(step_rates, axis=0)
    scores = jnp.einsum("tn,sn->ts", block_c, block_b, preferred_element_type=jnp.float32)
    by_head = jnp.transpose(cumulative)
    spread = by_head[:, :, None] - by_head[:, None, :]
    block_rows = block_values.shape[0]
    causal = (jnp.arange(block_rows)[:, None] >= jnp.arange(block_rows)[None, :])[None]
    decays = jnp.where(causal, jnp.exp(jnp.where(causal, spread, 0.0)), 0.0)
    mixing = scores[None] * decays
    driven = block_steps.astype(jnp.float32)[:, :, None] * block_values.astype(jnp.float32)
    within = jnp.einsum("rts,srp->trp", mixing, driven, precision=highest)
    readout = jnp.einsum(
        "tn,rpn->trp", block_c.astype(jnp.float32), carried_state, precision=highest
    )
    outputs = within + jnp.exp(cumulative)[:, :, None] * readout
    remaining = jnp.exp(cumulative[-1][None, :] - cumulative)
    injected = jnp.einsum(
        "srp,sn->rpn",
        driven * remaining[:, :, None],
        block_b.astype(jnp.float32),
        precision=highest,
    )
    next_state = jnp.exp(cumulative[-1])[:, None, None] * carried_state + injected
    return (next_state, outputs)


def ssd_group(start_state, group_values, group_b, group_c, group_steps, decay_neg):
    row_total = group_values.shape[0]
    block_count = row_total // SPAN

    def advance(carried_state, block_inputs):
        return ssd_block(carried_state, block_inputs, decay_neg)

    blocked = (
        group_values.reshape((block_count, SPAN) + group_values.shape[1:]),
        group_b.reshape(block_count, SPAN, -1),
        group_c.reshape(block_count, SPAN, -1),
        group_steps.reshape(block_count, SPAN, -1),
    )
    final_state, outputs = lax.scan(advance, start_state, blocked)
    return (final_state, outputs.reshape((row_total,) + outputs.shape[2:]))


def weights_travel(
    tokens,
    gate_weight,
    input_weight,
    group_weight,
    step_weight,
    step_bias,
    bucket_table,
    bucket_ids,
    decay_rate,
    conv_input,
    conv_input_bias,
    conv_group,
    conv_group_bias,
    skip_gain,
    norm_gain,
    out_weight,
):
    tok_rows = tokens.shape[0]
    heads_here = step_bias.shape[0]
    groups_here = group_weight.shape[1]
    per_group = heads_here // groups_here
    head_size = gate_weight.shape[2]
    state_size = group_weight.shape[3]
    tap_count = conv_input.shape[0]
    channel_width = heads_here * head_size
    group_width = groups_here * 2 * state_size
    pieces = (
        lax.all_gather(gate_weight, "seq", axis=0, tiled=True),
        lax.all_gather(input_weight, "seq", axis=0, tiled=True),
        lax.all_gather(group_weight, "seq", axis=0, tiled=True),
        lax.all_gather(step_weight, "seq", axis=0, tiled=True),
    )
    rows_here = pieces[0].shape[0]
    gate_sum, input_sum, group_sum, step_sum = tuple(
        (
            jnp.dot(tokens, piece.reshape(rows_here, -1), preferred_element_type=jnp.float32)
            for piece in pieces
        )
    )
    gate_act = gate_sum.astype(jnp.bfloat16)
    input_raw = input_sum.astype(jnp.bfloat16)
    group_raw = group_sum.astype(jnp.bfloat16)
    onehot = (bucket_ids[:, None] == jnp.arange(PLACE_BINS, dtype=jnp.int32)[None, :]).astype(
        jnp.float32
    )
    offsets = jnp.dot(onehot, bucket_table, precision=highest)
    steps_tok = jax.nn.softplus(step_sum + step_bias[None, :] + offsets).astype(jnp.bfloat16)
    decay_neg = -decay_rate
    seq_count = lax.axis_size("seq")
    piece_width = channel_width // seq_count
    sub_width = min(piece_width, head_size)
    sub_count = piece_width // sub_width
    subs_per_head = head_size // sub_width
    steps_sub = jnp.repeat(steps_tok, subs_per_head, axis=1)
    wide_groups = jnp.broadcast_to(
        group_raw[:, None, :], (tok_rows, seq_count, group_width)
    ).reshape(tok_rows, seq_count * group_width)
    head_inputs, head_steps, head_groups = (
        lax.all_to_all(input_raw, "seq", split_axis=1, concat_axis=0, tiled=True),
        lax.all_to_all(steps_sub, "seq", split_axis=1, concat_axis=0, tiled=True),
        lax.all_to_all(wide_groups, "seq", split_axis=1, concat_axis=0, tiled=True),
    )
    seq_total = head_inputs.shape[0]
    first_channel = lax.axis_index("seq") * piece_width
    input_taps = lax.dynamic_slice_in_dim(
        conv_input.reshape(tap_count, -1), first_channel, piece_width, 1
    )
    input_shift = lax.dynamic_slice_in_dim(
        conv_input_bias.reshape(-1), first_channel, piece_width, 0
    )
    conv_values = causal_conv(
        head_inputs, jnp.zeros((tap_count - 1, piece_width), jnp.bfloat16), input_taps, input_shift
    )
    conv_groups = causal_conv(
        head_groups,
        jnp.zeros((tap_count - 1, group_width), jnp.bfloat16),
        conv_group.reshape(tap_count, -1),
        conv_group_bias.reshape(-1),
    )
    conv_groups = conv_groups.reshape(seq_total, groups_here, 2, state_size)
    sub_heads = (first_channel + jnp.arange(sub_count, dtype=jnp.int32) * sub_width) // head_size
    sub_groups = sub_heads // per_group
    sub_decay = jnp.take(decay_neg, sub_heads)[:, None]
    sub_skip = jnp.take(skip_gain, sub_heads)
    values_sub = jnp.moveaxis(conv_values.reshape(seq_total, sub_count, 1, sub_width), 1, 0)
    steps_heads = jnp.moveaxis(head_steps, 1, 0)[:, :, None]

    def run_sub(member):
        chosen = lax.dynamic_index_in_dim(conv_groups, member[3], 1, False)
        start_state = jnp.zeros((1, sub_width, state_size), jnp.float32)
        return ssd_group(start_state, member[0], chosen[:, 0], chosen[:, 1], member[1], member[2])[
            1
        ]

    scanned = jnp.moveaxis(
        lax.map(run_sub, (values_sub, steps_heads, sub_decay, sub_groups)), 0, 1
    ).reshape(seq_total, sub_count, sub_width)
    head_out = (
        scanned
        + sub_skip[None, :, None]
        * conv_values.reshape(seq_total, sub_count, sub_width).astype(jnp.float32)
    ).astype(jnp.bfloat16)
    ssd_out = lax.all_to_all(
        head_out.reshape(seq_total, piece_width), "seq", split_axis=0, concat_axis=1, tiled=True
    )
    gated_out = ssd_out.astype(jnp.float32) * jax.nn.silu(gate_act.astype(jnp.float32))
    grouped = gated_out.reshape(tok_rows, groups_here, -1)
    mean_square = jnp.mean(grouped * grouped, axis=2)
    scales = lax.rsqrt(mean_square + norm_epsilon)
    normed = (
        (grouped * scales[:, :, None]).reshape(tok_rows, -1) * norm_gain.reshape(-1)[None, :]
    ).astype(jnp.bfloat16)
    flat_out = out_weight.reshape(-1, out_weight.shape[2])
    layer_out = lax.psum_scatter(
        jnp.dot(normed, flat_out, preferred_element_type=jnp.float32).astype(jnp.bfloat16),
        "mp",
        scatter_dimension=0,
        tiled=True,
    )
    return layer_out


bf16 = jnp.bfloat16
f32 = jnp.float32
ROW_PAD = 16


def matmul(left, right, dims=((1,), (0,))):
    return lax.dot_general(left, right, (dims, ((), ())), preferred_element_type=f32)


def softplus(value):
    return jnp.maximum(value, 0.0) + jnp.log1p(jnp.exp(-jnp.abs(value)))


def silu(value):
    return 0.5 * value * (1.0 + jnp.tanh(0.5 * value))


def parts_of(value, count):
    parts = []
    for _ in range(count):
        part = value.astype(bf16).astype(f32)
        parts.append(part)
        value = value - part
    return parts


def pack_kernel(at, tokens, groups, steps, ids, own, payload):
    seats, height, part = own.shape
    rows = tokens.shape[0] // seats
    for seat in range(seats):
        for panel in range(height // rows):
            own[seat, panel * rows : (panel + 1) * rows] = tokens[
                seat * rows : (seat + 1) * rows, panel * part : (panel + 1) * part
            ]
    payload[:height] = own[at[0]]
    low = height
    payload[low : low + groups.shape[0]] = groups[...]
    low += groups.shape[0]
    payload[low : low + steps.shape[0]] = steps[...]
    low += steps.shape[0]
    payload[low:] = jnp.broadcast_to(ids[...].astype(f32), (ROW_PAD, part)).astype(bf16)


def pack(at, seats, tokens, groups, steps, ids):
    rows, depth = tokens.shape
    part = groups.shape[1]
    height = rows * depth // (seats * part)
    full = height + groups.shape[0] + steps.shape[0] + ROW_PAD
    vmem = pl.BlockSpec(memory_space=pltpu.VMEM)
    return pl.pallas_call(
        pack_kernel,
        in_specs=[pl.BlockSpec(memory_space=pltpu.SMEM)] + [vmem] * 4,
        out_specs=[vmem, vmem],
        out_shape=[
            jax.ShapeDtypeStruct((seats, height, part), bf16),
            jax.ShapeDtypeStruct((full, part), bf16),
        ],
        name="pack",
    )(at, tokens, groups, steps, ids)


def layer_kernel(
    head_size, counts, table, pair, own, *refs
):
    ring = pair.shape[0]
    payloads, refs = refs[: ring], refs[ring:]
    pieces, refs = refs[: 4 * len(counts)], refs[4 * len(counts) :]
    per_head, params, g_taps, g_shift, out = refs[:5]
    tok, w_pair, w_group, st_rows, id_rows, w_x, w_step, x_all, g_all, gate_all, step_all, state, sems = refs[5:]
    seats = own.shape[0]
    height, part = own.shape[1:]
    channels = out.shape[2]
    rows = out.shape[1]
    quarter = rows // seats
    panels = height // quarter
    states = part // 2
    heads = channels // head_size
    step_heads = st_rows.shape[1]
    lines = w_step.shape[1]
    tap_count = g_taps.shape[0]
    rim = x_all.shape[0] - ring * rows

    pair_copy = pltpu.make_async_copy(pair, w_pair, sems.at[0])
    pair_copy.start()
    shared = []
    for order in range(ring):
        source = table[order]
        low = height
        for kind, target in enumerate((w_group, st_rows, id_rows)):
            size = target.shape[1]
            copy = pltpu.make_async_copy(
                payloads[order].at[pl.ds(low, size)],
                target.at[source],
                sems.at[1 + ring + kind * ring + order],
            )
            copy.start()
            shared.append(copy)
            low += size
    pltpu.make_async_copy(own, tok.at[table[0]], sems.at[1 + table[0]]).start()
    order = 1
    for group, count in enumerate(counts):
        for at in range(count):
            source = table[order]
            for hop in range(seats):
                pltpu.make_async_copy(
                    pieces[4 * group + hop].at[at],
                    tok.at[source, table[ring + hop]],
                    sems.at[1 + source],
                ).start()
            order += 1

    x_all[:rim] = jnp.zeros((rim, channels), f32)
    g_all[:rim] = jnp.zeros((rim, part), f32)
    state[...] = jnp.zeros_like(state)
    one = lambda flag: flag.astype(f32).astype(bf16)
    iota = lambda shape, dim: lax.broadcasted_iota(jnp.int32, shape, dim)
    same = one(iota((2 * channels, 2 * channels), 0) == iota((2 * channels, 2 * channels), 1))
    pick = one(
        (iota((lines, step_heads), 0) + table[0] * heads == iota((lines, step_heads), 1))
        & (iota((lines, step_heads), 0) < heads)
    )
    pair_copy.wait()
    for copy in shared:
        copy.wait()
    for panel in range(ring):
        w_x[panel] = matmul(w_pair[panel], same, ((0,), (0,))).astype(bf16)
        w_step[panel] = matmul(pick, st_rows[panel]).astype(bf16)

    upper = one(iota((rows, rows), 0) <= iota((rows, rows), 1))
    widen = one(iota((lines, channels), 1) // head_size == iota((lines, channels), 0))
    half = rows // 2
    causal = iota((half, half), 0) >= iota((half, half), 1)
    lane_head = iota((rows, channels), 1) // head_size
    bias, decay = per_head[:, 0:1], per_head[:, 1:2]
    skip = params[tap_count + 1 : tap_count + 2]

    def tok_wait(block):
        pltpu.make_async_copy(own, tok.at[block], sems.at[1 + block]).wait()

    def project(block):
        total_x = total_g = total_s = None
        for panel in range(panels):
            at = panel * quarter
            piece = jnp.concatenate(
                [tok[block, seat, at : at + quarter] for seat in range(seats)], axis=0
            )
            term_x = matmul(piece, w_x[panel])
            term_g = matmul(piece, w_group[panel])
            term_s = matmul(w_step[panel], piece, ((1,), (1,)))
            total_x = term_x if total_x is None else total_x + term_x
            total_g = term_g if total_g is None else total_g + term_g
            total_s = term_s if total_s is None else total_s + term_s
        base = pl.multiple_of(block * rows, rows)
        x_all[pl.ds(base + rim, rows)] = total_x[:, :channels].astype(bf16).astype(f32)
        gate_all[block] = total_x[:, channels:].astype(bf16).astype(f32)
        g_all[pl.ds(base + rim, rows)] = total_g.astype(bf16).astype(f32)
        step_all[block] = total_s

    def conv(ref, base, taps, shift):
        window = ref[pl.ds(base, rows + rim)]
        first = rim - tap_count + 1
        running = shift
        for tap in range(tap_count):
            running = running + taps[tap : tap + 1] * window[first + tap : first + tap + rows]
        return silu(running).astype(bf16)

    def stretch(value, count):
        low = jnp.concatenate(parts_of(value, count), axis=0).astype(bf16)
        return matmul(low, jnp.concatenate([widen] * count, axis=0), ((0,), (0,)))

    def scan(block):
        base = pl.multiple_of(block * rows, rows)
        values = conv(x_all, base, params[:tap_count], params[tap_count : tap_count + 1])
        values = values.astype(f32)
        groups = conv(g_all, base, g_taps[...], g_shift[...])
        b_rows, c_rows = groups[:, :states], groups[:, states:]
        bucket = id_rows[block].astype(f32)[:1]
        raw_step = step_all[block] + bias
        for entry in range(PLACE_BINS):
            raw_step = raw_step + jnp.where(
                bucket == float(entry), per_head[:, 2 + entry : 3 + entry], 0.0
            )
        sizes = softplus(raw_step).astype(bf16).astype(f32)
        rates = jnp.concatenate(parts_of(-decay * sizes, 3), axis=0).astype(bf16)
        sums = matmul(rates, upper)
        cumulative = sums[:lines] + (sums[lines : 2 * lines] + sums[2 * lines :])
        last = cumulative[:, rows - 1 : rows]
        grown = stretch(jnp.exp(cumulative), 3)
        left = stretch(sizes * jnp.exp(last - cumulative), 3)
        driven = (stretch(sizes, 1) * values).astype(f32)
        scores = matmul(c_rows, b_rows, ((1,), (1,)))
        cum_parts = parts_of(cumulative, 3)
        ones = jnp.ones((3, rows), f32)
        pad = jnp.zeros((2, rows), f32)
        top, low_left, low_right, inputs = [], [], [], []
        for head in range(heads):
            mine = jnp.concatenate([p[head : head + 1] for p in cum_parts], axis=0)
            spread = matmul(
                jnp.concatenate([mine, ones, pad], axis=0).astype(bf16),
                jnp.concatenate([ones, -mine, pad], axis=0).astype(bf16),
                ((0,), (0,)),
            )
            decays = lambda part: jnp.exp(jnp.where(causal, part, -1e30))
            top.append((scores[:half, :half] * decays(spread[:half, :half])).astype(bf16))
            low_left.append((scores[half:, :half] * jnp.exp(spread[half:, :half])).astype(bf16))
            low_right.append((scores[half:, half:] * decays(spread[half:, half:])).astype(bf16))
            inputs.append(jnp.where(lane_head == head, driven, 0.0).astype(bf16))
        upper_in = jnp.concatenate([d[:half] for d in inputs], axis=0)
        lower_in = jnp.concatenate([d[half:] for d in inputs], axis=0)
        upper_out = matmul(jnp.concatenate(top, axis=1), upper_in)
        lower_out = matmul(
            jnp.concatenate(low_left + low_right, axis=1),
            jnp.concatenate([upper_in, lower_in], axis=0),
        )
        within = jnp.concatenate([upper_out, lower_out], axis=0)
        held = state[...]
        scanned = within + grown * matmul(c_rows, held.astype(bf16)) + skip * values
        scanned = scanned.astype(bf16).astype(f32)
        out[block] = (scanned * silu(gate_all[block])).astype(bf16)
        injected = matmul(b_rows, (left * values).astype(bf16), ((0,), (0,)))
        state[...] = grown[rows - 1 : rows] * held + injected

    tok_wait(0)
    project(0)

    def advance(block, carry):
        tok_wait(block + 1)
        scan(block)
        project(block + 1)
        return carry

    lax.fori_loop(0, ring - 1, advance, 0)
    scan(ring - 1)


def layer(head_size, table, pair, own, payloads, groups, per_head, params, g_taps, g_shift):
    ring, wide, slab = pair.shape
    channels = wide // 2
    seats, height, part = own.shape
    rows = seats * height * part // (ring * slab)
    step_heads = payloads[0].shape[0] - height - slab - ROW_PAD
    lines = per_head.shape[0]
    rim = 8
    total = ring * rows
    counts = [group[0].shape[0] for group in groups]
    pieces = [piece for group in groups for piece in group]
    vmem = pl.BlockSpec(memory_space=pltpu.VMEM)
    anywhere = pl.BlockSpec(memory_space=pl.ANY)
    return pl.pallas_call(
        functools.partial(layer_kernel, head_size, counts),
        in_specs=[pl.BlockSpec(memory_space=pltpu.SMEM)]
        + [anywhere] * (2 + len(payloads) + len(pieces))
        + [vmem] * 4,
        out_specs=vmem,
        out_shape=jax.ShapeDtypeStruct((ring, rows, channels), bf16),
        scratch_shapes=[
            pltpu.VMEM((ring, seats, height, part), bf16),
            pltpu.VMEM(pair.shape, bf16),
            pltpu.VMEM((ring, slab, part), bf16),
            pltpu.VMEM((ring, step_heads, part), bf16),
            pltpu.VMEM((ring, ROW_PAD, part), bf16),
            pltpu.VMEM((ring, slab, wide), bf16),
            pltpu.VMEM((ring, lines, slab), bf16),
            pltpu.VMEM((rim + total, channels), f32),
            pltpu.VMEM((rim + total, part), f32),
            pltpu.VMEM((ring, rows, channels), f32),
            pltpu.VMEM((ring, lines, rows), f32),
            pltpu.VMEM((part // 2, channels), f32),
            pltpu.SemaphoreType.DMA((1 + 4 * ring,)),
        ],
        compiler_params=pltpu.CompilerParams(vmem_limit_bytes=48 * 1024 * 1024),
        cost_estimate=pl.CostEstimate(
            flops=2 * total * ring * slab * (wide + part),
            bytes_accessed=2 * total * ring * slab,
            transcendentals=0,
        ),
        name="layer",
    )(table, pair, own, *payloads, *pieces, per_head, params, g_taps, g_shift)


def close_kernel(gated, gain, weight, out):
    pieces, _, width = gated.shape
    square = jnp.zeros(gated.shape[1:], f32)
    total = jnp.zeros(out.shape, f32)
    parts = []
    for piece in range(pieces):
        part = gated[piece].astype(f32)
        square = square + part * part
        parts.append((part * gain[:, piece * width : (piece + 1) * width]).astype(bf16))
    total = matmul(jnp.concatenate(parts, axis=1), weight[...])
    mean = jnp.sum(square, axis=1, keepdims=True) * (1.0 / (pieces * width))
    out[...] = (total * lax.rsqrt(mean + norm_epsilon)).astype(bf16)


def close(gated, gain, weight):
    pieces, rows, width = gated.shape
    columns = 512
    return pl.pallas_call(
        close_kernel,
        grid=(weight.shape[1] // columns,),
        in_specs=[
            pl.BlockSpec(gated.shape, lambda i: (0, 0, 0)),
            pl.BlockSpec(gain.shape, lambda i: (0, 0)),
            pl.BlockSpec((weight.shape[0], columns), lambda i: (0, i)),
        ],
        out_specs=pl.BlockSpec((rows, columns), lambda i: (0, i)),
        out_shape=jax.ShapeDtypeStruct((rows, weight.shape[1]), bf16),
        compiler_params=pltpu.CompilerParams(vmem_limit_bytes=32 * 1024 * 1024),
        cost_estimate=pl.CostEstimate(
            flops=2 * rows * weight.size, bytes_accessed=2 * weight.size, transcendentals=0
        ),
        name="close",
    )(gated, gain, weight)


def tokens_travel(
    tokens,
    gate_weight,
    input_weight,
    group_weight,
    step_weight,
    step_bias,
    bucket_table,
    bucket_ids,
    decay_rate,
    conv_input,
    conv_input_bias,
    conv_group,
    conv_group_bias,
    skip_gain,
    norm_gain,
    out_weight,
):
    rows, depth = tokens.shape
    slab = gate_weight.shape[0]
    heads_here = step_bias.shape[0]
    head_size = gate_weight.shape[2]
    state_size = group_weight.shape[3]
    tap_count = conv_input.shape[0]
    ring = lax.axis_size("seq")
    seats = lax.axis_size("mp")
    me = lax.axis_index("seq")
    seat = lax.axis_index("mp")
    core = seat % 2
    channels = heads_here * head_size // ring
    heads = channels // head_size
    line = ring // 2
    swap = lambda size, bit: [(i, i ^ bit) for i in range(size)]
    column = lambda pairs: [(2 * a + w, 2 * b + w) for a, b in pairs for w in range(2)]
    others = [[1, 2, 3], [0, 2, 3], [3, 1, 0], [2, 1, 0]]
    lists = []
    for seq_at in range(ring):
        z, x = seq_at // 2, seq_at % 2
        sources = [seq_at, seq_at ^ 1]
        for other in others[z]:
            sources += [2 * other + x, 2 * other + 1 - x]
        for seat_at in range(seats):
            lists.append(sources + [seat_at ^ q for q in range(seats)])
    table = lax.dynamic_index_in_dim(
        jnp.asarray(lists, jnp.int32), lax.axis_index(("seq", "mp")), 0, False
    )

    by_channel = lambda w: jnp.transpose(w, (1, 2, 0)).reshape(ring, channels, slab)
    pair = jnp.concatenate([by_channel(input_weight), by_channel(gate_weight)], axis=1)
    pair = lax.all_to_all(pair, "seq", split_axis=0, concat_axis=0, tiled=True)

    own, payload = pack(
        table[ring : ring + 1],
        seats,
        tokens,
        group_weight.reshape(slab, 2 * state_size),
        jnp.transpose(step_weight),
        bucket_ids.reshape(1, rows),
    )
    inner = (me >= 2) & (me < 6)
    outward = column([(1, 0), (2, 3)])
    middle = column([(1, 2), (2, 1)])
    near = lax.ppermute(payload, "seq", swap(ring, 2))
    mid = lax.ppermute(payload, "seq", middle)
    mid_far = lax.ppermute(near, "seq", middle)
    out_near = lax.ppermute(mid, "seq", outward)
    out_far = lax.ppermute(mid_far, "seq", outward)
    arrived = [near, jnp.where(inner, mid, out_near), jnp.where(inner, mid_far, out_far)]
    payloads = [payload, lax.ppermute(payload, "seq", swap(ring, 1))]
    for item in arrived:
        payloads += [item, lax.ppermute(item, "seq", swap(ring, 1))]
    height = own.shape[1]
    groups = []
    for first in range(1, ring, 2):
        quarter = jnp.stack([item[:height] for item in payloads[first : first + 2]])
        beside = lax.ppermute(quarter, "mp", swap(seats, 1))
        across = lax.ppermute(quarter, "mp", swap(seats, 2))
        groups.append((quarter, beside, across, lax.ppermute(across, "mp", swap(seats, 1))))

    per_head = jnp.concatenate([jnp.stack([step_bias, decay_rate]), bucket_table], axis=0)
    per_head = lax.dynamic_slice_in_dim(jnp.transpose(per_head), me * heads, heads, 0)
    per_head = jnp.pad(per_head, ((0, 8 - heads), (0, 0)))
    params = jnp.concatenate(
        [
            conv_input,
            conv_input_bias[None],
            jnp.broadcast_to(skip_gain[None, :, None], (1, heads_here, head_size)),
        ],
        axis=0,
    )
    params = params.reshape(params.shape[0], ring, channels)
    params = lax.dynamic_index_in_dim(params, me, 1, False)
    gated = layer(
        head_size,
        table,
        pair,
        own,
        payloads,
        groups,
        per_head,
        params,
        conv_group.reshape(tap_count, 2 * state_size),
        conv_group_bias.reshape(1, 2 * state_size),
    )
    gated = lax.all_to_all(gated, "seq", split_axis=0, concat_axis=0, tiled=True)
    partial = close(
        gated, norm_gain.reshape(1, -1), out_weight.reshape(-1, out_weight.shape[2])
    )
    quarters = partial.reshape(seats // 2, 2, rows // seats, -1)
    keep = lax.dynamic_index_in_dim(quarters, core, 1, False)
    give = lax.dynamic_index_in_dim(quarters, 1 - core, 1, False)
    both = (keep.astype(f32) + lax.ppermute(give, "mp", swap(seats, 1)).astype(f32)).astype(bf16)
    chip = seat // 2
    keep = lax.dynamic_index_in_dim(both, chip, 0, False)
    give = lax.dynamic_index_in_dim(both, 1 - chip, 0, False)
    return (keep.astype(f32) + lax.ppermute(give, "mp", swap(seats, 2)).astype(f32)).astype(bf16)


def on_device(*arrays):
    tokens, gate_weight, group_weight = arrays[0], arrays[1], arrays[3]
    ring = lax.axis_size("seq")
    channels = gate_weight.shape[1] * gate_weight.shape[2] // ring
    weights = 2 * gate_weight.size + group_weight.size + arrays[4].size
    fits = (
        tokens.size <= weights
        and channels % 128 == 0
        and gate_weight.shape[0] == 2 * group_weight.shape[3] == tokens.shape[0]
        and channels % gate_weight.shape[2] == 0
        and group_weight.shape[1] == 1
        and lax.axis_size("mp") == 4
        and ring == 8
    )
    return (tokens_travel if fits else weights_travel)(*arrays)


def solution(mesh):
    placed = (
        P("seq", None),
        P("seq", "mp", None),
        P("seq", "mp", None),
        P("seq", "mp", None, None),
        P("seq", "mp"),
        P("mp"),
        P(None, "mp"),
        P("seq"),
        P("mp"),
        P(None, "mp", None),
        P("mp", None),
        P(None, "mp", None, None),
        P("mp", None, None),
        P("mp"),
        P("mp", None),
        P("mp", None, None),
    )
    return jax.shard_map(
        on_device, mesh=mesh, in_specs=placed, out_specs=P(("seq", "mp"), None), check_vma=False
    )
```

```python
import functools

import jax
import jax.numpy as jnp
from jax import lax
from jax.experimental import pallas as pl
from jax.experimental.pallas import tpu as pltpu
from jax.sharding import PartitionSpec as P

SPAN = 256
PLACE_BINS = 4


norm_epsilon = 1e-05
highest = lax.Precision.HIGHEST


def causal_conv(raw_rows, rim_rows, tap_weights, tap_bias):
    extended = jnp.concatenate([rim_rows, raw_rows], axis=0).astype(jnp.float32)
    row_count = raw_rows.shape[0]
    tap_count = tap_weights.shape[0]
    running = (
        tap_bias[None, :]
        + tap_weights[tap_count - 1][None, :] * extended[tap_count - 1 : tap_count - 1 + row_count]
    )
    for tap_index in range(tap_count - 1):
        running = (
            running + tap_weights[tap_index][None, :] * extended[tap_index : tap_index + row_count]
        )
    return jax.nn.silu(running).astype(jnp.bfloat16)


def ssd_block(carried_state, block_inputs, decay_neg):
    block_values, block_b, block_c, block_steps = block_inputs
    step_rates = block_steps.astype(jnp.float32) * decay_neg[None, :]
    cumulative = jnp.cumsum(step_rates, axis=0)
    scores = jnp.einsum("tn,sn->ts", block_c, block_b, preferred_element_type=jnp.float32)
    by_head = jnp.transpose(cumulative)
    spread = by_head[:, :, None] - by_head[:, None, :]
    block_rows = block_values.shape[0]
    causal = (jnp.arange(block_rows)[:, None] >= jnp.arange(block_rows)[None, :])[None]
    decays = jnp.where(causal, jnp.exp(jnp.where(causal, spread, 0.0)), 0.0)
    mixing = scores[None] * decays
    driven = block_steps.astype(jnp.float32)[:, :, None] * block_values.astype(jnp.float32)
    within = jnp.einsum("rts,srp->trp", mixing, driven, precision=highest)
    readout = jnp.einsum(
        "tn,rpn->trp", block_c.astype(jnp.float32), carried_state, precision=highest
    )
    outputs = within + jnp.exp(cumulative)[:, :, None] * readout
    remaining = jnp.exp(cumulative[-1][None, :] - cumulative)
    injected = jnp.einsum(
        "srp,sn->rpn",
        driven * remaining[:, :, None],
        block_b.astype(jnp.float32),
        precision=highest,
    )
    next_state = jnp.exp(cumulative[-1])[:, None, None] * carried_state + injected
    return (next_state, outputs)


def ssd_group(start_state, group_values, group_b, group_c, group_steps, decay_neg):
    row_total = group_values.shape[0]
    block_count = row_total // SPAN

    def advance(carried_state, block_inputs):
        return ssd_block(carried_state, block_inputs, decay_neg)

    blocked = (
        group_values.reshape((block_count, SPAN) + group_values.shape[1:]),
        group_b.reshape(block_count, SPAN, -1),
        group_c.reshape(block_count, SPAN, -1),
        group_steps.reshape(block_count, SPAN, -1),
    )
    final_state, outputs = lax.scan(advance, start_state, blocked)
    return (final_state, outputs.reshape((row_total,) + outputs.shape[2:]))


def weights_travel(
    tokens,
    gate_weight,
    input_weight,
    group_weight,
    step_weight,
    step_bias,
    bucket_table,
    bucket_ids,
    decay_rate,
    conv_input,
    conv_input_bias,
    conv_group,
    conv_group_bias,
    skip_gain,
    norm_gain,
    out_weight,
):
    tok_rows = tokens.shape[0]
    heads_here = step_bias.shape[0]
    groups_here = group_weight.shape[1]
    per_group = heads_here // groups_here
    head_size = gate_weight.shape[2]
    state_size = group_weight.shape[3]
    tap_count = conv_input.shape[0]
    channel_width = heads_here * head_size
    group_width = groups_here * 2 * state_size
    pieces = (
        lax.all_gather(gate_weight, "seq", axis=0, tiled=True),
        lax.all_gather(input_weight, "seq", axis=0, tiled=True),
        lax.all_gather(group_weight, "seq", axis=0, tiled=True),
        lax.all_gather(step_weight, "seq", axis=0, tiled=True),
    )
    rows_here = pieces[0].shape[0]
    gate_sum, input_sum, group_sum, step_sum = tuple(
        (
            jnp.dot(tokens, piece.reshape(rows_here, -1), preferred_element_type=jnp.float32)
            for piece in pieces
        )
    )
    gate_act = gate_sum.astype(jnp.bfloat16)
    input_raw = input_sum.astype(jnp.bfloat16)
    group_raw = group_sum.astype(jnp.bfloat16)
    onehot = (bucket_ids[:, None] == jnp.arange(PLACE_BINS, dtype=jnp.int32)[None, :]).astype(
        jnp.float32
    )
    offsets = jnp.dot(onehot, bucket_table, precision=highest)
    steps_tok = jax.nn.softplus(step_sum + step_bias[None, :] + offsets).astype(jnp.bfloat16)
    decay_neg = -decay_rate
    seq_count = lax.axis_size("seq")
    piece_width = channel_width // seq_count
    sub_width = min(piece_width, head_size)
    sub_count = piece_width // sub_width
    subs_per_head = head_size // sub_width
    steps_sub = jnp.repeat(steps_tok, subs_per_head, axis=1)
    wide_groups = jnp.broadcast_to(
        group_raw[:, None, :], (tok_rows, seq_count, group_width)
    ).reshape(tok_rows, seq_count * group_width)
    head_inputs, head_steps, head_groups = (
        lax.all_to_all(input_raw, "seq", split_axis=1, concat_axis=0, tiled=True),
        lax.all_to_all(steps_sub, "seq", split_axis=1, concat_axis=0, tiled=True),
        lax.all_to_all(wide_groups, "seq", split_axis=1, concat_axis=0, tiled=True),
    )
    seq_total = head_inputs.shape[0]
    first_channel = lax.axis_index("seq") * piece_width
    input_taps = lax.dynamic_slice_in_dim(
        conv_input.reshape(tap_count, -1), first_channel, piece_width, 1
    )
    input_shift = lax.dynamic_slice_in_dim(
        conv_input_bias.reshape(-1), first_channel, piece_width, 0
    )
    conv_values = causal_conv(
        head_inputs, jnp.zeros((tap_count - 1, piece_width), jnp.bfloat16), input_taps, input_shift
    )
    conv_groups = causal_conv(
        head_groups,
        jnp.zeros((tap_count - 1, group_width), jnp.bfloat16),
        conv_group.reshape(tap_count, -1),
        conv_group_bias.reshape(-1),
    )
    conv_groups = conv_groups.reshape(seq_total, groups_here, 2, state_size)
    sub_heads = (first_channel + jnp.arange(sub_count, dtype=jnp.int32) * sub_width) // head_size
    sub_groups = sub_heads // per_group
    sub_decay = jnp.take(decay_neg, sub_heads)[:, None]
    sub_skip = jnp.take(skip_gain, sub_heads)
    values_sub = jnp.moveaxis(conv_values.reshape(seq_total, sub_count, 1, sub_width), 1, 0)
    steps_heads = jnp.moveaxis(head_steps, 1, 0)[:, :, None]

    def run_sub(member):
        chosen = lax.dynamic_index_in_dim(conv_groups, member[3], 1, False)
        start_state = jnp.zeros((1, sub_width, state_size), jnp.float32)
        return ssd_group(start_state, member[0], chosen[:, 0], chosen[:, 1], member[1], member[2])[
            1
        ]

    scanned = jnp.moveaxis(
        lax.map(run_sub, (values_sub, steps_heads, sub_decay, sub_groups)), 0, 1
    ).reshape(seq_total, sub_count, sub_width)
    head_out = (
        scanned
        + sub_skip[None, :, None]
        * conv_values.reshape(seq_total, sub_count, sub_width).astype(jnp.float32)
    ).astype(jnp.bfloat16)
    ssd_out = lax.all_to_all(
        head_out.reshape(seq_total, piece_width), "seq", split_axis=0, concat_axis=1, tiled=True
    )
    gated_out = ssd_out.astype(jnp.float32) * jax.nn.silu(gate_act.astype(jnp.float32))
    grouped = gated_out.reshape(tok_rows, groups_here, -1)
    mean_square = jnp.mean(grouped * grouped, axis=2)
    scales = lax.rsqrt(mean_square + norm_epsilon)
    normed = (
        (grouped * scales[:, :, None]).reshape(tok_rows, -1) * norm_gain.reshape(-1)[None, :]
    ).astype(jnp.bfloat16)
    flat_out = out_weight.reshape(-1, out_weight.shape[2])
    layer_out = lax.psum_scatter(
        jnp.dot(normed, flat_out, preferred_element_type=jnp.float32).astype(jnp.bfloat16),
        "mp",
        scatter_dimension=0,
        tiled=True,
    )
    return layer_out


bf16 = jnp.bfloat16
f32 = jnp.float32
ROW_PAD = 16
LANES = 128


def matmul(left, right, dims=((1,), (0,))):
    return lax.dot_general(left, right, (dims, ((), ())), preferred_element_type=f32)


def softplus(value):
    return jnp.maximum(value, 0.0) + jnp.log1p(jnp.exp(-jnp.abs(value)))


def silu(value):
    return 0.5 * value * (1.0 + jnp.tanh(0.5 * value))


def parts_of(value, count):
    parts = []
    for _ in range(count):
        part = value.astype(bf16).astype(f32)
        parts.append(part)
        value = value - part
    return parts


HBM = pl.BlockSpec(memory_space=pl.ANY)
VMEM = pl.BlockSpec(memory_space=pltpu.VMEM)


def pack_kernel(tokens, groups, steps, ids, payload, mine, sem):
    rows, depth = mine.shape
    seat = lax.axis_index("mp")
    copy = pltpu.make_async_copy(
        tokens.at[pl.ds(pl.multiple_of(seat * rows, rows), rows)], mine, sem
    )
    copy.start()
    panels = depth // LANES
    low = panels * rows
    payload[low : low + groups.shape[0]] = groups[...]
    low += groups.shape[0]
    high = steps.shape[0]
    for part in range(steps.shape[1] // LANES):
        payload[low : low + high] = steps[:, part * LANES : (part + 1) * LANES]
        low += high
    marks = ids[...].astype(f32)
    rest = jnp.zeros((ROW_PAD - marks.shape[0], LANES), f32)
    payload[low:] = jnp.concatenate([marks, rest], axis=0).astype(bf16)
    copy.wait()
    for panel in range(panels):
        payload[panel * rows : (panel + 1) * rows] = mine[:, panel * LANES : (panel + 1) * LANES]


def payload_rows(tokens):
    return tokens.shape[0] // 4


def pack(tokens, groups, steps, ids):
    rows, depth = tokens.shape
    extra = steps.size // LANES + ROW_PAD
    full = payload_rows(tokens) * depth // LANES + groups.shape[0] + extra
    return pl.pallas_call(
        pack_kernel,
        in_specs=[HBM, VMEM, VMEM, VMEM],
        out_specs=VMEM,
        out_shape=jax.ShapeDtypeStruct((full, LANES), bf16),
        scratch_shapes=[
            pltpu.VMEM((payload_rows(tokens), depth), bf16),
            pltpu.SemaphoreType.DMA,
        ],
        name="pack",
    )(tokens, groups, steps, ids)


def layer_kernel(head_size, counts, tokens, *refs):
    columns, refs = refs[:2], refs[2:]
    ring, channels, slab = columns[0].shape
    payloads, refs = refs[:ring], refs[ring:]
    pieces, refs = refs[: 4 * len(counts)], refs[4 * len(counts) :]
    per_head_all, params_all, g_taps, g_shift, out = refs[:5]
    tok, w_pair, shared, w_x, w_group, w_step, x_all, g_all, gate_all, step_all, state, sems = refs[5:]
    seats = 4
    rows = out.shape[1]
    quarter = rows // seats
    panels = tok.shape[1]
    height = panels * quarter
    part = 2 * g_shift.shape[1] // 2
    states = part // 2
    heads = channels // head_size
    lines = w_step.shape[1]
    tap_count = g_taps.shape[0]
    rim = x_all.shape[0] - ring * rows
    step_rows = shared.shape[1] - 2 * slab - ROW_PAD
    step_heads = step_rows * LANES // slab
    me = lax.axis_index("seq")
    seat = lax.axis_index("mp")
    beside = me & 1
    upper_half = me >> 2
    sources = [me, me ^ 1]
    for other in ((me >> 1) ^ 1, 2 - upper_half, 3 - 3 * upper_half):
        sources += [2 * other + beside, 2 * other + 1 - beside]

    arrivals = [2, 1, 4, 3, 6, 5, 7]
    shared_copies = []
    for order in range(ring):
        copy = pltpu.make_async_copy(
            payloads[order].at[pl.ds(height, shared.shape[1])],
            shared.at[sources[order]],
            sems.at[1 + ring + order],
        )
        copy.start()
        shared_copies.append(copy)
    for kind in range(2):
        pltpu.make_async_copy(
            columns[kind], w_pair.at[:, pl.ds(kind * channels, channels)], sems.at[0]
        ).start()
    for panel in range(panels):
        pltpu.make_async_copy(
            tokens.at[:, pl.ds(panel * LANES, LANES)], tok.at[me, panel], sems.at[1 + me]
        ).start()
    order = 0
    for group, count in enumerate(counts):
        for at in range(count):
            source = sources[arrivals[order]]
            for hop in range(seats):
                first = pl.multiple_of((seat ^ hop) * quarter, quarter)
                pltpu.make_async_copy(
                    pieces[4 * group + hop].at[at],
                    tok.at[source, :, pl.ds(first, quarter)],
                    sems.at[1 + source],
                ).start()
            order += 1

    x_all[:rim] = jnp.zeros((rim, channels), f32)
    g_all[:rim] = jnp.zeros((rim, part), f32)
    state[...] = jnp.zeros_like(state)
    one = lambda flag: flag.astype(f32).astype(bf16)
    iota = lambda shape, dim: lax.broadcasted_iota(jnp.int32, shape, dim)
    same = one(iota((2 * channels, 2 * channels), 0) == iota((2 * channels, 2 * channels), 1))
    pick = one(
        (iota((lines, step_heads), 0) + me * heads == iota((lines, step_heads), 1))
        & (iota((lines, step_heads), 0) < heads)
    )
    unpick = [
        one(2 * iota((slab, 2 * slab), 0) + kind == iota((slab, 2 * slab), 1)) for kind in range(2)
    ]
    for copy in shared_copies:
        copy.wait()
    for panel in range(ring):
        slab_rows = shared[panel, : 2 * slab]
        for kind in range(2):
            w_group[panel, :, kind * states : (kind + 1) * states] = matmul(
                unpick[kind], slab_rows
            ).astype(bf16)
        step_panel = jnp.concatenate(
            [
                shared[panel, 2 * slab + low : 2 * slab + low + step_heads]
                for low in range(0, step_rows, step_heads)
            ],
            axis=1,
        )
        w_step[panel] = matmul(pick, step_panel).astype(bf16)
    pltpu.make_async_copy(w_pair, w_pair, sems.at[0]).wait()
    for panel in range(ring):
        w_x[panel] = matmul(w_pair[panel], same, ((0,), (0,))).astype(bf16)

    upper = one(iota((rows, rows), 0) <= iota((rows, rows), 1))
    widen = one(iota((lines, channels), 1) // head_size == iota((lines, channels), 0))
    half = rows // 2
    causal = iota((half, half), 0) >= iota((half, half), 1)
    lane_head = iota((rows, channels), 1) // head_size
    per_head = per_head_all[me]
    params = params_all[me]
    bias, decay = per_head[:, 0:1], per_head[:, 1:2]
    skip = params[tap_count + 1 : tap_count + 2]

    def tok_wait(block):
        pltpu.make_async_copy(tok.at[block], tok.at[block], sems.at[1 + block]).wait()

    def project(block):
        total_x = total_g = total_s = None
        each = panels // ring
        for panel in range(ring):
            piece = jnp.concatenate(
                [tok[block, panel * each + low] for low in range(each)], axis=1
            )
            term_x = matmul(piece, w_x[panel])
            term_g = matmul(piece, w_group[panel])
            term_s = matmul(w_step[panel], piece, ((1,), (1,)))
            total_x = term_x if total_x is None else total_x + term_x
            total_g = term_g if total_g is None else total_g + term_g
            total_s = term_s if total_s is None else total_s + term_s
        base = pl.multiple_of(block * rows, rows)
        x_all[pl.ds(base + rim, rows)] = total_x[:, :channels].astype(bf16).astype(f32)
        gate_all[block] = total_x[:, channels:].astype(bf16).astype(f32)
        g_all[pl.ds(base + rim, rows)] = total_g.astype(bf16).astype(f32)
        step_all[block] = total_s

    def conv(ref, base, taps, shift):
        window = ref[pl.ds(base, rows + rim)]
        first = rim - tap_count + 1
        running = shift
        for tap in range(tap_count):
            running = running + taps[tap : tap + 1] * window[first + tap : first + tap + rows]
        return silu(running).astype(bf16)

    def stretch(value, count):
        low = jnp.concatenate(parts_of(value, count), axis=0).astype(bf16)
        return matmul(low, jnp.concatenate([widen] * count, axis=0), ((0,), (0,)))

    def scan(block):
        base = pl.multiple_of(block * rows, rows)
        values = conv(x_all, base, params[:tap_count], params[tap_count : tap_count + 1])
        values = values.astype(f32)
        groups = conv(g_all, base, g_taps[...], g_shift[...])
        b_rows, c_rows = groups[:, :states], groups[:, states:]
        marks = shared[block, 2 * slab + step_rows :].astype(f32)
        bucket = jnp.concatenate(
            [marks[low : low + 1] for low in range(rows // LANES)], axis=1
        )
        raw_step = step_all[block] + bias
        for entry in range(PLACE_BINS):
            raw_step = raw_step + jnp.where(
                bucket == float(entry), per_head[:, 2 + entry : 3 + entry], 0.0
            )
        sizes = softplus(raw_step).astype(bf16).astype(f32)
        rates = jnp.concatenate(parts_of(-decay * sizes, 3), axis=0).astype(bf16)
        sums = matmul(rates, upper)
        cumulative = sums[:lines] + (sums[lines : 2 * lines] + sums[2 * lines :])
        last = cumulative[:, rows - 1 : rows]
        grown = stretch(jnp.exp(cumulative), 3)
        left = stretch(sizes * jnp.exp(last - cumulative), 3)
        driven = (stretch(sizes, 1) * values).astype(f32)
        scores = matmul(c_rows, b_rows, ((1,), (1,)))
        cum_parts = parts_of(cumulative, 3)
        ones = jnp.ones((3, rows), f32)
        pad = jnp.zeros((2, rows), f32)
        top, low_left, low_right, inputs = [], [], [], []
        for head in range(heads):
            mine = jnp.concatenate([p[head : head + 1] for p in cum_parts], axis=0)
            spread = matmul(
                jnp.concatenate([mine, ones, pad], axis=0).astype(bf16),
                jnp.concatenate([ones, -mine, pad], axis=0).astype(bf16),
                ((0,), (0,)),
            )
            decays = lambda part: jnp.exp(jnp.where(causal, part, -1e30))
            top.append((scores[:half, :half] * decays(spread[:half, :half])).astype(bf16))
            low_left.append((scores[half:, :half] * jnp.exp(spread[half:, :half])).astype(bf16))
            low_right.append((scores[half:, half:] * decays(spread[half:, half:])).astype(bf16))
            inputs.append(jnp.where(lane_head == head, driven, 0.0).astype(bf16))
        upper_in = jnp.concatenate([d[:half] for d in inputs], axis=0)
        lower_in = jnp.concatenate([d[half:] for d in inputs], axis=0)
        upper_out = matmul(jnp.concatenate(top, axis=1), upper_in)
        lower_out = matmul(
            jnp.concatenate(low_left + low_right, axis=1),
            jnp.concatenate([upper_in, lower_in], axis=0),
        )
        within = jnp.concatenate([upper_out, lower_out], axis=0)
        held = state[...]
        scanned = within + grown * matmul(c_rows, held.astype(bf16)) + skip * values
        scanned = scanned.astype(bf16).astype(f32)
        out[block] = (scanned * silu(gate_all[block])).astype(bf16)
        injected = matmul(b_rows, (left * values).astype(bf16), ((0,), (0,)))
        state[...] = grown[rows - 1 : rows] * held + injected

    tok_wait(0)
    project(0)

    def advance(block, carry):
        tok_wait(block + 1)
        scan(block)
        project(block + 1)
        return carry

    lax.fori_loop(0, ring - 1, advance, 0)
    scan(ring - 1)


def layer(head_size, tokens, columns, payloads, groups, per_head, params, g_taps, g_shift):
    ring, channels, slab = columns[0].shape
    wide = 2 * channels
    rows, depth = tokens.shape
    part = g_shift.shape[1]
    lines = per_head.shape[1]
    rim = 8
    total = ring * rows
    counts = [group[0].shape[0] for group in groups]
    pieces = [piece for group in groups for piece in group]
    shared_rows = payloads[0].shape[0] - payload_rows(tokens) * depth // LANES
    return pl.pallas_call(
        functools.partial(layer_kernel, head_size, counts),
        in_specs=[HBM] * (3 + len(payloads) + len(pieces)) + [VMEM] * 4,
        out_specs=VMEM,
        out_shape=jax.ShapeDtypeStruct((ring, rows, channels), bf16),
        scratch_shapes=[
            pltpu.VMEM((ring, depth // LANES, rows, LANES), bf16),
            pltpu.VMEM((ring, wide, slab), bf16),
            pltpu.VMEM((ring, shared_rows, LANES), bf16),
            pltpu.VMEM((ring, slab, wide), bf16),
            pltpu.VMEM((ring, slab, part), bf16),
            pltpu.VMEM((ring, lines, slab), bf16),
            pltpu.VMEM((rim + total, channels), f32),
            pltpu.VMEM((rim + total, part), f32),
            pltpu.VMEM((ring, rows, channels), f32),
            pltpu.VMEM((ring, lines, rows), f32),
            pltpu.VMEM((part // 2, channels), f32),
            pltpu.SemaphoreType.DMA((1 + 2 * ring,)),
        ],
        compiler_params=pltpu.CompilerParams(vmem_limit_bytes=60 * 1024 * 1024),
        cost_estimate=pl.CostEstimate(
            flops=2 * total * ring * slab * (wide + part),
            bytes_accessed=2 * total * ring * slab,
            transcendentals=0,
        ),
        name="layer",
    )(tokens, *columns, *payloads, *pieces, per_head, params, g_taps, g_shift)


def close_kernel(gated, gain, weight, keep, give, landing, sems):
    pieces, rows, width = gated.shape
    steps, _, columns = landing.shape
    seats = 4
    quarter = rows // seats
    copies = [
        pltpu.make_async_copy(
            weight.at[:, pl.ds(step * columns, columns)], landing.at[step], sems.at[step]
        )
        for step in range(steps)
    ]
    for copy in copies:
        copy.start()
    seat = lax.axis_index("mp")
    square = jnp.zeros((rows, width), f32)
    parts = []
    for piece in range(pieces):
        part = gated[piece].astype(f32)
        square = square + part * part
        parts.append((part * gain[:, piece * width : (piece + 1) * width]).astype(bf16))
    inputs = jnp.concatenate(parts, axis=1)
    mean = jnp.sum(square, axis=1, keepdims=True) * (1.0 / (pieces * width))
    scale = lax.rsqrt(mean + norm_epsilon)
    for step, copy in enumerate(copies):
        copy.wait()
        total = (matmul(inputs, landing[step]) * scale).astype(bf16)
        at = pl.ds(step * columns, columns)
        for core in range(2):

            @pl.when((seat & 1) == core)
            def _(core=core):
                for owner in range(seats):
                    block = total[owner * quarter : (owner + 1) * quarter]
                    target = keep if owner % 2 == core else give
                    target[(owner // 2) ^ (seat >> 1), :, at] = block


def close(gated, gain, weight):
    pieces, rows, width = gated.shape
    steps = 4
    depth, columns = weight.shape
    shape = jax.ShapeDtypeStruct((2, rows // 4, columns), bf16)
    return pl.pallas_call(
        close_kernel,
        in_specs=[VMEM, VMEM, HBM],
        out_specs=[VMEM, VMEM],
        out_shape=[shape, shape],
        scratch_shapes=[
            pltpu.VMEM((steps, depth, columns // steps), bf16),
            pltpu.SemaphoreType.DMA((steps,)),
        ],
        compiler_params=pltpu.CompilerParams(vmem_limit_bytes=60 * 1024 * 1024),
        cost_estimate=pl.CostEstimate(
            flops=2 * rows * weight.size, bytes_accessed=2 * weight.size, transcendentals=0
        ),
        name="close",
    )(gated, gain, weight)


def tokens_travel(
    tokens,
    gate_weight,
    input_weight,
    group_weight,
    step_weight,
    step_bias,
    bucket_table,
    bucket_ids,
    decay_rate,
    conv_input,
    conv_input_bias,
    conv_group,
    conv_group_bias,
    skip_gain,
    norm_gain,
    out_weight,
):
    rows, depth = tokens.shape
    slab = gate_weight.shape[0]
    heads_here = step_bias.shape[0]
    head_size = gate_weight.shape[2]
    state_size = group_weight.shape[3]
    tap_count = conv_input.shape[0]
    ring = lax.axis_size("seq")
    seats = lax.axis_size("mp")
    me = lax.axis_index("seq")
    channels = heads_here * head_size // ring
    heads = channels // head_size
    swap = lambda size, bit: [(i, i ^ bit) for i in range(size)]
    column = lambda pairs: [(2 * a + w, 2 * b + w) for a, b in pairs for w in range(2)]

    payload = pack(
        tokens,
        group_weight.reshape(2 * slab, state_size),
        jnp.transpose(step_weight),
        bucket_ids.reshape(rows // LANES, LANES),
    )
    inner = (me >= 2) & (me < 6)
    outward = column([(1, 0), (2, 3)])
    middle = column([(1, 2), (2, 1)])
    near = lax.ppermute(payload, "seq", swap(ring, 2))
    mid = lax.ppermute(payload, "seq", middle)
    across_own = lax.ppermute(payload, "seq", swap(ring, 1))

    by_channel = lambda w: jnp.transpose(w, (1, 2, 0)).reshape(ring, channels, slab)
    trade = lambda w: lax.all_to_all(w, "seq", split_axis=0, concat_axis=0, tiled=True)
    cross = lambda item: lax.ppermute(item, "seq", swap(ring, 1))
    x_weight, gate = by_channel(input_weight), by_channel(gate_weight)
    per_head = jnp.concatenate([jnp.stack([step_bias, decay_rate]), bucket_table], axis=0)
    per_head = jnp.transpose(per_head).reshape(ring, heads, -1)
    per_head = jnp.pad(per_head, ((0, 0), (0, 8 - heads), (0, 0)))
    params = jnp.concatenate(
        [
            conv_input,
            conv_input_bias[None],
            jnp.broadcast_to(skip_gain[None, :, None], (1, heads_here, head_size)),
        ],
        axis=0,
    )
    params = jnp.moveaxis(params.reshape(params.shape[0], ring, channels), 1, 0)
    g_taps = conv_group.reshape(tap_count, 2 * state_size)
    g_shift = conv_group_bias.reshape(1, 2 * state_size)
    after = lambda value, *others: lax.optimization_barrier((value,) + others)[0]
    quarter = payload_rows(tokens)
    panels = depth // LANES

    def spread(*items):
        own = jnp.stack(
            [item[: panels * quarter].reshape(panels, quarter, LANES) for item in items]
        )
        beside = lax.ppermute(own, "mp", swap(seats, 1))
        across = lax.ppermute(own, "mp", swap(seats, 2))
        return own, beside, across, lax.ppermute(across, "mp", swap(seats, 1))

    near, mid, across_own, x_weight, per_head, params, g_taps, g_shift = lax.optimization_barrier(
        (near, mid, across_own, x_weight, per_head, params, g_taps, g_shift)
    )
    mid_far = lax.ppermute(near, "seq", middle)
    out_near = lax.ppermute(mid, "seq", outward)
    across_near = cross(near)
    x_weight = trade(x_weight)
    groups = [spread(near, across_own)]

    out_far = lax.ppermute(mid_far, "seq", outward)
    second = jnp.where(inner, mid, out_near)
    groups.append(spread(second, across_near))
    gate = trade(after(gate, mid_far, x_weight))
    third = jnp.where(inner, mid_far, out_far)
    across_second = cross(after(second, across_near))
    third = after(third, groups[0][1], groups[0][3], groups[1][2], across_second)
    across_third = cross(third)
    groups.append(spread(third, across_second))
    across_third = after(across_third, groups[1][1], groups[1][3], groups[2][2])
    groups.append(spread(across_third))
    columns = [x_weight, gate]
    payloads = [payload, across_own, near, across_near, second, across_second, third, across_third]

    gated = layer(head_size, tokens, columns, payloads, groups, per_head, params, g_taps, g_shift)
    gated = lax.all_to_all(gated, "seq", split_axis=0, concat_axis=0, tiled=True)
    keep, give = close(gated, norm_gain.reshape(1, -1), out_weight.reshape(-1, depth))
    took = lax.ppermute(give, "mp", swap(seats, 1))
    send = (keep[1].astype(f32) + took[1].astype(f32)).astype(bf16)
    took_far = lax.ppermute(send, "mp", swap(seats, 2))
    return (keep[0].astype(f32) + took[0].astype(f32) + took_far.astype(f32)).astype(bf16)


def on_device(*arrays):
    tokens, gate_weight, group_weight = arrays[0], arrays[1], arrays[3]
    ring = lax.axis_size("seq")
    channels = gate_weight.shape[1] * gate_weight.shape[2] // ring
    weights = 2 * gate_weight.size + group_weight.size + arrays[4].size
    fits = (
        tokens.size <= weights
        and channels % 128 == 0
        and gate_weight.shape[0] == 2 * group_weight.shape[3] == tokens.shape[0]
        and channels % gate_weight.shape[2] == 0
        and group_weight.shape[1] == 1
        and lax.axis_size("mp") == 4
        and ring == 8
    )
    return (tokens_travel if fits else weights_travel)(*arrays)


def solution(mesh):
    placed = (
        P("seq", None),
        P("seq", "mp", None),
        P("seq", "mp", None),
        P("seq", "mp", None, None),
        P("seq", "mp"),
        P("mp"),
        P(None, "mp"),
        P("seq"),
        P("mp"),
        P(None, "mp", None),
        P("mp", None),
        P(None, "mp", None, None),
        P("mp", None, None),
        P("mp"),
        P("mp", None),
        P("mp", None, None),
    )
    return jax.shard_map(
        on_device, mesh=mesh, in_specs=placed, out_specs=P(("seq", "mp"), None), check_vma=False
    )
```

```python
import functools

import jax
import jax.numpy as jnp
from jax import lax
from jax.experimental import pallas as pl
from jax.experimental.pallas import tpu as pltpu
from jax.sharding import PartitionSpec as P

SPAN = 256
PLACE_BINS = 4


norm_epsilon = 1e-05
highest = lax.Precision.HIGHEST


def causal_conv(raw_rows, rim_rows, tap_weights, tap_bias):
    extended = jnp.concatenate([rim_rows, raw_rows], axis=0).astype(jnp.float32)
    row_count = raw_rows.shape[0]
    tap_count = tap_weights.shape[0]
    running = (
        tap_bias[None, :]
        + tap_weights[tap_count - 1][None, :] * extended[tap_count - 1 : tap_count - 1 + row_count]
    )
    for tap_index in range(tap_count - 1):
        running = (
            running + tap_weights[tap_index][None, :] * extended[tap_index : tap_index + row_count]
        )
    return jax.nn.silu(running).astype(jnp.bfloat16)


def ssd_block(carried_state, block_inputs, decay_neg):
    block_values, block_b, block_c, block_steps = block_inputs
    step_rates = block_steps.astype(jnp.float32) * decay_neg[None, :]
    cumulative = jnp.cumsum(step_rates, axis=0)
    scores = jnp.einsum("tn,sn->ts", block_c, block_b, preferred_element_type=jnp.float32)
    by_head = jnp.transpose(cumulative)
    spread = by_head[:, :, None] - by_head[:, None, :]
    block_rows = block_values.shape[0]
    causal = (jnp.arange(block_rows)[:, None] >= jnp.arange(block_rows)[None, :])[None]
    decays = jnp.where(causal, jnp.exp(jnp.where(causal, spread, 0.0)), 0.0)
    mixing = scores[None] * decays
    driven = block_steps.astype(jnp.float32)[:, :, None] * block_values.astype(jnp.float32)
    within = jnp.einsum("rts,srp->trp", mixing, driven, precision=highest)
    readout = jnp.einsum(
        "tn,rpn->trp", block_c.astype(jnp.float32), carried_state, precision=highest
    )
    outputs = within + jnp.exp(cumulative)[:, :, None] * readout
    remaining = jnp.exp(cumulative[-1][None, :] - cumulative)
    injected = jnp.einsum(
        "srp,sn->rpn",
        driven * remaining[:, :, None],
        block_b.astype(jnp.float32),
        precision=highest,
    )
    next_state = jnp.exp(cumulative[-1])[:, None, None] * carried_state + injected
    return (next_state, outputs)


def ssd_group(start_state, group_values, group_b, group_c, group_steps, decay_neg):
    row_total = group_values.shape[0]
    block_count = row_total // SPAN

    def advance(carried_state, block_inputs):
        return ssd_block(carried_state, block_inputs, decay_neg)

    blocked = (
        group_values.reshape((block_count, SPAN) + group_values.shape[1:]),
        group_b.reshape(block_count, SPAN, -1),
        group_c.reshape(block_count, SPAN, -1),
        group_steps.reshape(block_count, SPAN, -1),
    )
    final_state, outputs = lax.scan(advance, start_state, blocked)
    return (final_state, outputs.reshape((row_total,) + outputs.shape[2:]))


def weights_travel(
    tokens,
    gate_weight,
    input_weight,
    group_weight,
    step_weight,
    step_bias,
    bucket_table,
    bucket_ids,
    decay_rate,
    conv_input,
    conv_input_bias,
    conv_group,
    conv_group_bias,
    skip_gain,
    norm_gain,
    out_weight,
):
    tok_rows = tokens.shape[0]
    heads_here = step_bias.shape[0]
    groups_here = group_weight.shape[1]
    per_group = heads_here // groups_here
    head_size = gate_weight.shape[2]
    state_size = group_weight.shape[3]
    tap_count = conv_input.shape[0]
    channel_width = heads_here * head_size
    group_width = groups_here * 2 * state_size
    pieces = (
        lax.all_gather(gate_weight, "seq", axis=0, tiled=True),
        lax.all_gather(input_weight, "seq", axis=0, tiled=True),
        lax.all_gather(group_weight, "seq", axis=0, tiled=True),
        lax.all_gather(step_weight, "seq", axis=0, tiled=True),
    )
    rows_here = pieces[0].shape[0]
    gate_sum, input_sum, group_sum, step_sum = tuple(
        (
            jnp.dot(tokens, piece.reshape(rows_here, -1), preferred_element_type=jnp.float32)
            for piece in pieces
        )
    )
    gate_act = gate_sum.astype(jnp.bfloat16)
    input_raw = input_sum.astype(jnp.bfloat16)
    group_raw = group_sum.astype(jnp.bfloat16)
    onehot = (bucket_ids[:, None] == jnp.arange(PLACE_BINS, dtype=jnp.int32)[None, :]).astype(
        jnp.float32
    )
    offsets = jnp.dot(onehot, bucket_table, precision=highest)
    steps_tok = jax.nn.softplus(step_sum + step_bias[None, :] + offsets).astype(jnp.bfloat16)
    decay_neg = -decay_rate
    seq_count = lax.axis_size("seq")
    piece_width = channel_width // seq_count
    sub_width = min(piece_width, head_size)
    sub_count = piece_width // sub_width
    subs_per_head = head_size // sub_width
    steps_sub = jnp.repeat(steps_tok, subs_per_head, axis=1)
    wide_groups = jnp.broadcast_to(
        group_raw[:, None, :], (tok_rows, seq_count, group_width)
    ).reshape(tok_rows, seq_count * group_width)
    head_inputs, head_steps, head_groups = (
        lax.all_to_all(input_raw, "seq", split_axis=1, concat_axis=0, tiled=True),
        lax.all_to_all(steps_sub, "seq", split_axis=1, concat_axis=0, tiled=True),
        lax.all_to_all(wide_groups, "seq", split_axis=1, concat_axis=0, tiled=True),
    )
    seq_total = head_inputs.shape[0]
    first_channel = lax.axis_index("seq") * piece_width
    input_taps = lax.dynamic_slice_in_dim(
        conv_input.reshape(tap_count, -1), first_channel, piece_width, 1
    )
    input_shift = lax.dynamic_slice_in_dim(
        conv_input_bias.reshape(-1), first_channel, piece_width, 0
    )
    conv_values = causal_conv(
        head_inputs, jnp.zeros((tap_count - 1, piece_width), jnp.bfloat16), input_taps, input_shift
    )
    conv_groups = causal_conv(
        head_groups,
        jnp.zeros((tap_count - 1, group_width), jnp.bfloat16),
        conv_group.reshape(tap_count, -1),
        conv_group_bias.reshape(-1),
    )
    conv_groups = conv_groups.reshape(seq_total, groups_here, 2, state_size)
    sub_heads = (first_channel + jnp.arange(sub_count, dtype=jnp.int32) * sub_width) // head_size
    sub_groups = sub_heads // per_group
    sub_decay = jnp.take(decay_neg, sub_heads)[:, None]
    sub_skip = jnp.take(skip_gain, sub_heads)
    values_sub = jnp.moveaxis(conv_values.reshape(seq_total, sub_count, 1, sub_width), 1, 0)
    steps_heads = jnp.moveaxis(head_steps, 1, 0)[:, :, None]

    def run_sub(member):
        chosen = lax.dynamic_index_in_dim(conv_groups, member[3], 1, False)
        start_state = jnp.zeros((1, sub_width, state_size), jnp.float32)
        return ssd_group(start_state, member[0], chosen[:, 0], chosen[:, 1], member[1], member[2])[
            1
        ]

    scanned = jnp.moveaxis(
        lax.map(run_sub, (values_sub, steps_heads, sub_decay, sub_groups)), 0, 1
    ).reshape(seq_total, sub_count, sub_width)
    head_out = (
        scanned
        + sub_skip[None, :, None]
        * conv_values.reshape(seq_total, sub_count, sub_width).astype(jnp.float32)
    ).astype(jnp.bfloat16)
    ssd_out = lax.all_to_all(
        head_out.reshape(seq_total, piece_width), "seq", split_axis=0, concat_axis=1, tiled=True
    )
    gated_out = ssd_out.astype(jnp.float32) * jax.nn.silu(gate_act.astype(jnp.float32))
    grouped = gated_out.reshape(tok_rows, groups_here, -1)
    mean_square = jnp.mean(grouped * grouped, axis=2)
    scales = lax.rsqrt(mean_square + norm_epsilon)
    normed = (
        (grouped * scales[:, :, None]).reshape(tok_rows, -1) * norm_gain.reshape(-1)[None, :]
    ).astype(jnp.bfloat16)
    flat_out = out_weight.reshape(-1, out_weight.shape[2])
    layer_out = lax.psum_scatter(
        jnp.dot(normed, flat_out, preferred_element_type=jnp.float32).astype(jnp.bfloat16),
        "mp",
        scatter_dimension=0,
        tiled=True,
    )
    return layer_out


bf16 = jnp.bfloat16
f32 = jnp.float32
ROW_PAD = 16
LANES = 128


def matmul(left, right, dims=((1,), (0,))):
    return lax.dot_general(left, right, (dims, ((), ())), preferred_element_type=f32)


def softplus(value):
    return jnp.maximum(value, 0.0) + jnp.log1p(jnp.exp(-jnp.abs(value)))


def silu(value):
    return 0.5 * value * (1.0 + jnp.tanh(0.5 * value))


def parts_of(value, count):
    parts = []
    for _ in range(count):
        part = value.astype(bf16).astype(f32)
        parts.append(part)
        value = value - part
    return parts


HBM = pl.BlockSpec(memory_space=pl.ANY)
VMEM = pl.BlockSpec(memory_space=pltpu.VMEM)


def pack_kernel(tokens, groups, steps, ids, payload, mine, sem):
    rows, depth = mine.shape
    seat = lax.axis_index("mp")
    copy = pltpu.make_async_copy(
        tokens.at[pl.ds(pl.multiple_of(seat * rows, rows), rows)], mine, sem
    )
    copy.start()
    panels = depth // LANES
    low = panels * rows
    payload[low : low + groups.shape[0]] = groups[...]
    low += groups.shape[0]
    high = steps.shape[0]
    for part in range(steps.shape[1] // LANES):
        payload[low : low + high] = steps[:, part * LANES : (part + 1) * LANES]
        low += high
    marks = ids[...].astype(f32)
    rest = jnp.zeros((ROW_PAD - marks.shape[0], LANES), f32)
    payload[low:] = jnp.concatenate([marks, rest], axis=0).astype(bf16)
    copy.wait()
    for panel in range(panels):
        payload[panel * rows : (panel + 1) * rows] = mine[:, panel * LANES : (panel + 1) * LANES]


def payload_rows(tokens):
    return tokens.shape[0] // 4


def pack(tokens, groups, steps, ids):
    rows, depth = tokens.shape
    extra = steps.size // LANES + ROW_PAD
    full = payload_rows(tokens) * depth // LANES + groups.shape[0] + extra
    return pl.pallas_call(
        pack_kernel,
        in_specs=[HBM, VMEM, VMEM, VMEM],
        out_specs=VMEM,
        out_shape=jax.ShapeDtypeStruct((full, LANES), bf16),
        scratch_shapes=[
            pltpu.VMEM((payload_rows(tokens), depth), bf16),
            pltpu.SemaphoreType.DMA,
        ],
        name="pack",
    )(tokens, groups, steps, ids)


def layer_kernel(head_size, counts, tokens, *refs):
    columns, refs = refs[:2], refs[2:]
    ring, channels, slab = columns[0].shape
    payloads, refs = refs[:ring], refs[ring:]
    pieces, refs = refs[: 4 * len(counts)], refs[4 * len(counts) :]
    per_head_all, params_all, g_taps, g_shift, out = refs[:5]
    tok, shared, w_x, w_group, w_step, x_all, g_all, gate_all, step_all, state, sems = refs[5:]
    seats = 4
    rows = out.shape[1]
    quarter = rows // seats
    panels = tok.shape[1]
    height = panels * quarter
    part = 2 * g_shift.shape[1] // 2
    states = part // 2
    heads = channels // head_size
    lines = w_step.shape[1]
    tap_count = g_taps.shape[0]
    rim = x_all.shape[0] - ring * rows
    step_rows = shared.shape[1] - 2 * slab - ROW_PAD
    step_heads = step_rows * LANES // slab
    me = lax.axis_index("seq")
    seat = lax.axis_index("mp")
    beside = me & 1
    upper_half = me >> 2
    sources = [me, me ^ 1]
    for other in ((me >> 1) ^ 1, 2 - upper_half, 3 - 3 * upper_half):
        sources += [2 * other + beside, 2 * other + 1 - beside]

    arrivals = [2, 1, 4, 3, 6, 5, 7]
    shared_copies = []
    for order in range(ring):
        copy = pltpu.make_async_copy(
            payloads[order].at[pl.ds(height, shared.shape[1])],
            shared.at[sources[order]],
            sems.at[1 + ring + order],
        )
        copy.start()
        shared_copies.append(copy)
    for kind in range(2):
        pltpu.make_async_copy(
            columns[kind], w_x.at[:, pl.ds(kind * channels, channels)], sems.at[0]
        ).start()
    for panel in range(panels):
        pltpu.make_async_copy(
            tokens.at[:, pl.ds(panel * LANES, LANES)], tok.at[me, panel], sems.at[1 + me]
        ).start()
    order = 0
    for group, count in enumerate(counts):
        for at in range(count):
            source = sources[arrivals[order]]
            for hop in range(seats):
                first = pl.multiple_of((seat ^ hop) * quarter, quarter)
                pltpu.make_async_copy(
                    pieces[4 * group + hop].at[at],
                    tok.at[source, :, pl.ds(first, quarter)],
                    sems.at[1 + source],
                ).start()
            order += 1

    x_all[:rim] = jnp.zeros((rim, channels), f32)
    g_all[:rim] = jnp.zeros((rim, part), f32)
    state[...] = jnp.zeros_like(state)
    one = lambda flag: flag.astype(f32).astype(bf16)
    iota = lambda shape, dim: lax.broadcasted_iota(jnp.int32, shape, dim)
    pick = one(
        (iota((lines, step_heads), 0) + me * heads == iota((lines, step_heads), 1))
        & (iota((lines, step_heads), 0) < heads)
    )
    unpick = [
        one(2 * iota((slab, 2 * slab), 0) + kind == iota((slab, 2 * slab), 1)) for kind in range(2)
    ]
    for copy in shared_copies:
        copy.wait()
    for panel in range(ring):
        slab_rows = shared[panel, : 2 * slab]
        for kind in range(2):
            w_group[panel, :, kind * states : (kind + 1) * states] = matmul(
                unpick[kind], slab_rows
            ).astype(bf16)
        step_panel = jnp.concatenate(
            [
                shared[panel, 2 * slab + low : 2 * slab + low + step_heads]
                for low in range(0, step_rows, step_heads)
            ],
            axis=1,
        )
        w_step[panel] = matmul(pick, step_panel).astype(bf16)
    pltpu.make_async_copy(w_x, w_x, sems.at[0]).wait()

    upper = one(iota((rows, rows), 0) <= iota((rows, rows), 1))
    widen = one(iota((lines, channels), 1) // head_size == iota((lines, channels), 0))
    half = rows // 2
    causal = iota((half, half), 0) >= iota((half, half), 1)
    lane_head = iota((rows, channels), 1) // head_size
    per_head = per_head_all[me]
    params = params_all[me]
    bias, decay = per_head[:, 0:1], per_head[:, 1:2]
    skip = params[tap_count + 1 : tap_count + 2]

    def tok_wait(block):
        pltpu.make_async_copy(tok.at[block], tok.at[block], sems.at[1 + block]).wait()

    def project(block):
        total_x = total_g = total_s = None
        each = panels // ring
        for panel in range(ring):
            piece = jnp.concatenate(
                [tok[block, panel * each + low] for low in range(each)], axis=1
            )
            term_x = matmul(piece, w_x[panel], ((1,), (1,)))
            term_g = matmul(piece, w_group[panel])
            term_s = matmul(w_step[panel], piece, ((1,), (1,)))
            total_x = term_x if total_x is None else total_x + term_x
            total_g = term_g if total_g is None else total_g + term_g
            total_s = term_s if total_s is None else total_s + term_s
        base = pl.multiple_of(block * rows, rows)
        x_all[pl.ds(base + rim, rows)] = total_x[:, :channels].astype(bf16).astype(f32)
        gate_all[block] = total_x[:, channels:].astype(bf16).astype(f32)
        g_all[pl.ds(base + rim, rows)] = total_g.astype(bf16).astype(f32)
        step_all[block] = total_s

    def conv(ref, base, taps, shift):
        window = ref[pl.ds(base, rows + rim)]
        first = rim - tap_count + 1
        running = shift
        for tap in range(tap_count):
            running = running + taps[tap : tap + 1] * window[first + tap : first + tap + rows]
        return silu(running).astype(bf16)

    def stretch(value, count):
        low = jnp.concatenate(parts_of(value, count), axis=0).astype(bf16)
        return matmul(low, jnp.concatenate([widen] * count, axis=0), ((0,), (0,)))

    def scan(block):
        base = pl.multiple_of(block * rows, rows)
        values = conv(x_all, base, params[:tap_count], params[tap_count : tap_count + 1])
        values = values.astype(f32)
        groups = conv(g_all, base, g_taps[...], g_shift[...])
        b_rows, c_rows = groups[:, :states], groups[:, states:]
        marks = shared[block, 2 * slab + step_rows :].astype(f32)
        bucket = jnp.concatenate(
            [marks[low : low + 1] for low in range(rows // LANES)], axis=1
        )
        raw_step = step_all[block] + bias
        for entry in range(PLACE_BINS):
            raw_step = raw_step + jnp.where(
                bucket == float(entry), per_head[:, 2 + entry : 3 + entry], 0.0
            )
        sizes = softplus(raw_step).astype(bf16).astype(f32)
        rates = jnp.concatenate(parts_of(-decay * sizes, 3), axis=0).astype(bf16)
        sums = matmul(rates, upper)
        cumulative = sums[:lines] + (sums[lines : 2 * lines] + sums[2 * lines :])
        last = cumulative[:, rows - 1 : rows]
        grown = stretch(jnp.exp(cumulative), 3)
        left = stretch(sizes * jnp.exp(last - cumulative), 3)
        driven = (stretch(sizes, 1) * values).astype(f32)
        scores = matmul(c_rows, b_rows, ((1,), (1,)))
        cum_parts = parts_of(cumulative, 3)
        ones = jnp.ones((3, rows), f32)
        pad = jnp.zeros((2, rows), f32)
        top, low_left, low_right, inputs = [], [], [], []
        for head in range(heads):
            mine = jnp.concatenate([p[head : head + 1] for p in cum_parts], axis=0)
            spread = matmul(
                jnp.concatenate([mine, ones, pad], axis=0).astype(bf16),
                jnp.concatenate([ones, -mine, pad], axis=0).astype(bf16),
                ((0,), (0,)),
            )
            decays = lambda part: jnp.exp(jnp.where(causal, part, -1e30))
            top.append((scores[:half, :half] * decays(spread[:half, :half])).astype(bf16))
            low_left.append((scores[half:, :half] * jnp.exp(spread[half:, :half])).astype(bf16))
            low_right.append((scores[half:, half:] * decays(spread[half:, half:])).astype(bf16))
            inputs.append(jnp.where(lane_head == head, driven, 0.0).astype(bf16))
        upper_in = jnp.concatenate([d[:half] for d in inputs], axis=0)
        lower_in = jnp.concatenate([d[half:] for d in inputs], axis=0)
        upper_out = matmul(jnp.concatenate(top, axis=1), upper_in)
        lower_out = matmul(
            jnp.concatenate(low_left + low_right, axis=1),
            jnp.concatenate([upper_in, lower_in], axis=0),
        )
        within = jnp.concatenate([upper_out, lower_out], axis=0)
        held = state[...]
        scanned = within + grown * matmul(c_rows, held.astype(bf16)) + skip * values
        scanned = scanned.astype(bf16).astype(f32)
        out[me ^ block] = (scanned * silu(gate_all[block])).astype(bf16)
        injected = matmul(b_rows, (left * values).astype(bf16), ((0,), (0,)))
        state[...] = grown[rows - 1 : rows] * held + injected

    def project_step(step, carry):
        for low in range(1):
            tok_wait(1 * step + low)
            project(1 * step + low)
        return carry

    lax.fori_loop(0, ring // 1, project_step, 0)

    def advance(step, carry):
        for low in range(8):
            scan(8 * step + low)
        return carry

    lax.fori_loop(0, ring // 8, advance, 0)


def layer(head_size, tokens, columns, payloads, groups, per_head, params, g_taps, g_shift):
    ring, channels, slab = columns[0].shape
    wide = 2 * channels
    rows, depth = tokens.shape
    part = g_shift.shape[1]
    lines = per_head.shape[1]
    rim = 8
    total = ring * rows
    counts = [group[0].shape[0] for group in groups]
    pieces = [piece for group in groups for piece in group]
    shared_rows = payloads[0].shape[0] - payload_rows(tokens) * depth // LANES
    return pl.pallas_call(
        functools.partial(layer_kernel, head_size, counts),
        in_specs=[HBM] * (3 + len(payloads) + len(pieces)) + [VMEM] * 4,
        out_specs=VMEM,
        out_shape=jax.ShapeDtypeStruct((ring, rows, channels), bf16),
        scratch_shapes=[
            pltpu.VMEM((ring, depth // LANES, rows, LANES), bf16),
            pltpu.VMEM((ring, shared_rows, LANES), bf16),
            pltpu.VMEM((ring, wide, slab), bf16),
            pltpu.VMEM((ring, slab, part), bf16),
            pltpu.VMEM((ring, lines, slab), bf16),
            pltpu.VMEM((rim + total, channels), f32),
            pltpu.VMEM((rim + total, part), f32),
            pltpu.VMEM((ring, rows, channels), f32),
            pltpu.VMEM((ring, lines, rows), f32),
            pltpu.VMEM((part // 2, channels), f32),
            pltpu.SemaphoreType.DMA((1 + 2 * ring,)),
        ],
        compiler_params=pltpu.CompilerParams(vmem_limit_bytes=60 * 1024 * 1024),
        cost_estimate=pl.CostEstimate(
            flops=2 * total * ring * slab * (wide + part),
            bytes_accessed=2 * total * ring * slab,
            transcendentals=0,
        ),
        name="layer",
    )(tokens, *columns, *payloads, *pieces, per_head, params, g_taps, g_shift)


def close_kernel(offsets, gain, weight, *refs):
    parts, (keep, give, inputs) = refs[:-3], refs[-3:]
    rows, width = parts[0].shape
    seats = 4
    quarter = rows // seats
    columns = weight.shape[1] // 4
    me = lax.axis_index("seq")
    seat = lax.axis_index("mp")
    square = jnp.zeros((rows, width), f32)
    for offset, part in zip(offsets, parts):
        value = part[...].astype(f32)
        square = square + value * value
        at = pl.multiple_of((me ^ offset) * width, width)
        inputs[:, pl.ds(at, width)] = (value * gain[:, pl.ds(at, width)]).astype(bf16)
    mean = jnp.sum(square, axis=1, keepdims=True) * (1.0 / (len(parts) * width))
    scale = lax.rsqrt(mean + norm_epsilon)
    for step in range(4):
        at = pl.ds(step * columns, columns)
        total = (matmul(inputs[...], weight[:, at]) * scale).astype(bf16)
        for core in range(2):

            @pl.when((seat & 1) == core)
            def _(core=core):
                for owner in range(seats):
                    block = total[owner * quarter : (owner + 1) * quarter]
                    target = keep if owner % 2 == core else give
                    target[(owner // 2) ^ (seat >> 1), :, at] = block


def close(offsets, gain, weight, parts):
    rows, width = parts[0].shape
    shape = jax.ShapeDtypeStruct((2, rows // 4, weight.shape[1]), bf16)
    return pl.pallas_call(
        functools.partial(close_kernel, offsets),
        in_specs=[VMEM] * (2 + len(parts)),
        out_specs=[VMEM] * 2,
        out_shape=[shape, shape],
        scratch_shapes=[pltpu.VMEM((rows, len(parts) * width), bf16)],
        compiler_params=pltpu.CompilerParams(vmem_limit_bytes=16 * 1024 * 1024),
        cost_estimate=pl.CostEstimate(
            flops=2 * rows * weight.size, bytes_accessed=2 * weight.size, transcendentals=0
        ),
        name="close",
    )(gain, weight, *parts)


def tokens_travel(
    tokens,
    gate_weight,
    input_weight,
    group_weight,
    step_weight,
    step_bias,
    bucket_table,
    bucket_ids,
    decay_rate,
    conv_input,
    conv_input_bias,
    conv_group,
    conv_group_bias,
    skip_gain,
    norm_gain,
    out_weight,
):
    rows, depth = tokens.shape
    slab = gate_weight.shape[0]
    heads_here = step_bias.shape[0]
    head_size = gate_weight.shape[2]
    state_size = group_weight.shape[3]
    tap_count = conv_input.shape[0]
    ring = lax.axis_size("seq")
    seats = lax.axis_size("mp")
    me = lax.axis_index("seq")
    channels = heads_here * head_size // ring
    heads = channels // head_size
    swap = lambda size, bit: [(i, i ^ bit) for i in range(size)]
    column = lambda pairs: [(2 * a + w, 2 * b + w) for a, b in pairs for w in range(2)]

    payload = pack(
        tokens,
        group_weight.reshape(2 * slab, state_size),
        jnp.transpose(step_weight),
        bucket_ids.reshape(rows // LANES, LANES),
    )
    inner = (me >= 2) & (me < 6)
    outward = column([(1, 0), (2, 3)])
    middle = column([(1, 2), (2, 1)])
    near = lax.ppermute(payload, "seq", swap(ring, 2))
    mid = lax.ppermute(payload, "seq", middle)
    across_own = lax.ppermute(payload, "seq", swap(ring, 1))

    by_channel = lambda w: jnp.transpose(w, (1, 2, 0)).reshape(ring, channels, slab)
    trade = lambda w: lax.all_to_all(w, "seq", split_axis=0, concat_axis=0, tiled=True)
    cross = lambda item: lax.ppermute(item, "seq", swap(ring, 1))
    x_weight, gate = by_channel(input_weight), by_channel(gate_weight)
    per_head = jnp.concatenate([jnp.stack([step_bias, decay_rate]), bucket_table], axis=0)
    per_head = jnp.transpose(per_head).reshape(ring, heads, -1)
    per_head = jnp.pad(per_head, ((0, 0), (0, 8 - heads), (0, 0)))
    params = jnp.concatenate(
        [
            conv_input,
            conv_input_bias[None],
            jnp.broadcast_to(skip_gain[None, :, None], (1, heads_here, head_size)),
        ],
        axis=0,
    )
    params = jnp.moveaxis(params.reshape(params.shape[0], ring, channels), 1, 0)
    g_taps = conv_group.reshape(tap_count, 2 * state_size)
    g_shift = conv_group_bias.reshape(1, 2 * state_size)
    after = lambda value, *others: lax.optimization_barrier((value,) + others)[0]
    quarter = payload_rows(tokens)
    panels = depth // LANES

    def spread(*items):
        own = jnp.stack(
            [item[: panels * quarter].reshape(panels, quarter, LANES) for item in items]
        )
        beside = lax.ppermute(own, "mp", swap(seats, 1))
        across = lax.ppermute(own, "mp", swap(seats, 2))
        return own, beside, across, lax.ppermute(across, "mp", swap(seats, 1))

    near, mid, across_own, x_weight, per_head, params, g_taps, g_shift = lax.optimization_barrier(
        (near, mid, across_own, x_weight, per_head, params, g_taps, g_shift)
    )
    mid_far = lax.ppermute(near, "seq", middle)
    out_near = lax.ppermute(mid, "seq", outward)
    across_near = cross(near)
    x_weight = trade(x_weight)
    groups = [spread(near, across_own)]

    out_far = lax.ppermute(mid_far, "seq", outward)
    second = jnp.where(inner, mid, out_near)
    groups.append(spread(second, across_near))
    gate = trade(after(gate, mid_far, x_weight))
    third = jnp.where(inner, mid_far, out_far)
    across_second = cross(after(second, across_near))
    third = after(third, groups[0][1], groups[0][3], groups[1][2], across_second)
    across_third = cross(third)
    groups.append(spread(third, across_second))
    across_third = after(across_third, groups[1][1], groups[1][3], groups[2][2])
    groups.append(spread(across_third))
    columns = [x_weight, gate]
    payloads = [payload, across_own, near, across_near, second, across_second, third, across_third]

    gated = layer(head_size, tokens, columns, payloads, groups, per_head, params, g_taps, g_shift)
    offsets = (6, 7, 5, 4, 3, 2, 1)
    parts = [lax.ppermute(gated[at], "seq", swap(ring, at)) for at in offsets] + [gated[0]]
    gain, weight = norm_gain.reshape(1, -1), out_weight.reshape(-1, depth)
    keep, give = close(offsets + (0,), gain, weight, parts)
    took = lax.ppermute(give, "mp", swap(seats, 1))
    send = (keep[1].astype(f32) + took[1].astype(f32)).astype(bf16)
    took_far = lax.ppermute(send, "mp", swap(seats, 2))
    return (keep[0].astype(f32) + took[0].astype(f32) + took_far.astype(f32)).astype(bf16)


def on_device(*arrays):
    tokens, gate_weight, group_weight = arrays[0], arrays[1], arrays[3]
    ring = lax.axis_size("seq")
    channels = gate_weight.shape[1] * gate_weight.shape[2] // ring
    weights = 2 * gate_weight.size + group_weight.size + arrays[4].size
    fits = (
        tokens.size <= weights
        and channels % 128 == 0
        and gate_weight.shape[0] == 2 * group_weight.shape[3] == tokens.shape[0]
        and channels % gate_weight.shape[2] == 0
        and group_weight.shape[1] == 1
        and lax.axis_size("mp") == 4
        and ring == 8
    )
    return (tokens_travel if fits else weights_travel)(*arrays)


def solution(mesh):
    placed = (
        P("seq", None),
        P("seq", "mp", None),
        P("seq", "mp", None),
        P("seq", "mp", None, None),
        P("seq", "mp"),
        P("mp"),
        P(None, "mp"),
        P("seq"),
        P("mp"),
        P(None, "mp", None),
        P("mp", None),
        P(None, "mp", None, None),
        P("mp", None, None),
        P("mp"),
        P("mp", None),
        P("mp", None, None),
    )
    return jax.shard_map(
        on_device, mesh=mesh, in_specs=placed, out_specs=P(("seq", "mp"), None), check_vma=False
    )
```

```python
import functools

import jax
import jax.numpy as jnp
from jax import lax
from jax.experimental import pallas as pl
from jax.experimental.pallas import tpu as pltpu
from jax.sharding import PartitionSpec as P

SPAN = 256
PLACE_BINS = 4


norm_epsilon = 1e-05
highest = lax.Precision.HIGHEST


def causal_conv(raw_rows, rim_rows, tap_weights, tap_bias):
    extended = jnp.concatenate([rim_rows, raw_rows], axis=0).astype(jnp.float32)
    row_count = raw_rows.shape[0]
    tap_count = tap_weights.shape[0]
    running = (
        tap_bias[None, :]
        + tap_weights[tap_count - 1][None, :] * extended[tap_count - 1 : tap_count - 1 + row_count]
    )
    for tap_index in range(tap_count - 1):
        running = (
            running + tap_weights[tap_index][None, :] * extended[tap_index : tap_index + row_count]
        )
    return jax.nn.silu(running).astype(jnp.bfloat16)


def ssd_block(carried_state, block_inputs, decay_neg):
    block_values, block_b, block_c, block_steps = block_inputs
    step_rates = block_steps.astype(jnp.float32) * decay_neg[None, :]
    cumulative = jnp.cumsum(step_rates, axis=0)
    scores = jnp.einsum("tn,sn->ts", block_c, block_b, preferred_element_type=jnp.float32)
    by_head = jnp.transpose(cumulative)
    spread = by_head[:, :, None] - by_head[:, None, :]
    block_rows = block_values.shape[0]
    causal = (jnp.arange(block_rows)[:, None] >= jnp.arange(block_rows)[None, :])[None]
    decays = jnp.where(causal, jnp.exp(jnp.where(causal, spread, 0.0)), 0.0)
    mixing = scores[None] * decays
    driven = block_steps.astype(jnp.float32)[:, :, None] * block_values.astype(jnp.float32)
    within = jnp.einsum("rts,srp->trp", mixing, driven, precision=highest)
    readout = jnp.einsum(
        "tn,rpn->trp", block_c.astype(jnp.float32), carried_state, precision=highest
    )
    outputs = within + jnp.exp(cumulative)[:, :, None] * readout
    remaining = jnp.exp(cumulative[-1][None, :] - cumulative)
    injected = jnp.einsum(
        "srp,sn->rpn",
        driven * remaining[:, :, None],
        block_b.astype(jnp.float32),
        precision=highest,
    )
    next_state = jnp.exp(cumulative[-1])[:, None, None] * carried_state + injected
    return (next_state, outputs)


def ssd_group(start_state, group_values, group_b, group_c, group_steps, decay_neg):
    row_total = group_values.shape[0]
    block_count = row_total // SPAN

    def advance(carried_state, block_inputs):
        return ssd_block(carried_state, block_inputs, decay_neg)

    blocked = (
        group_values.reshape((block_count, SPAN) + group_values.shape[1:]),
        group_b.reshape(block_count, SPAN, -1),
        group_c.reshape(block_count, SPAN, -1),
        group_steps.reshape(block_count, SPAN, -1),
    )
    final_state, outputs = lax.scan(advance, start_state, blocked)
    return (final_state, outputs.reshape((row_total,) + outputs.shape[2:]))


def weights_travel(
    tokens,
    gate_weight,
    input_weight,
    group_weight,
    step_weight,
    step_bias,
    bucket_table,
    bucket_ids,
    decay_rate,
    conv_input,
    conv_input_bias,
    conv_group,
    conv_group_bias,
    skip_gain,
    norm_gain,
    out_weight,
):
    tok_rows = tokens.shape[0]
    heads_here = step_bias.shape[0]
    groups_here = group_weight.shape[1]
    per_group = heads_here // groups_here
    head_size = gate_weight.shape[2]
    state_size = group_weight.shape[3]
    tap_count = conv_input.shape[0]
    channel_width = heads_here * head_size
    group_width = groups_here * 2 * state_size
    pieces = (
        lax.all_gather(gate_weight, "seq", axis=0, tiled=True),
        lax.all_gather(input_weight, "seq", axis=0, tiled=True),
        lax.all_gather(group_weight, "seq", axis=0, tiled=True),
        lax.all_gather(step_weight, "seq", axis=0, tiled=True),
    )
    rows_here = pieces[0].shape[0]
    gate_sum, input_sum, group_sum, step_sum = tuple(
        (
            jnp.dot(tokens, piece.reshape(rows_here, -1), preferred_element_type=jnp.float32)
            for piece in pieces
        )
    )
    gate_act = gate_sum.astype(jnp.bfloat16)
    input_raw = input_sum.astype(jnp.bfloat16)
    group_raw = group_sum.astype(jnp.bfloat16)
    onehot = (bucket_ids[:, None] == jnp.arange(PLACE_BINS, dtype=jnp.int32)[None, :]).astype(
        jnp.float32
    )
    offsets = jnp.dot(onehot, bucket_table, precision=highest)
    steps_tok = jax.nn.softplus(step_sum + step_bias[None, :] + offsets).astype(jnp.bfloat16)
    decay_neg = -decay_rate
    seq_count = lax.axis_size("seq")
    piece_width = channel_width // seq_count
    sub_width = min(piece_width, head_size)
    sub_count = piece_width // sub_width
    subs_per_head = head_size // sub_width
    steps_sub = jnp.repeat(steps_tok, subs_per_head, axis=1)
    wide_groups = jnp.broadcast_to(
        group_raw[:, None, :], (tok_rows, seq_count, group_width)
    ).reshape(tok_rows, seq_count * group_width)
    head_inputs, head_steps, head_groups = (
        lax.all_to_all(input_raw, "seq", split_axis=1, concat_axis=0, tiled=True),
        lax.all_to_all(steps_sub, "seq", split_axis=1, concat_axis=0, tiled=True),
        lax.all_to_all(wide_groups, "seq", split_axis=1, concat_axis=0, tiled=True),
    )
    seq_total = head_inputs.shape[0]
    first_channel = lax.axis_index("seq") * piece_width
    input_taps = lax.dynamic_slice_in_dim(
        conv_input.reshape(tap_count, -1), first_channel, piece_width, 1
    )
    input_shift = lax.dynamic_slice_in_dim(
        conv_input_bias.reshape(-1), first_channel, piece_width, 0
    )
    conv_values = causal_conv(
        head_inputs, jnp.zeros((tap_count - 1, piece_width), jnp.bfloat16), input_taps, input_shift
    )
    conv_groups = causal_conv(
        head_groups,
        jnp.zeros((tap_count - 1, group_width), jnp.bfloat16),
        conv_group.reshape(tap_count, -1),
        conv_group_bias.reshape(-1),
    )
    conv_groups = conv_groups.reshape(seq_total, groups_here, 2, state_size)
    sub_heads = (first_channel + jnp.arange(sub_count, dtype=jnp.int32) * sub_width) // head_size
    sub_groups = sub_heads // per_group
    sub_decay = jnp.take(decay_neg, sub_heads)[:, None]
    sub_skip = jnp.take(skip_gain, sub_heads)
    values_sub = jnp.moveaxis(conv_values.reshape(seq_total, sub_count, 1, sub_width), 1, 0)
    steps_heads = jnp.moveaxis(head_steps, 1, 0)[:, :, None]

    def run_sub(member):
        chosen = lax.dynamic_index_in_dim(conv_groups, member[3], 1, False)
        start_state = jnp.zeros((1, sub_width, state_size), jnp.float32)
        return ssd_group(start_state, member[0], chosen[:, 0], chosen[:, 1], member[1], member[2])[
            1
        ]

    scanned = jnp.moveaxis(
        lax.map(run_sub, (values_sub, steps_heads, sub_decay, sub_groups)), 0, 1
    ).reshape(seq_total, sub_count, sub_width)
    head_out = (
        scanned
        + sub_skip[None, :, None]
        * conv_values.reshape(seq_total, sub_count, sub_width).astype(jnp.float32)
    ).astype(jnp.bfloat16)
    ssd_out = lax.all_to_all(
        head_out.reshape(seq_total, piece_width), "seq", split_axis=0, concat_axis=1, tiled=True
    )
    gated_out = ssd_out.astype(jnp.float32) * jax.nn.silu(gate_act.astype(jnp.float32))
    grouped = gated_out.reshape(tok_rows, groups_here, -1)
    mean_square = jnp.mean(grouped * grouped, axis=2)
    scales = lax.rsqrt(mean_square + norm_epsilon)
    normed = (
        (grouped * scales[:, :, None]).reshape(tok_rows, -1) * norm_gain.reshape(-1)[None, :]
    ).astype(jnp.bfloat16)
    flat_out = out_weight.reshape(-1, out_weight.shape[2])
    layer_out = lax.psum_scatter(
        jnp.dot(normed, flat_out, preferred_element_type=jnp.float32).astype(jnp.bfloat16),
        "mp",
        scatter_dimension=0,
        tiled=True,
    )
    return layer_out


bf16 = jnp.bfloat16
f32 = jnp.float32
ROW_PAD = 16
LANES = 128


def matmul(left, right, dims=((1,), (0,))):
    return lax.dot_general(left, right, (dims, ((), ())), preferred_element_type=f32)


def softplus(value):
    return jnp.maximum(value, 0.0) + jnp.log1p(jnp.exp(-jnp.abs(value)))


def silu(value):
    return 0.5 * value * (1.0 + jnp.tanh(0.5 * value))


def parts_of(value, count):
    parts = []
    for _ in range(count):
        part = value.astype(bf16).astype(f32)
        parts.append(part)
        value = value - part
    return parts


HBM = pl.BlockSpec(memory_space=pl.ANY)
VMEM = pl.BlockSpec(memory_space=pltpu.VMEM)


def pack_kernel(tokens, groups, steps, ids, payload, mine, sem):
    rows, depth = mine.shape
    seat = lax.axis_index("mp")
    copy = pltpu.make_async_copy(
        tokens.at[pl.ds(pl.multiple_of(seat * rows, rows), rows)], mine, sem
    )
    copy.start()
    panels = depth // LANES
    low = panels * rows
    payload[low : low + groups.shape[0]] = groups[...]
    low += groups.shape[0]
    high = steps.shape[0]
    for part in range(steps.shape[1] // LANES):
        payload[low : low + high] = steps[:, part * LANES : (part + 1) * LANES]
        low += high
    marks = ids[...].astype(f32)
    rest = jnp.zeros((ROW_PAD - marks.shape[0], LANES), f32)
    payload[low:] = jnp.concatenate([marks, rest], axis=0).astype(bf16)
    copy.wait()
    for panel in range(panels):
        payload[panel * rows : (panel + 1) * rows] = mine[:, panel * LANES : (panel + 1) * LANES]


def payload_rows(tokens):
    return tokens.shape[0] // 4


def pack(tokens, groups, steps, ids):
    rows, depth = tokens.shape
    extra = steps.size // LANES + ROW_PAD
    full = payload_rows(tokens) * depth // LANES + groups.shape[0] + extra
    return pl.pallas_call(
        pack_kernel,
        in_specs=[HBM, VMEM, VMEM, VMEM],
        out_specs=VMEM,
        out_shape=jax.ShapeDtypeStruct((full, LANES), bf16),
        scratch_shapes=[
            pltpu.VMEM((payload_rows(tokens), depth), bf16),
            pltpu.SemaphoreType.DMA,
        ],
        name="pack",
    )(tokens, groups, steps, ids)


def layer_kernel(head_size, counts, tokens, *refs):
    columns, refs = refs[:2], refs[2:]
    ring, channels, slab = columns[0].shape
    payloads, refs = refs[:ring], refs[ring:]
    pieces, refs = refs[: 4 * len(counts)], refs[4 * len(counts) :]
    per_head_all, params_all, g_taps, g_shift, out = refs[:5]
    tok, shared, w_x, w_group, w_step, x_all, g_all, gate_all, step_all, state, sems = refs[5:]
    seats = 4
    rows = out.shape[1]
    quarter = rows // seats
    panels = tok.shape[1]
    height = panels * quarter
    part = 2 * g_shift.shape[1] // 2
    states = part // 2
    heads = channels // head_size
    lines = w_step.shape[1]
    tap_count = g_taps.shape[0]
    rim = x_all.shape[0] - ring * rows
    step_rows = shared.shape[1] - 2 * slab - ROW_PAD
    step_heads = step_rows * LANES // slab
    me = lax.axis_index("seq")
    seat = lax.axis_index("mp")
    beside = me & 1
    upper_half = me >> 2
    sources = [me, me ^ 1]
    for other in ((me >> 1) ^ 1, 2 - upper_half, 3 - 3 * upper_half):
        sources += [2 * other + beside, 2 * other + 1 - beside]

    arrivals = [2, 1, 4, 3, 6, 5, 7]
    shared_copies = []
    for order in range(ring):
        copy = pltpu.make_async_copy(
            payloads[order].at[pl.ds(height, shared.shape[1])],
            shared.at[sources[order]],
            sems.at[1 + ring + order],
        )
        copy.start()
        shared_copies.append(copy)
    for kind in range(2):
        pltpu.make_async_copy(
            columns[kind], w_x.at[:, pl.ds(kind * channels, channels)], sems.at[0]
        ).start()
    for panel in range(panels):
        pltpu.make_async_copy(
            tokens.at[:, pl.ds(panel * LANES, LANES)], tok.at[me, panel], sems.at[1 + me]
        ).start()
    order = 0
    for group, count in enumerate(counts):
        for at in range(count):
            source = sources[arrivals[order]]
            for hop in range(seats):
                first = pl.multiple_of((seat ^ hop) * quarter, quarter)
                pltpu.make_async_copy(
                    pieces[4 * group + hop].at[at],
                    tok.at[source, :, pl.ds(first, quarter)],
                    sems.at[1 + source],
                ).start()
            order += 1

    x_all[:rim] = jnp.zeros((rim, channels), f32)
    g_all[:rim] = jnp.zeros((rim, part), f32)
    state[...] = jnp.zeros_like(state)
    one = lambda flag: flag.astype(f32).astype(bf16)
    iota = lambda shape, dim: lax.broadcasted_iota(jnp.int32, shape, dim)
    pick = one(
        (iota((lines, step_heads), 0) + me * heads == iota((lines, step_heads), 1))
        & (iota((lines, step_heads), 0) < heads)
    )
    unpick = [
        one(2 * iota((slab, 2 * slab), 0) + kind == iota((slab, 2 * slab), 1)) for kind in range(2)
    ]
    for copy in shared_copies:
        copy.wait()
    for panel in range(ring):
        slab_rows = shared[panel, : 2 * slab]
        for kind in range(2):
            w_group[panel, :, kind * states : (kind + 1) * states] = matmul(
                unpick[kind], slab_rows
            ).astype(bf16)
        step_panel = jnp.concatenate(
            [
                shared[panel, 2 * slab + low : 2 * slab + low + step_heads]
                for low in range(0, step_rows, step_heads)
            ],
            axis=1,
        )
        w_step[panel] = matmul(pick, step_panel).astype(bf16)
    pltpu.make_async_copy(w_x, w_x, sems.at[0]).wait()

    upper = one(iota((rows, rows), 0) <= iota((rows, rows), 1))
    widen = one(iota((lines, channels), 1) // head_size == iota((lines, channels), 0))
    half = rows // 2
    causal = iota((half, half), 0) >= iota((half, half), 1)
    lane_head = iota((rows, channels), 1) // head_size
    per_head = per_head_all[me]
    params = params_all[me]
    bias, decay = per_head[:, 0:1], per_head[:, 1:2]
    skip = params[tap_count + 1 : tap_count + 2]

    def tok_wait(block):
        pltpu.make_async_copy(tok.at[block], tok.at[block], sems.at[1 + block]).wait()

    def project(block):
        total_x = total_g = total_s = None
        each = panels // ring
        for panel in range(ring):
            piece = jnp.concatenate(
                [tok[block, panel * each + low] for low in range(each)], axis=1
            )
            term_x = matmul(piece, w_x[panel], ((1,), (1,)))
            term_g = matmul(piece, w_group[panel])
            term_s = matmul(w_step[panel], piece, ((1,), (1,)))
            total_x = term_x if total_x is None else total_x + term_x
            total_g = term_g if total_g is None else total_g + term_g
            total_s = term_s if total_s is None else total_s + term_s
        base = pl.multiple_of(block * rows, rows)
        x_all[pl.ds(base + rim, rows)] = total_x[:, :channels].astype(bf16).astype(f32)
        gate_all[block] = total_x[:, channels:].astype(bf16).astype(f32)
        g_all[pl.ds(base + rim, rows)] = total_g.astype(bf16).astype(f32)
        step_all[block] = total_s

    def conv(ref, base, taps, shift):
        window = ref[pl.ds(base, rows + rim)]
        first = rim - tap_count + 1
        running = shift
        for tap in range(tap_count):
            running = running + taps[tap : tap + 1] * window[first + tap : first + tap + rows]
        return silu(running).astype(bf16)

    def stretch(value, count):
        low = jnp.concatenate(parts_of(value, count), axis=0).astype(bf16)
        return matmul(low, jnp.concatenate([widen] * count, axis=0), ((0,), (0,)))

    def scan(block):
        base = pl.multiple_of(block * rows, rows)
        values = conv(x_all, base, params[:tap_count], params[tap_count : tap_count + 1])
        values = values.astype(f32)
        groups = conv(g_all, base, g_taps[...], g_shift[...])
        b_rows, c_rows = groups[:, :states], groups[:, states:]
        marks = shared[block, 2 * slab + step_rows :].astype(f32)
        bucket = jnp.concatenate(
            [marks[low : low + 1] for low in range(rows // LANES)], axis=1
        )
        raw_step = step_all[block] + bias
        for entry in range(PLACE_BINS):
            raw_step = raw_step + jnp.where(
                bucket == float(entry), per_head[:, 2 + entry : 3 + entry], 0.0
            )
        sizes = softplus(raw_step).astype(bf16).astype(f32)
        rates = jnp.concatenate(parts_of(-decay * sizes, 3), axis=0).astype(bf16)
        sums = matmul(rates, upper)
        cumulative = sums[:lines] + (sums[lines : 2 * lines] + sums[2 * lines :])
        last = cumulative[:, rows - 1 : rows]
        grown = stretch(jnp.exp(cumulative), 3)
        left = stretch(sizes * jnp.exp(last - cumulative), 3)
        driven = (stretch(sizes, 1) * values).astype(f32)
        scores = matmul(c_rows, b_rows, ((1,), (1,)))
        cum_parts = parts_of(cumulative, 3)
        ones = jnp.ones((3, rows), f32)
        pad = jnp.zeros((2, rows), f32)
        top, low_left, low_right, inputs = [], [], [], []
        for head in range(heads):
            mine = jnp.concatenate([p[head : head + 1] for p in cum_parts], axis=0)
            spread = matmul(
                jnp.concatenate([mine, ones, pad], axis=0).astype(bf16),
                jnp.concatenate([ones, -mine, pad], axis=0).astype(bf16),
                ((0,), (0,)),
            )
            decays = lambda part: jnp.exp(jnp.where(causal, part, -1e30))
            top.append((scores[:half, :half] * decays(spread[:half, :half])).astype(bf16))
            low_left.append((scores[half:, :half] * jnp.exp(spread[half:, :half])).astype(bf16))
            low_right.append((scores[half:, half:] * decays(spread[half:, half:])).astype(bf16))
            inputs.append(jnp.where(lane_head == head, driven, 0.0).astype(bf16))
        upper_in = jnp.concatenate([d[:half] for d in inputs], axis=0)
        lower_in = jnp.concatenate([d[half:] for d in inputs], axis=0)
        upper_out = matmul(jnp.concatenate(top, axis=1), upper_in)
        lower_out = matmul(
            jnp.concatenate(low_left + low_right, axis=1),
            jnp.concatenate([upper_in, lower_in], axis=0),
        )
        within = jnp.concatenate([upper_out, lower_out], axis=0)
        held = state[...]
        scanned = within + grown * matmul(c_rows, held.astype(bf16)) + skip * values
        scanned = scanned.astype(bf16).astype(f32)
        out[me ^ block] = (scanned * silu(gate_all[block])).astype(bf16)
        injected = matmul(b_rows, (left * values).astype(bf16), ((0,), (0,)))
        state[...] = grown[rows - 1 : rows] * held + injected

    def project_step(step, carry):
        for low in range(1):
            tok_wait(1 * step + low)
            project(1 * step + low)
        return carry

    lax.fori_loop(0, ring // 1, project_step, 0)

    def advance(step, carry):
        for low in range(8):
            scan(8 * step + low)
        return carry

    lax.fori_loop(0, ring // 8, advance, 0)


def layer(head_size, tokens, columns, payloads, groups, per_head, params, g_taps, g_shift):
    ring, channels, slab = columns[0].shape
    wide = 2 * channels
    rows, depth = tokens.shape
    part = g_shift.shape[1]
    lines = per_head.shape[1]
    rim = 8
    total = ring * rows
    counts = [group[0].shape[0] for group in groups]
    pieces = [piece for group in groups for piece in group]
    shared_rows = payloads[0].shape[0] - payload_rows(tokens) * depth // LANES
    return pl.pallas_call(
        functools.partial(layer_kernel, head_size, counts),
        in_specs=[HBM] * (3 + len(payloads) + len(pieces)) + [VMEM] * 4,
        out_specs=VMEM,
        out_shape=jax.ShapeDtypeStruct((ring, rows, channels), bf16),
        scratch_shapes=[
            pltpu.VMEM((ring, depth // LANES, rows, LANES), bf16),
            pltpu.VMEM((ring, shared_rows, LANES), bf16),
            pltpu.VMEM((ring, wide, slab), bf16),
            pltpu.VMEM((ring, slab, part), bf16),
            pltpu.VMEM((ring, lines, slab), bf16),
            pltpu.VMEM((rim + total, channels), f32),
            pltpu.VMEM((rim + total, part), f32),
            pltpu.VMEM((ring, rows, channels), f32),
            pltpu.VMEM((ring, lines, rows), f32),
            pltpu.VMEM((part // 2, channels), f32),
            pltpu.SemaphoreType.DMA((1 + 2 * ring,)),
        ],
        compiler_params=pltpu.CompilerParams(vmem_limit_bytes=60 * 1024 * 1024),
        cost_estimate=pl.CostEstimate(
            flops=2 * total * ring * slab * (wide + part),
            bytes_accessed=2 * total * ring * slab,
            transcendentals=0,
        ),
        name="layer",
    )(tokens, *columns, *payloads, *pieces, per_head, params, g_taps, g_shift)


def hold_kernel(gated, weight, held, sem):
    del gated
    copy = pltpu.make_async_copy(weight, held, sem)
    copy.start()
    copy.wait()


def hold(gated, weight):
    return pl.pallas_call(
        hold_kernel,
        in_specs=[HBM, HBM],
        out_specs=VMEM,
        out_shape=pltpu.VMEM(weight.shape, weight.dtype),
        scratch_shapes=[pltpu.SemaphoreType.DMA],
        compiler_params=pltpu.CompilerParams(vmem_limit_bytes=48 * 1024 * 1024),
        cost_estimate=pl.CostEstimate(
            flops=0, bytes_accessed=4 * weight.size, transcendentals=0
        ),
        name="hold",
    )(gated, weight)


def close_kernel(offsets, gain, weight, *refs):
    parts, (keep, give, inputs) = refs[:-3], refs[-3:]
    rows, width = parts[0].shape
    seats = 4
    quarter = rows // seats
    columns = weight.shape[1] // 4
    me = lax.axis_index("seq")
    seat = lax.axis_index("mp")
    square = jnp.zeros((rows, width), f32)
    for offset, part in zip(offsets, parts):
        value = part[...].astype(f32)
        square = square + value * value
        at = pl.multiple_of((me ^ offset) * width, width)
        inputs[:, pl.ds(at, width)] = (value * gain[:, pl.ds(at, width)]).astype(bf16)
    mean = jnp.sum(square, axis=1, keepdims=True) * (1.0 / (len(parts) * width))
    scale = lax.rsqrt(mean + norm_epsilon)
    for step in range(4):
        at = pl.ds(step * columns, columns)
        total = (matmul(inputs[...], weight[:, at]) * scale).astype(bf16)
        for core in range(2):

            @pl.when((seat & 1) == core)
            def _(core=core):
                for owner in range(seats):
                    block = total[owner * quarter : (owner + 1) * quarter]
                    target = keep if owner % 2 == core else give
                    target[(owner // 2) ^ (seat >> 1), :, at] = block


def close(offsets, gain, weight, parts):
    rows, width = parts[0].shape
    shape = jax.ShapeDtypeStruct((2, rows // 4, weight.shape[1]), bf16)
    return pl.pallas_call(
        functools.partial(close_kernel, offsets),
        in_specs=[VMEM] * (2 + len(parts)),
        out_specs=[VMEM] * 2,
        out_shape=[shape, shape],
        scratch_shapes=[pltpu.VMEM((rows, len(parts) * width), bf16)],
        compiler_params=pltpu.CompilerParams(vmem_limit_bytes=16 * 1024 * 1024),
        cost_estimate=pl.CostEstimate(
            flops=2 * rows * weight.size, bytes_accessed=2 * weight.size, transcendentals=0
        ),
        name="close",
    )(gain, pltpu.with_memory_space_constraint(weight, pltpu.VMEM), *parts)


def tokens_travel(
    tokens,
    gate_weight,
    input_weight,
    group_weight,
    step_weight,
    step_bias,
    bucket_table,
    bucket_ids,
    decay_rate,
    conv_input,
    conv_input_bias,
    conv_group,
    conv_group_bias,
    skip_gain,
    norm_gain,
    out_weight,
):
    rows, depth = tokens.shape
    slab = gate_weight.shape[0]
    heads_here = step_bias.shape[0]
    head_size = gate_weight.shape[2]
    state_size = group_weight.shape[3]
    tap_count = conv_input.shape[0]
    ring = lax.axis_size("seq")
    seats = lax.axis_size("mp")
    me = lax.axis_index("seq")
    channels = heads_here * head_size // ring
    heads = channels // head_size
    swap = lambda size, bit: [(i, i ^ bit) for i in range(size)]
    column = lambda pairs: [(2 * a + w, 2 * b + w) for a, b in pairs for w in range(2)]

    payload = pack(
        tokens,
        group_weight.reshape(2 * slab, state_size),
        jnp.transpose(step_weight),
        bucket_ids.reshape(rows // LANES, LANES),
    )
    inner = (me >= 2) & (me < 6)
    outward = column([(1, 0), (2, 3)])
    middle = column([(1, 2), (2, 1)])
    near = lax.ppermute(payload, "seq", swap(ring, 2))
    mid = lax.ppermute(payload, "seq", middle)
    across_own = lax.ppermute(payload, "seq", swap(ring, 1))

    by_channel = lambda w: jnp.transpose(w, (1, 2, 0)).reshape(ring, channels, slab)
    trade = lambda w: lax.all_to_all(w, "seq", split_axis=0, concat_axis=0, tiled=True)
    cross = lambda item: lax.ppermute(item, "seq", swap(ring, 1))
    x_weight, gate = by_channel(input_weight), by_channel(gate_weight)
    per_head = jnp.concatenate([jnp.stack([step_bias, decay_rate]), bucket_table], axis=0)
    per_head = jnp.transpose(per_head).reshape(ring, heads, -1)
    per_head = jnp.pad(per_head, ((0, 0), (0, 8 - heads), (0, 0)))
    params = jnp.concatenate(
        [
            conv_input,
            conv_input_bias[None],
            jnp.broadcast_to(skip_gain[None, :, None], (1, heads_here, head_size)),
        ],
        axis=0,
    )
    params = jnp.moveaxis(params.reshape(params.shape[0], ring, channels), 1, 0)
    g_taps = conv_group.reshape(tap_count, 2 * state_size)
    g_shift = conv_group_bias.reshape(1, 2 * state_size)
    after = lambda value, *others: lax.optimization_barrier((value,) + others)[0]
    quarter = payload_rows(tokens)
    panels = depth // LANES

    def spread(*items):
        own = jnp.stack(
            [item[: panels * quarter].reshape(panels, quarter, LANES) for item in items]
        )
        beside = lax.ppermute(own, "mp", swap(seats, 1))
        across = lax.ppermute(own, "mp", swap(seats, 2))
        return own, beside, across, lax.ppermute(across, "mp", swap(seats, 1))

    near, mid, across_own, x_weight, per_head, params, g_taps, g_shift = lax.optimization_barrier(
        (near, mid, across_own, x_weight, per_head, params, g_taps, g_shift)
    )
    mid_far = lax.ppermute(near, "seq", middle)
    out_near = lax.ppermute(mid, "seq", outward)
    across_near = cross(near)
    x_weight = trade(x_weight)
    groups = [spread(near, across_own)]

    out_far = lax.ppermute(mid_far, "seq", outward)
    second = jnp.where(inner, mid, out_near)
    groups.append(spread(second, across_near))
    gate = trade(after(gate, mid_far, x_weight))
    third = jnp.where(inner, mid_far, out_far)
    across_second = cross(after(second, across_near))
    third = after(third, groups[0][1], groups[0][3], groups[1][2], across_second)
    across_third = cross(third)
    groups.append(spread(third, across_second))
    across_third = after(across_third, groups[1][1], groups[1][3], groups[2][2])
    groups.append(spread(across_third))
    columns = [x_weight, gate]
    payloads = [payload, across_own, near, across_near, second, across_second, third, across_third]

    gated = layer(head_size, tokens, columns, payloads, groups, per_head, params, g_taps, g_shift)
    offsets = (6, 7, 5, 4, 3, 2, 1)
    parts = [lax.ppermute(gated[at], "seq", swap(ring, at)) for at in offsets] + [gated[0]]
    gain, weight = norm_gain.reshape(1, -1), out_weight.reshape(-1, depth)
    keep, give = close(offsets + (0,), gain, hold(gated[0, :ROW_PAD], weight), parts)
    took = lax.ppermute(give, "mp", swap(seats, 1))
    send = (keep[1].astype(f32) + took[1].astype(f32)).astype(bf16)
    took_far = lax.ppermute(send, "mp", swap(seats, 2))
    return (keep[0].astype(f32) + took[0].astype(f32) + took_far.astype(f32)).astype(bf16)


def on_device(*arrays):
    tokens, gate_weight, group_weight = arrays[0], arrays[1], arrays[3]
    ring = lax.axis_size("seq")
    channels = gate_weight.shape[1] * gate_weight.shape[2] // ring
    weights = 2 * gate_weight.size + group_weight.size + arrays[4].size
    fits = (
        tokens.size <= weights
        and channels % 128 == 0
        and gate_weight.shape[0] == 2 * group_weight.shape[3] == tokens.shape[0]
        and channels % gate_weight.shape[2] == 0
        and group_weight.shape[1] == 1
        and lax.axis_size("mp") == 4
        and ring == 8
    )
    return (tokens_travel if fits else weights_travel)(*arrays)


def solution(mesh):
    placed = (
        P("seq", None),
        P("seq", "mp", None),
        P("seq", "mp", None),
        P("seq", "mp", None, None),
        P("seq", "mp"),
        P("mp"),
        P(None, "mp"),
        P("seq"),
        P("mp"),
        P(None, "mp", None),
        P("mp", None),
        P(None, "mp", None, None),
        P("mp", None, None),
        P("mp"),
        P("mp", None),
        P("mp", None, None),
    )
    return jax.shard_map(
        on_device, mesh=mesh, in_specs=placed, out_specs=P(("seq", "mp"), None), check_vma=False
    )
```

```python
import functools

import jax
import jax.numpy as jnp
from jax import lax
from jax.experimental import pallas as pl
from jax.experimental.pallas import tpu as pltpu
from jax.sharding import PartitionSpec as P

SPAN = 256
PLACE_BINS = 4


norm_epsilon = 1e-05
highest = lax.Precision.HIGHEST


def causal_conv(raw_rows, rim_rows, tap_weights, tap_bias):
    extended = jnp.concatenate([rim_rows, raw_rows], axis=0).astype(jnp.float32)
    row_count = raw_rows.shape[0]
    tap_count = tap_weights.shape[0]
    running = (
        tap_bias[None, :]
        + tap_weights[tap_count - 1][None, :] * extended[tap_count - 1 : tap_count - 1 + row_count]
    )
    for tap_index in range(tap_count - 1):
        running = (
            running + tap_weights[tap_index][None, :] * extended[tap_index : tap_index + row_count]
        )
    return jax.nn.silu(running).astype(jnp.bfloat16)


def ssd_block(carried_state, block_inputs, decay_neg):
    block_values, block_b, block_c, block_steps = block_inputs
    step_rates = block_steps.astype(jnp.float32) * decay_neg[None, :]
    cumulative = jnp.cumsum(step_rates, axis=0)
    scores = jnp.einsum("tn,sn->ts", block_c, block_b, preferred_element_type=jnp.float32)
    by_head = jnp.transpose(cumulative)
    spread = by_head[:, :, None] - by_head[:, None, :]
    block_rows = block_values.shape[0]
    causal = (jnp.arange(block_rows)[:, None] >= jnp.arange(block_rows)[None, :])[None]
    decays = jnp.where(causal, jnp.exp(jnp.where(causal, spread, 0.0)), 0.0)
    mixing = scores[None] * decays
    driven = block_steps.astype(jnp.float32)[:, :, None] * block_values.astype(jnp.float32)
    within = jnp.einsum("rts,srp->trp", mixing, driven, precision=highest)
    readout = jnp.einsum(
        "tn,rpn->trp", block_c.astype(jnp.float32), carried_state, precision=highest
    )
    outputs = within + jnp.exp(cumulative)[:, :, None] * readout
    remaining = jnp.exp(cumulative[-1][None, :] - cumulative)
    injected = jnp.einsum(
        "srp,sn->rpn",
        driven * remaining[:, :, None],
        block_b.astype(jnp.float32),
        precision=highest,
    )
    next_state = jnp.exp(cumulative[-1])[:, None, None] * carried_state + injected
    return (next_state, outputs)


def ssd_group(start_state, group_values, group_b, group_c, group_steps, decay_neg):
    row_total = group_values.shape[0]
    block_count = row_total // SPAN

    def advance(carried_state, block_inputs):
        return ssd_block(carried_state, block_inputs, decay_neg)

    blocked = (
        group_values.reshape((block_count, SPAN) + group_values.shape[1:]),
        group_b.reshape(block_count, SPAN, -1),
        group_c.reshape(block_count, SPAN, -1),
        group_steps.reshape(block_count, SPAN, -1),
    )
    final_state, outputs = lax.scan(advance, start_state, blocked)
    return (final_state, outputs.reshape((row_total,) + outputs.shape[2:]))


def weights_travel(
    tokens,
    gate_weight,
    input_weight,
    group_weight,
    step_weight,
    step_bias,
    bucket_table,
    bucket_ids,
    decay_rate,
    conv_input,
    conv_input_bias,
    conv_group,
    conv_group_bias,
    skip_gain,
    norm_gain,
    out_weight,
):
    tok_rows = tokens.shape[0]
    heads_here = step_bias.shape[0]
    groups_here = group_weight.shape[1]
    per_group = heads_here // groups_here
    head_size = gate_weight.shape[2]
    state_size = group_weight.shape[3]
    tap_count = conv_input.shape[0]
    channel_width = heads_here * head_size
    group_width = groups_here * 2 * state_size
    pieces = (
        lax.all_gather(gate_weight, "seq", axis=0, tiled=True),
        lax.all_gather(input_weight, "seq", axis=0, tiled=True),
        lax.all_gather(group_weight, "seq", axis=0, tiled=True),
        lax.all_gather(step_weight, "seq", axis=0, tiled=True),
    )
    rows_here = pieces[0].shape[0]
    gate_sum, input_sum, group_sum, step_sum = tuple(
        (
            jnp.dot(tokens, piece.reshape(rows_here, -1), preferred_element_type=jnp.float32)
            for piece in pieces
        )
    )
    gate_act = gate_sum.astype(jnp.bfloat16)
    input_raw = input_sum.astype(jnp.bfloat16)
    group_raw = group_sum.astype(jnp.bfloat16)
    onehot = (bucket_ids[:, None] == jnp.arange(PLACE_BINS, dtype=jnp.int32)[None, :]).astype(
        jnp.float32
    )
    offsets = jnp.dot(onehot, bucket_table, precision=highest)
    steps_tok = jax.nn.softplus(step_sum + step_bias[None, :] + offsets).astype(jnp.bfloat16)
    decay_neg = -decay_rate
    seq_count = lax.axis_size("seq")
    piece_width = channel_width // seq_count
    sub_width = min(piece_width, head_size)
    sub_count = piece_width // sub_width
    subs_per_head = head_size // sub_width
    steps_sub = jnp.repeat(steps_tok, subs_per_head, axis=1)
    wide_groups = jnp.broadcast_to(
        group_raw[:, None, :], (tok_rows, seq_count, group_width)
    ).reshape(tok_rows, seq_count * group_width)
    head_inputs, head_steps, head_groups = (
        lax.all_to_all(input_raw, "seq", split_axis=1, concat_axis=0, tiled=True),
        lax.all_to_all(steps_sub, "seq", split_axis=1, concat_axis=0, tiled=True),
        lax.all_to_all(wide_groups, "seq", split_axis=1, concat_axis=0, tiled=True),
    )
    seq_total = head_inputs.shape[0]
    first_channel = lax.axis_index("seq") * piece_width
    input_taps = lax.dynamic_slice_in_dim(
        conv_input.reshape(tap_count, -1), first_channel, piece_width, 1
    )
    input_shift = lax.dynamic_slice_in_dim(
        conv_input_bias.reshape(-1), first_channel, piece_width, 0
    )
    conv_values = causal_conv(
        head_inputs, jnp.zeros((tap_count - 1, piece_width), jnp.bfloat16), input_taps, input_shift
    )
    conv_groups = causal_conv(
        head_groups,
        jnp.zeros((tap_count - 1, group_width), jnp.bfloat16),
        conv_group.reshape(tap_count, -1),
        conv_group_bias.reshape(-1),
    )
    conv_groups = conv_groups.reshape(seq_total, groups_here, 2, state_size)
    sub_heads = (first_channel + jnp.arange(sub_count, dtype=jnp.int32) * sub_width) // head_size
    sub_groups = sub_heads // per_group
    sub_decay = jnp.take(decay_neg, sub_heads)[:, None]
    sub_skip = jnp.take(skip_gain, sub_heads)
    values_sub = jnp.moveaxis(conv_values.reshape(seq_total, sub_count, 1, sub_width), 1, 0)
    steps_heads = jnp.moveaxis(head_steps, 1, 0)[:, :, None]

    def run_sub(member):
        chosen = lax.dynamic_index_in_dim(conv_groups, member[3], 1, False)
        start_state = jnp.zeros((1, sub_width, state_size), jnp.float32)
        return ssd_group(start_state, member[0], chosen[:, 0], chosen[:, 1], member[1], member[2])[
            1
        ]

    scanned = jnp.moveaxis(
        lax.map(run_sub, (values_sub, steps_heads, sub_decay, sub_groups)), 0, 1
    ).reshape(seq_total, sub_count, sub_width)
    head_out = (
        scanned
        + sub_skip[None, :, None]
        * conv_values.reshape(seq_total, sub_count, sub_width).astype(jnp.float32)
    ).astype(jnp.bfloat16)
    ssd_out = lax.all_to_all(
        head_out.reshape(seq_total, piece_width), "seq", split_axis=0, concat_axis=1, tiled=True
    )
    gated_out = ssd_out.astype(jnp.float32) * jax.nn.silu(gate_act.astype(jnp.float32))
    grouped = gated_out.reshape(tok_rows, groups_here, -1)
    mean_square = jnp.mean(grouped * grouped, axis=2)
    scales = lax.rsqrt(mean_square + norm_epsilon)
    normed = (
        (grouped * scales[:, :, None]).reshape(tok_rows, -1) * norm_gain.reshape(-1)[None, :]
    ).astype(jnp.bfloat16)
    flat_out = out_weight.reshape(-1, out_weight.shape[2])
    layer_out = lax.psum_scatter(
        jnp.dot(normed, flat_out, preferred_element_type=jnp.float32).astype(jnp.bfloat16),
        "mp",
        scatter_dimension=0,
        tiled=True,
    )
    return layer_out


bf16 = jnp.bfloat16
f32 = jnp.float32
ROW_PAD = 16
LANES = 128


def matmul(left, right, dims=((1,), (0,))):
    return lax.dot_general(left, right, (dims, ((), ())), preferred_element_type=f32)


def softplus(value):
    return jnp.maximum(value, 0.0) + jnp.log1p(jnp.exp(-jnp.abs(value)))


def silu(value):
    return 0.5 * value * (1.0 + jnp.tanh(0.5 * value))


def parts_of(value, count):
    parts = []
    for _ in range(count):
        part = value.astype(bf16).astype(f32)
        parts.append(part)
        value = value - part
    return parts


HBM = pl.BlockSpec(memory_space=pl.ANY)
VMEM = pl.BlockSpec(memory_space=pltpu.VMEM)


def pack_kernel(tokens, groups, steps, ids, payload, mine, sem):
    rows, depth = mine.shape
    seat = lax.axis_index("mp")
    copy = pltpu.make_async_copy(
        tokens.at[pl.ds(pl.multiple_of(seat * rows, rows), rows)], mine, sem
    )
    copy.start()
    panels = depth // LANES
    low = panels * rows
    payload[low : low + groups.shape[0]] = groups[...]
    low += groups.shape[0]
    high = steps.shape[0]
    for part in range(steps.shape[1] // LANES):
        payload[low : low + high] = steps[:, part * LANES : (part + 1) * LANES]
        low += high
    marks = ids[...].astype(f32)
    rest = jnp.zeros((ROW_PAD - marks.shape[0], LANES), f32)
    payload[low:] = jnp.concatenate([marks, rest], axis=0).astype(bf16)
    copy.wait()
    for panel in range(panels):
        payload[panel * rows : (panel + 1) * rows] = mine[:, panel * LANES : (panel + 1) * LANES]


def payload_rows(tokens):
    return tokens.shape[0] // 4


def pack(tokens, groups, steps, ids):
    rows, depth = tokens.shape
    extra = steps.size // LANES + ROW_PAD
    full = payload_rows(tokens) * depth // LANES + groups.shape[0] + extra
    return pl.pallas_call(
        pack_kernel,
        in_specs=[HBM, VMEM, VMEM, VMEM],
        out_specs=VMEM,
        out_shape=jax.ShapeDtypeStruct((full, LANES), bf16),
        scratch_shapes=[
            pltpu.VMEM((payload_rows(tokens), depth), bf16),
            pltpu.SemaphoreType.DMA,
        ],
        name="pack",
    )(tokens, groups, steps, ids)


def layer_kernel(head_size, counts, tokens, *refs):
    columns, refs = refs[:2], refs[2:]
    ring, channels, slab = columns[0].shape
    payloads, refs = refs[:ring], refs[ring:]
    pieces, refs = refs[: 4 * len(counts)], refs[4 * len(counts) :]
    per_head_all, params_all, g_taps, g_shift = refs[:4]
    parts, refs = refs[4 : 4 + ring], refs[4 + ring :]
    tok, shared, w_x, w_group, w_step, x_all, g_all, gate_all, step_all, state, out, sems = refs
    seats = 4
    rows = parts[0].shape[0]
    quarter = rows // seats
    panels = tok.shape[1]
    height = panels * quarter
    part = 2 * g_shift.shape[1] // 2
    states = part // 2
    heads = channels // head_size
    lines = w_step.shape[1]
    tap_count = g_taps.shape[0]
    rim = x_all.shape[0] - ring * rows
    step_rows = shared.shape[1] - 2 * slab - ROW_PAD
    step_heads = step_rows * LANES // slab
    me = lax.axis_index("seq")
    seat = lax.axis_index("mp")
    beside = me & 1
    upper_half = me >> 2
    sources = [me, me ^ 1]
    for other in ((me >> 1) ^ 1, 2 - upper_half, 3 - 3 * upper_half):
        sources += [2 * other + beside, 2 * other + 1 - beside]

    arrivals = [2, 1, 4, 3, 6, 5, 7]
    shared_copies = []
    for order in range(ring):
        copy = pltpu.make_async_copy(
            payloads[order].at[pl.ds(height, shared.shape[1])],
            shared.at[sources[order]],
            sems.at[1 + ring + order],
        )
        copy.start()
        shared_copies.append(copy)
    for kind in range(2):
        pltpu.make_async_copy(
            columns[kind], w_x.at[:, pl.ds(kind * channels, channels)], sems.at[0]
        ).start()
    for panel in range(panels):
        pltpu.make_async_copy(
            tokens.at[:, pl.ds(panel * LANES, LANES)], tok.at[me, panel], sems.at[1 + me]
        ).start()
    order = 0
    for group, count in enumerate(counts):
        for at in range(count):
            source = sources[arrivals[order]]
            for hop in range(seats):
                first = pl.multiple_of((seat ^ hop) * quarter, quarter)
                pltpu.make_async_copy(
                    pieces[4 * group + hop].at[at],
                    tok.at[source, :, pl.ds(first, quarter)],
                    sems.at[1 + source],
                ).start()
            order += 1

    x_all[:rim] = jnp.zeros((rim, channels), f32)
    g_all[:rim] = jnp.zeros((rim, part), f32)
    state[...] = jnp.zeros_like(state)
    one = lambda flag: flag.astype(f32).astype(bf16)
    iota = lambda shape, dim: lax.broadcasted_iota(jnp.int32, shape, dim)
    pick = one(
        (iota((lines, step_heads), 0) + me * heads == iota((lines, step_heads), 1))
        & (iota((lines, step_heads), 0) < heads)
    )
    unpick = [
        one(2 * iota((slab, 2 * slab), 0) + kind == iota((slab, 2 * slab), 1)) for kind in range(2)
    ]
    for copy in shared_copies:
        copy.wait()
    for panel in range(ring):
        slab_rows = shared[panel, : 2 * slab]
        for kind in range(2):
            w_group[panel, :, kind * states : (kind + 1) * states] = matmul(
                unpick[kind], slab_rows
            ).astype(bf16)
        step_panel = jnp.concatenate(
            [
                shared[panel, 2 * slab + low : 2 * slab + low + step_heads]
                for low in range(0, step_rows, step_heads)
            ],
            axis=1,
        )
        w_step[panel] = matmul(pick, step_panel).astype(bf16)
    pltpu.make_async_copy(w_x, w_x, sems.at[0]).wait()

    upper = one(iota((rows, rows), 0) <= iota((rows, rows), 1))
    widen = one(iota((lines, channels), 1) // head_size == iota((lines, channels), 0))
    half = rows // 2
    causal = iota((half, half), 0) >= iota((half, half), 1)
    lane_head = iota((rows, channels), 1) // head_size
    per_head = per_head_all[me]
    params = params_all[me]
    bias, decay = per_head[:, 0:1], per_head[:, 1:2]
    skip = params[tap_count + 1 : tap_count + 2]

    def tok_wait(block):
        pltpu.make_async_copy(tok.at[block], tok.at[block], sems.at[1 + block]).wait()

    def project(block):
        total_x = total_g = total_s = None
        each = panels // ring
        for panel in range(ring):
            piece = jnp.concatenate(
                [tok[block, panel * each + low] for low in range(each)], axis=1
            )
            term_x = matmul(piece, w_x[panel], ((1,), (1,)))
            term_g = matmul(piece, w_group[panel])
            term_s = matmul(w_step[panel], piece, ((1,), (1,)))
            total_x = term_x if total_x is None else total_x + term_x
            total_g = term_g if total_g is None else total_g + term_g
            total_s = term_s if total_s is None else total_s + term_s
        base = pl.multiple_of(block * rows, rows)
        x_all[pl.ds(base + rim, rows)] = total_x[:, :channels].astype(bf16).astype(f32)
        gate_all[block] = total_x[:, channels:].astype(bf16).astype(f32)
        g_all[pl.ds(base + rim, rows)] = total_g.astype(bf16).astype(f32)
        step_all[block] = total_s

    def conv(ref, base, taps, shift):
        window = ref[pl.ds(base, rows + rim)]
        first = rim - tap_count + 1
        running = shift
        for tap in range(tap_count):
            running = running + taps[tap : tap + 1] * window[first + tap : first + tap + rows]
        return silu(running).astype(bf16)

    def stretch(value, count):
        low = jnp.concatenate(parts_of(value, count), axis=0).astype(bf16)
        return matmul(low, jnp.concatenate([widen] * count, axis=0), ((0,), (0,)))

    def scan(block):
        base = pl.multiple_of(block * rows, rows)
        values = conv(x_all, base, params[:tap_count], params[tap_count : tap_count + 1])
        values = values.astype(f32)
        groups = conv(g_all, base, g_taps[...], g_shift[...])
        b_rows, c_rows = groups[:, :states], groups[:, states:]
        marks = shared[block, 2 * slab + step_rows :].astype(f32)
        bucket = jnp.concatenate(
            [marks[low : low + 1] for low in range(rows // LANES)], axis=1
        )
        raw_step = step_all[block] + bias
        for entry in range(PLACE_BINS):
            raw_step = raw_step + jnp.where(
                bucket == float(entry), per_head[:, 2 + entry : 3 + entry], 0.0
            )
        sizes = softplus(raw_step).astype(bf16).astype(f32)
        rates = jnp.concatenate(parts_of(-decay * sizes, 3), axis=0).astype(bf16)
        sums = matmul(rates, upper)
        cumulative = sums[:lines] + (sums[lines : 2 * lines] + sums[2 * lines :])
        last = cumulative[:, rows - 1 : rows]
        grown = stretch(jnp.exp(cumulative), 3)
        left = stretch(sizes * jnp.exp(last - cumulative), 3)
        driven = (stretch(sizes, 1) * values).astype(f32)
        scores = matmul(c_rows, b_rows, ((1,), (1,)))
        cum_parts = parts_of(cumulative, 3)
        ones = jnp.ones((3, rows), f32)
        pad = jnp.zeros((2, rows), f32)
        top, low_left, low_right, inputs = [], [], [], []
        for head in range(heads):
            mine = jnp.concatenate([p[head : head + 1] for p in cum_parts], axis=0)
            spread = matmul(
                jnp.concatenate([mine, ones, pad], axis=0).astype(bf16),
                jnp.concatenate([ones, -mine, pad], axis=0).astype(bf16),
                ((0,), (0,)),
            )
            decays = lambda part: jnp.exp(jnp.where(causal, part, -1e30))
            top.append((scores[:half, :half] * decays(spread[:half, :half])).astype(bf16))
            low_left.append((scores[half:, :half] * jnp.exp(spread[half:, :half])).astype(bf16))
            low_right.append((scores[half:, half:] * decays(spread[half:, half:])).astype(bf16))
            inputs.append(jnp.where(lane_head == head, driven, 0.0).astype(bf16))
        upper_in = jnp.concatenate([d[:half] for d in inputs], axis=0)
        lower_in = jnp.concatenate([d[half:] for d in inputs], axis=0)
        upper_out = matmul(jnp.concatenate(top, axis=1), upper_in)
        lower_out = matmul(
            jnp.concatenate(low_left + low_right, axis=1),
            jnp.concatenate([upper_in, lower_in], axis=0),
        )
        within = jnp.concatenate([upper_out, lower_out], axis=0)
        held = state[...]
        scanned = within + grown * matmul(c_rows, held.astype(bf16)) + skip * values
        scanned = scanned.astype(bf16).astype(f32)
        out[block] = (scanned * silu(gate_all[block])).astype(bf16)
        injected = matmul(b_rows, (left * values).astype(bf16), ((0,), (0,)))
        state[...] = grown[rows - 1 : rows] * held + injected

    def project_step(step, carry):
        for low in range(1):
            tok_wait(1 * step + low)
            project(1 * step + low)
        return carry

    lax.fori_loop(0, ring // 1, project_step, 0)

    def advance(step, carry):
        for low in range(8):
            scan(8 * step + low)
        return carry

    lax.fori_loop(0, ring // 8, advance, 0)
    for offset, part_out in enumerate(parts):
        part_out[...] = out[me ^ offset]


def layer(head_size, tokens, columns, payloads, groups, per_head, params, g_taps, g_shift):
    ring, channels, slab = columns[0].shape
    wide = 2 * channels
    rows, depth = tokens.shape
    part = g_shift.shape[1]
    lines = per_head.shape[1]
    rim = 8
    total = ring * rows
    counts = [group[0].shape[0] for group in groups]
    pieces = [piece for group in groups for piece in group]
    shared_rows = payloads[0].shape[0] - payload_rows(tokens) * depth // LANES
    return pl.pallas_call(
        functools.partial(layer_kernel, head_size, counts),
        in_specs=[HBM] * (3 + len(payloads) + len(pieces)) + [VMEM] * 4,
        out_specs=[VMEM] * ring,
        out_shape=[jax.ShapeDtypeStruct((rows, channels), bf16)] * ring,
        scratch_shapes=[
            pltpu.VMEM((ring, depth // LANES, rows, LANES), bf16),
            pltpu.VMEM((ring, shared_rows, LANES), bf16),
            pltpu.VMEM((ring, wide, slab), bf16),
            pltpu.VMEM((ring, slab, part), bf16),
            pltpu.VMEM((ring, lines, slab), bf16),
            pltpu.VMEM((rim + total, channels), f32),
            pltpu.VMEM((rim + total, part), f32),
            pltpu.VMEM((ring, rows, channels), f32),
            pltpu.VMEM((ring, lines, rows), f32),
            pltpu.VMEM((part // 2, channels), f32),
            pltpu.VMEM((ring, rows, channels), bf16),
            pltpu.SemaphoreType.DMA((1 + 2 * ring,)),
        ],
        compiler_params=pltpu.CompilerParams(vmem_limit_bytes=60 * 1024 * 1024),
        cost_estimate=pl.CostEstimate(
            flops=2 * total * ring * slab * (wide + part),
            bytes_accessed=2 * total * ring * slab,
            transcendentals=0,
        ),
        name="layer",
    )(tokens, *columns, *payloads, *pieces, per_head, params, g_taps, g_shift)


def hold_kernel(gated, weight, held, sem):
    del gated
    copy = pltpu.make_async_copy(weight, held, sem)
    copy.start()
    copy.wait()


def hold(gated, weight):
    return pl.pallas_call(
        hold_kernel,
        in_specs=[HBM, HBM],
        out_specs=VMEM,
        out_shape=pltpu.VMEM(weight.shape, weight.dtype),
        scratch_shapes=[pltpu.SemaphoreType.DMA],
        compiler_params=pltpu.CompilerParams(vmem_limit_bytes=48 * 1024 * 1024),
        cost_estimate=pl.CostEstimate(
            flops=0, bytes_accessed=4 * weight.size, transcendentals=0
        ),
        name="hold",
    )(gated, weight)


def close_kernel(offsets, other, gain, weight, *refs):
    parts, (keep, give, inputs) = refs[:-3], refs[-3:]
    rows, width = parts[0].shape
    rows = rows // 2
    quarter = rows // 2
    columns = weight.shape[1] // 4
    me = lax.axis_index("seq")
    seat = lax.axis_index("mp")
    first = pl.multiple_of(((seat >> 1) ^ other) * rows, rows)
    square = jnp.zeros((rows, width), f32)
    for offset, part in zip(offsets, parts):
        value = part[pl.ds(first, rows)].astype(f32)
        square = square + value * value
        at = pl.multiple_of((me ^ offset) * width, width)
        inputs[:, pl.ds(at, width)] = (value * gain[:, pl.ds(at, width)]).astype(bf16)
    mean = jnp.sum(square, axis=1, keepdims=True) * (1.0 / (len(parts) * width))
    scale = lax.rsqrt(mean + norm_epsilon)
    for step in range(4):
        at = pl.ds(step * columns, columns)
        total = (matmul(inputs[...], weight[:, at]) * scale).astype(bf16)
        for core in range(2):

            @pl.when((seat & 1) == core)
            def _(core=core):
                for owner in range(2):
                    target = keep if owner == core else give
                    target[:, at] = total[owner * quarter : (owner + 1) * quarter]


def close(offsets, other, gain, weight, parts):
    rows, width = parts[0].shape
    shape = jax.ShapeDtypeStruct((rows // 4, weight.shape[1]), bf16)
    return pl.pallas_call(
        functools.partial(close_kernel, offsets, other),
        in_specs=[VMEM] * (2 + len(parts)),
        out_specs=[VMEM] * 2,
        out_shape=[shape, shape],
        scratch_shapes=[pltpu.VMEM((rows // 2, len(parts) * width), bf16)],
        compiler_params=pltpu.CompilerParams(vmem_limit_bytes=16 * 1024 * 1024),
        cost_estimate=pl.CostEstimate(
            flops=rows * weight.size, bytes_accessed=2 * weight.size, transcendentals=0
        ),
        name="close",
    )(gain, pltpu.with_memory_space_constraint(weight, pltpu.VMEM), *parts)


def tokens_travel(
    tokens,
    gate_weight,
    input_weight,
    group_weight,
    step_weight,
    step_bias,
    bucket_table,
    bucket_ids,
    decay_rate,
    conv_input,
    conv_input_bias,
    conv_group,
    conv_group_bias,
    skip_gain,
    norm_gain,
    out_weight,
):
    rows, depth = tokens.shape
    slab = gate_weight.shape[0]
    heads_here = step_bias.shape[0]
    head_size = gate_weight.shape[2]
    state_size = group_weight.shape[3]
    tap_count = conv_input.shape[0]
    ring = lax.axis_size("seq")
    seats = lax.axis_size("mp")
    me = lax.axis_index("seq")
    channels = heads_here * head_size // ring
    heads = channels // head_size
    swap = lambda size, bit: [(i, i ^ bit) for i in range(size)]
    column = lambda pairs: [(2 * a + w, 2 * b + w) for a, b in pairs for w in range(2)]

    payload = pack(
        tokens,
        group_weight.reshape(2 * slab, state_size),
        jnp.transpose(step_weight),
        bucket_ids.reshape(rows // LANES, LANES),
    )
    inner = (me >= 2) & (me < 6)
    outward = column([(1, 0), (2, 3)])
    middle = column([(1, 2), (2, 1)])
    near = lax.ppermute(payload, "seq", swap(ring, 2))
    mid = lax.ppermute(payload, "seq", middle)
    across_own = lax.ppermute(payload, "seq", swap(ring, 1))

    by_channel = lambda w: jnp.transpose(w, (1, 2, 0)).reshape(ring, channels, slab)
    trade = lambda w: lax.all_to_all(w, "seq", split_axis=0, concat_axis=0, tiled=True)
    cross = lambda item: lax.ppermute(item, "seq", swap(ring, 1))
    x_weight, gate = by_channel(input_weight), by_channel(gate_weight)
    per_head = jnp.concatenate([jnp.stack([step_bias, decay_rate]), bucket_table], axis=0)
    per_head = jnp.transpose(per_head).reshape(ring, heads, -1)
    per_head = jnp.pad(per_head, ((0, 0), (0, 8 - heads), (0, 0)))
    params = jnp.concatenate(
        [
            conv_input,
            conv_input_bias[None],
            jnp.broadcast_to(skip_gain[None, :, None], (1, heads_here, head_size)),
        ],
        axis=0,
    )
    params = jnp.moveaxis(params.reshape(params.shape[0], ring, channels), 1, 0)
    g_taps = conv_group.reshape(tap_count, 2 * state_size)
    g_shift = conv_group_bias.reshape(1, 2 * state_size)
    after = lambda value, *others: lax.optimization_barrier((value,) + others)[0]
    quarter = payload_rows(tokens)
    panels = depth // LANES

    def spread(*items):
        own = jnp.stack(
            [item[: panels * quarter].reshape(panels, quarter, LANES) for item in items]
        )
        beside = lax.ppermute(own, "mp", swap(seats, 1))
        across = lax.ppermute(own, "mp", swap(seats, 2))
        return own, beside, across, lax.ppermute(across, "mp", swap(seats, 1))

    near, mid, across_own, x_weight, per_head, params, g_taps, g_shift = lax.optimization_barrier(
        (near, mid, across_own, x_weight, per_head, params, g_taps, g_shift)
    )
    mid_far = lax.ppermute(near, "seq", middle)
    out_near = lax.ppermute(mid, "seq", outward)
    across_near = cross(near)
    x_weight = trade(x_weight)
    groups = [spread(near, across_own)]

    out_far = lax.ppermute(mid_far, "seq", outward)
    second = jnp.where(inner, mid, out_near)
    groups.append(spread(second, across_near))
    gate = trade(after(gate, mid_far, x_weight))
    third = jnp.where(inner, mid_far, out_far)
    across_second = cross(after(second, across_near))
    third = after(third, groups[0][1], groups[0][3], groups[1][2], across_second)
    across_third = cross(third)
    groups.append(spread(third, across_second))
    across_third = after(across_third, groups[1][1], groups[1][3], groups[2][2])
    groups.append(spread(across_third))
    columns = [x_weight, gate]
    payloads = [payload, across_own, near, across_near, second, across_second, third, across_third]

    gated = layer(head_size, tokens, columns, payloads, groups, per_head, params, g_taps, g_shift)
    offsets = (6, 7, 5, 4, 3, 2, 1)
    parts = [lax.ppermute(gated[at], "seq", swap(ring, at)) for at in offsets] + [gated[0]]
    gain, weight = norm_gain.reshape(1, -1), out_weight.reshape(-1, depth)
    held = hold(gated[0][:ROW_PAD], weight)
    keep, give = close(offsets + (0,), 1, gain, held, parts)
    took = lax.ppermute(give, "mp", swap(seats, 1))
    send = (keep.astype(f32) + took.astype(f32)).astype(bf16)
    keep, give = close(offsets + (0,), 0, gain, held, parts)
    took = lax.ppermute(give, "mp", swap(seats, 1))
    took_far = lax.ppermute(send, "mp", swap(seats, 2))
    return (keep.astype(f32) + took.astype(f32) + took_far.astype(f32)).astype(bf16)


def on_device(*arrays):
    tokens, gate_weight, group_weight = arrays[0], arrays[1], arrays[3]
    ring = lax.axis_size("seq")
    channels = gate_weight.shape[1] * gate_weight.shape[2] // ring
    weights = 2 * gate_weight.size + group_weight.size + arrays[4].size
    fits = (
        tokens.size <= weights
        and channels % 128 == 0
        and gate_weight.shape[0] == 2 * group_weight.shape[3] == tokens.shape[0]
        and channels % gate_weight.shape[2] == 0
        and group_weight.shape[1] == 1
        and lax.axis_size("mp") == 4
        and ring == 8
    )
    return (tokens_travel if fits else weights_travel)(*arrays)


def solution(mesh):
    placed = (
        P("seq", None),
        P("seq", "mp", None),
        P("seq", "mp", None),
        P("seq", "mp", None, None),
        P("seq", "mp"),
        P("mp"),
        P(None, "mp"),
        P("seq"),
        P("mp"),
        P(None, "mp", None),
        P("mp", None),
        P(None, "mp", None, None),
        P("mp", None, None),
        P("mp"),
        P("mp", None),
        P("mp", None, None),
    )
    return jax.shard_map(
        on_device, mesh=mesh, in_specs=placed, out_specs=P(("seq", "mp"), None), check_vma=False
    )
```

```python
import functools

import jax
import jax.numpy as jnp
from jax import lax
from jax.experimental import pallas as pl
from jax.experimental.pallas import tpu as pltpu
from jax.sharding import PartitionSpec as P

SPAN = 256
PLACE_BINS = 4


norm_epsilon = 1e-05
highest = lax.Precision.HIGHEST


def causal_conv(raw_rows, rim_rows, tap_weights, tap_bias):
    extended = jnp.concatenate([rim_rows, raw_rows], axis=0).astype(jnp.float32)
    row_count = raw_rows.shape[0]
    tap_count = tap_weights.shape[0]
    running = (
        tap_bias[None, :]
        + tap_weights[tap_count - 1][None, :] * extended[tap_count - 1 : tap_count - 1 + row_count]
    )
    for tap_index in range(tap_count - 1):
        running = (
            running + tap_weights[tap_index][None, :] * extended[tap_index : tap_index + row_count]
        )
    return jax.nn.silu(running).astype(jnp.bfloat16)


def ssd_block(carried_state, block_inputs, decay_neg):
    block_values, block_b, block_c, block_steps = block_inputs
    step_rates = block_steps.astype(jnp.float32) * decay_neg[None, :]
    cumulative = jnp.cumsum(step_rates, axis=0)
    scores = jnp.einsum("tn,sn->ts", block_c, block_b, preferred_element_type=jnp.float32)
    by_head = jnp.transpose(cumulative)
    spread = by_head[:, :, None] - by_head[:, None, :]
    block_rows = block_values.shape[0]
    causal = (jnp.arange(block_rows)[:, None] >= jnp.arange(block_rows)[None, :])[None]
    decays = jnp.where(causal, jnp.exp(jnp.where(causal, spread, 0.0)), 0.0)
    mixing = scores[None] * decays
    driven = block_steps.astype(jnp.float32)[:, :, None] * block_values.astype(jnp.float32)
    within = jnp.einsum("rts,srp->trp", mixing, driven, precision=highest)
    readout = jnp.einsum(
        "tn,rpn->trp", block_c.astype(jnp.float32), carried_state, precision=highest
    )
    outputs = within + jnp.exp(cumulative)[:, :, None] * readout
    remaining = jnp.exp(cumulative[-1][None, :] - cumulative)
    injected = jnp.einsum(
        "srp,sn->rpn",
        driven * remaining[:, :, None],
        block_b.astype(jnp.float32),
        precision=highest,
    )
    next_state = jnp.exp(cumulative[-1])[:, None, None] * carried_state + injected
    return (next_state, outputs)


def ssd_group(start_state, group_values, group_b, group_c, group_steps, decay_neg):
    row_total = group_values.shape[0]
    block_count = row_total // SPAN

    def advance(carried_state, block_inputs):
        return ssd_block(carried_state, block_inputs, decay_neg)

    blocked = (
        group_values.reshape((block_count, SPAN) + group_values.shape[1:]),
        group_b.reshape(block_count, SPAN, -1),
        group_c.reshape(block_count, SPAN, -1),
        group_steps.reshape(block_count, SPAN, -1),
    )
    final_state, outputs = lax.scan(advance, start_state, blocked)
    return (final_state, outputs.reshape((row_total,) + outputs.shape[2:]))


def weights_travel(
    tokens,
    gate_weight,
    input_weight,
    group_weight,
    step_weight,
    step_bias,
    bucket_table,
    bucket_ids,
    decay_rate,
    conv_input,
    conv_input_bias,
    conv_group,
    conv_group_bias,
    skip_gain,
    norm_gain,
    out_weight,
):
    tok_rows = tokens.shape[0]
    heads_here = step_bias.shape[0]
    groups_here = group_weight.shape[1]
    per_group = heads_here // groups_here
    head_size = gate_weight.shape[2]
    state_size = group_weight.shape[3]
    tap_count = conv_input.shape[0]
    channel_width = heads_here * head_size
    group_width = groups_here * 2 * state_size
    pieces = (
        lax.all_gather(gate_weight, "seq", axis=0, tiled=True),
        lax.all_gather(input_weight, "seq", axis=0, tiled=True),
        lax.all_gather(group_weight, "seq", axis=0, tiled=True),
        lax.all_gather(step_weight, "seq", axis=0, tiled=True),
    )
    rows_here = pieces[0].shape[0]
    gate_sum, input_sum, group_sum, step_sum = tuple(
        (
            jnp.dot(tokens, piece.reshape(rows_here, -1), preferred_element_type=jnp.float32)
            for piece in pieces
        )
    )
    gate_act = gate_sum.astype(jnp.bfloat16)
    input_raw = input_sum.astype(jnp.bfloat16)
    group_raw = group_sum.astype(jnp.bfloat16)
    onehot = (bucket_ids[:, None] == jnp.arange(PLACE_BINS, dtype=jnp.int32)[None, :]).astype(
        jnp.float32
    )
    offsets = jnp.dot(onehot, bucket_table, precision=highest)
    steps_tok = jax.nn.softplus(step_sum + step_bias[None, :] + offsets).astype(jnp.bfloat16)
    decay_neg = -decay_rate
    seq_count = lax.axis_size("seq")
    piece_width = channel_width // seq_count
    sub_width = min(piece_width, head_size)
    sub_count = piece_width // sub_width
    subs_per_head = head_size // sub_width
    steps_sub = jnp.repeat(steps_tok, subs_per_head, axis=1)
    wide_groups = jnp.broadcast_to(
        group_raw[:, None, :], (tok_rows, seq_count, group_width)
    ).reshape(tok_rows, seq_count * group_width)
    head_inputs, head_steps, head_groups = (
        lax.all_to_all(input_raw, "seq", split_axis=1, concat_axis=0, tiled=True),
        lax.all_to_all(steps_sub, "seq", split_axis=1, concat_axis=0, tiled=True),
        lax.all_to_all(wide_groups, "seq", split_axis=1, concat_axis=0, tiled=True),
    )
    seq_total = head_inputs.shape[0]
    first_channel = lax.axis_index("seq") * piece_width
    input_taps = lax.dynamic_slice_in_dim(
        conv_input.reshape(tap_count, -1), first_channel, piece_width, 1
    )
    input_shift = lax.dynamic_slice_in_dim(
        conv_input_bias.reshape(-1), first_channel, piece_width, 0
    )
    conv_values = causal_conv(
        head_inputs, jnp.zeros((tap_count - 1, piece_width), jnp.bfloat16), input_taps, input_shift
    )
    conv_groups = causal_conv(
        head_groups,
        jnp.zeros((tap_count - 1, group_width), jnp.bfloat16),
        conv_group.reshape(tap_count, -1),
        conv_group_bias.reshape(-1),
    )
    conv_groups = conv_groups.reshape(seq_total, groups_here, 2, state_size)
    sub_heads = (first_channel + jnp.arange(sub_count, dtype=jnp.int32) * sub_width) // head_size
    sub_groups = sub_heads // per_group
    sub_decay = jnp.take(decay_neg, sub_heads)[:, None]
    sub_skip = jnp.take(skip_gain, sub_heads)
    values_sub = jnp.moveaxis(conv_values.reshape(seq_total, sub_count, 1, sub_width), 1, 0)
    steps_heads = jnp.moveaxis(head_steps, 1, 0)[:, :, None]

    def run_sub(member):
        chosen = lax.dynamic_index_in_dim(conv_groups, member[3], 1, False)
        start_state = jnp.zeros((1, sub_width, state_size), jnp.float32)
        return ssd_group(start_state, member[0], chosen[:, 0], chosen[:, 1], member[1], member[2])[
            1
        ]

    scanned = jnp.moveaxis(
        lax.map(run_sub, (values_sub, steps_heads, sub_decay, sub_groups)), 0, 1
    ).reshape(seq_total, sub_count, sub_width)
    head_out = (
        scanned
        + sub_skip[None, :, None]
        * conv_values.reshape(seq_total, sub_count, sub_width).astype(jnp.float32)
    ).astype(jnp.bfloat16)
    ssd_out = lax.all_to_all(
        head_out.reshape(seq_total, piece_width), "seq", split_axis=0, concat_axis=1, tiled=True
    )
    gated_out = ssd_out.astype(jnp.float32) * jax.nn.silu(gate_act.astype(jnp.float32))
    grouped = gated_out.reshape(tok_rows, groups_here, -1)
    mean_square = jnp.mean(grouped * grouped, axis=2)
    scales = lax.rsqrt(mean_square + norm_epsilon)
    normed = (
        (grouped * scales[:, :, None]).reshape(tok_rows, -1) * norm_gain.reshape(-1)[None, :]
    ).astype(jnp.bfloat16)
    flat_out = out_weight.reshape(-1, out_weight.shape[2])
    layer_out = lax.psum_scatter(
        jnp.dot(normed, flat_out, preferred_element_type=jnp.float32).astype(jnp.bfloat16),
        "mp",
        scatter_dimension=0,
        tiled=True,
    )
    return layer_out


bf16 = jnp.bfloat16
f32 = jnp.float32
ROW_PAD = 16
LANES = 128


def matmul(left, right, dims=((1,), (0,))):
    return lax.dot_general(left, right, (dims, ((), ())), preferred_element_type=f32)


def softplus(value):
    return jnp.maximum(value, 0.0) + jnp.log1p(jnp.exp(-jnp.abs(value)))


def silu(value):
    return 0.5 * value * (1.0 + jnp.tanh(0.5 * value))


def parts_of(value, count):
    parts = []
    for _ in range(count):
        part = value.astype(bf16).astype(f32)
        parts.append(part)
        value = value - part
    return parts


HBM = pl.BlockSpec(memory_space=pl.ANY)
VMEM = pl.BlockSpec(memory_space=pltpu.VMEM)


def pack_kernel(tokens, groups, steps, ids, payload, mine, sem):
    rows, depth = mine.shape
    seat = lax.axis_index("mp")
    copy = pltpu.make_async_copy(
        tokens.at[pl.ds(pl.multiple_of(seat * rows, rows), rows)], mine, sem
    )
    copy.start()
    panels = depth // LANES
    low = panels * rows
    payload[low : low + groups.shape[0]] = groups[...]
    low += groups.shape[0]
    high = steps.shape[0]
    for part in range(steps.shape[1] // LANES):
        payload[low : low + high] = steps[:, part * LANES : (part + 1) * LANES]
        low += high
    marks = ids[...].astype(f32)
    rest = jnp.zeros((ROW_PAD - marks.shape[0], LANES), f32)
    payload[low:] = jnp.concatenate([marks, rest], axis=0).astype(bf16)
    copy.wait()
    for panel in range(panels):
        payload[panel * rows : (panel + 1) * rows] = mine[:, panel * LANES : (panel + 1) * LANES]


def payload_rows(tokens):
    return tokens.shape[0] // 4


def pack(tokens, groups, steps, ids):
    rows, depth = tokens.shape
    extra = steps.size // LANES + ROW_PAD
    full = payload_rows(tokens) * depth // LANES + groups.shape[0] + extra
    return pl.pallas_call(
        pack_kernel,
        in_specs=[HBM, VMEM, VMEM, VMEM],
        out_specs=VMEM,
        out_shape=jax.ShapeDtypeStruct((full, LANES), bf16),
        scratch_shapes=[
            pltpu.VMEM((payload_rows(tokens), depth), bf16),
            pltpu.SemaphoreType.DMA,
        ],
        name="pack",
    )(tokens, groups, steps, ids)


def layer_kernel(head_size, counts, tokens, *refs):
    columns, refs = refs[:2], refs[2:]
    ring, channels, slab = columns[0].shape
    payloads, refs = refs[:ring], refs[ring:]
    pieces, refs = refs[: 4 * len(counts)], refs[4 * len(counts) :]
    per_head_all, params_all, g_taps, g_shift = refs[:4]
    parts, refs = refs[4 : 4 + ring], refs[4 + ring :]
    tok, shared, w_x, w_group, w_step, x_all, g_all, gate_all, step_all, state, out, sems = refs
    seats = 4
    rows = parts[0].shape[0]
    quarter = rows // seats
    panels = tok.shape[1]
    height = panels * quarter
    part = 2 * g_shift.shape[1] // 2
    states = part // 2
    heads = channels // head_size
    lines = w_step.shape[1]
    tap_count = g_taps.shape[0]
    rim = x_all.shape[0] - ring * rows
    step_rows = shared.shape[1] - 2 * slab - ROW_PAD
    step_heads = step_rows * LANES // slab
    me = lax.axis_index("seq")
    seat = lax.axis_index("mp")
    beside = me & 1
    upper_half = me >> 2
    sources = [me, me ^ 1]
    for other in ((me >> 1) ^ 1, 2 - upper_half, 3 - 3 * upper_half):
        sources += [2 * other + beside, 2 * other + 1 - beside]

    arrivals = [2, 1, 4, 3, 6, 5, 7]
    shared_copies = []
    for order in range(ring):
        copy = pltpu.make_async_copy(
            payloads[order].at[pl.ds(height, shared.shape[1])],
            shared.at[sources[order]],
            sems.at[1 + ring + order],
        )
        copy.start()
        shared_copies.append(copy)
    for kind in range(2):
        pltpu.make_async_copy(
            columns[kind], w_x.at[:, pl.ds(kind * channels, channels)], sems.at[0]
        ).start()
    for panel in range(panels):
        pltpu.make_async_copy(
            tokens.at[:, pl.ds(panel * LANES, LANES)], tok.at[me, panel], sems.at[1 + me]
        ).start()
    order = 0
    for group, count in enumerate(counts):
        for at in range(count):
            source = sources[arrivals[order]]
            for hop in range(seats):
                first = pl.multiple_of((seat ^ hop) * quarter, quarter)
                pltpu.make_async_copy(
                    pieces[4 * group + hop].at[at],
                    tok.at[source, :, pl.ds(first, quarter)],
                    sems.at[1 + source],
                ).start()
            order += 1

    x_all[:rim] = jnp.zeros((rim, channels), f32)
    g_all[:rim] = jnp.zeros((rim, part), f32)
    state[...] = jnp.zeros_like(state)
    one = lambda flag: flag.astype(f32).astype(bf16)
    iota = lambda shape, dim: lax.broadcasted_iota(jnp.int32, shape, dim)
    pick = one(
        (iota((lines, step_heads), 0) + me * heads == iota((lines, step_heads), 1))
        & (iota((lines, step_heads), 0) < heads)
    )
    unpick = [
        one(2 * iota((slab, 2 * slab), 0) + kind == iota((slab, 2 * slab), 1)) for kind in range(2)
    ]
    for copy in shared_copies:
        copy.wait()
    for panel in range(ring):
        slab_rows = shared[panel, : 2 * slab]
        for kind in range(2):
            w_group[panel, :, kind * states : (kind + 1) * states] = matmul(
                unpick[kind], slab_rows
            ).astype(bf16)
        step_panel = jnp.concatenate(
            [
                shared[panel, 2 * slab + low : 2 * slab + low + step_heads]
                for low in range(0, step_rows, step_heads)
            ],
            axis=1,
        )
        w_step[panel] = matmul(pick, step_panel).astype(bf16)
    pltpu.make_async_copy(w_x, w_x, sems.at[0]).wait()

    upper = one(iota((rows, rows), 0) <= iota((rows, rows), 1))
    widen = one(iota((lines, channels), 1) // head_size == iota((lines, channels), 0))
    half = rows // 2
    causal = iota((half, half), 0) >= iota((half, half), 1)
    lane_head = iota((rows, channels), 1) // head_size
    per_head = per_head_all[me]
    params = params_all[me]
    bias, decay = per_head[:, 0:1], per_head[:, 1:2]
    skip = params[tap_count + 1 : tap_count + 2]

    def tok_wait(block):
        pltpu.make_async_copy(tok.at[block], tok.at[block], sems.at[1 + block]).wait()

    def project(block):
        total_x = total_g = total_s = None
        each = panels // ring
        for panel in range(ring):
            piece = jnp.concatenate(
                [tok[block, panel * each + low] for low in range(each)], axis=1
            )
            term_x = matmul(piece, w_x[panel], ((1,), (1,)))
            term_g = matmul(piece, w_group[panel])
            term_s = matmul(w_step[panel], piece, ((1,), (1,)))
            total_x = term_x if total_x is None else total_x + term_x
            total_g = term_g if total_g is None else total_g + term_g
            total_s = term_s if total_s is None else total_s + term_s
        base = pl.multiple_of(block * rows, rows)
        x_all[pl.ds(base + rim, rows)] = total_x[:, :channels].astype(bf16).astype(f32)
        gate_all[block] = total_x[:, channels:].astype(bf16).astype(f32)
        g_all[pl.ds(base + rim, rows)] = total_g.astype(bf16).astype(f32)
        step_all[block] = total_s

    def conv(ref, base, taps, shift):
        window = ref[pl.ds(base, rows + rim)]
        first = rim - tap_count + 1
        running = shift
        for tap in range(tap_count):
            running = running + taps[tap : tap + 1] * window[first + tap : first + tap + rows]
        return silu(running).astype(bf16)

    def stretch(value, count):
        low = jnp.concatenate(parts_of(value, count), axis=0).astype(bf16)
        return matmul(low, jnp.concatenate([widen] * count, axis=0), ((0,), (0,)))

    def scan(block):
        base = pl.multiple_of(block * rows, rows)
        values = conv(x_all, base, params[:tap_count], params[tap_count : tap_count + 1])
        values = values.astype(f32)
        groups = conv(g_all, base, g_taps[...], g_shift[...])
        b_rows, c_rows = groups[:, :states], groups[:, states:]
        marks = shared[block, 2 * slab + step_rows :].astype(f32)
        bucket = jnp.concatenate(
            [marks[low : low + 1] for low in range(rows // LANES)], axis=1
        )
        raw_step = step_all[block] + bias
        for entry in range(PLACE_BINS):
            raw_step = raw_step + jnp.where(
                bucket == float(entry), per_head[:, 2 + entry : 3 + entry], 0.0
            )
        sizes = softplus(raw_step).astype(bf16).astype(f32)
        rates = jnp.concatenate(parts_of(-decay * sizes, 3), axis=0).astype(bf16)
        sums = matmul(rates, upper)
        cumulative = sums[:lines] + (sums[lines : 2 * lines] + sums[2 * lines :])
        last = cumulative[:, rows - 1 : rows]
        grown = stretch(jnp.exp(cumulative), 3)
        left = stretch(sizes * jnp.exp(last - cumulative), 3)
        driven = (stretch(sizes, 1) * values).astype(f32)
        scores = matmul(c_rows, b_rows, ((1,), (1,)))
        cum_parts = parts_of(cumulative, 3)
        ones = jnp.ones((3, rows), f32)
        pad = jnp.zeros((2, rows), f32)
        top, low_left, low_right, inputs = [], [], [], []
        for head in range(heads):
            mine = jnp.concatenate([p[head : head + 1] for p in cum_parts], axis=0)
            spread = matmul(
                jnp.concatenate([mine, ones, pad], axis=0).astype(bf16),
                jnp.concatenate([ones, -mine, pad], axis=0).astype(bf16),
                ((0,), (0,)),
            )
            decays = lambda part: jnp.exp(jnp.where(causal, part, -1e30))
            top.append((scores[:half, :half] * decays(spread[:half, :half])).astype(bf16))
            low_left.append((scores[half:, :half] * jnp.exp(spread[half:, :half])).astype(bf16))
            low_right.append((scores[half:, half:] * decays(spread[half:, half:])).astype(bf16))
            inputs.append(jnp.where(lane_head == head, driven, 0.0).astype(bf16))
        upper_in = jnp.concatenate([d[:half] for d in inputs], axis=0)
        lower_in = jnp.concatenate([d[half:] for d in inputs], axis=0)
        upper_out = matmul(jnp.concatenate(top, axis=1), upper_in)
        lower_out = matmul(
            jnp.concatenate(low_left + low_right, axis=1),
            jnp.concatenate([upper_in, lower_in], axis=0),
        )
        within = jnp.concatenate([upper_out, lower_out], axis=0)
        held = state[...]
        scanned = within + grown * matmul(c_rows, held.astype(bf16)) + skip * values
        scanned = scanned.astype(bf16).astype(f32)
        out[block] = (scanned * silu(gate_all[block])).astype(bf16)
        injected = matmul(b_rows, (left * values).astype(bf16), ((0,), (0,)))
        state[...] = grown[rows - 1 : rows] * held + injected

    def project_step(step, carry):
        for low in range(1):
            tok_wait(1 * step + low)
            project(1 * step + low)
        return carry

    lax.fori_loop(0, ring // 1, project_step, 0)

    def advance(step, carry):
        for low in range(8):
            scan(8 * step + low)
        return carry

    lax.fori_loop(0, ring // 8, advance, 0)
    for offset, part_out in enumerate(parts):
        part_out[...] = out[me ^ offset]


def layer(head_size, tokens, columns, payloads, groups, per_head, params, g_taps, g_shift):
    ring, channels, slab = columns[0].shape
    wide = 2 * channels
    rows, depth = tokens.shape
    part = g_shift.shape[1]
    lines = per_head.shape[1]
    rim = 8
    total = ring * rows
    counts = [group[0].shape[0] for group in groups]
    pieces = [piece for group in groups for piece in group]
    shared_rows = payloads[0].shape[0] - payload_rows(tokens) * depth // LANES
    return pl.pallas_call(
        functools.partial(layer_kernel, head_size, counts),
        in_specs=[HBM] * (3 + len(payloads) + len(pieces)) + [VMEM] * 4,
        out_specs=[VMEM] * ring,
        out_shape=[jax.ShapeDtypeStruct((rows, channels), bf16)] * ring,
        scratch_shapes=[
            pltpu.VMEM((ring, depth // LANES, rows, LANES), bf16),
            pltpu.VMEM((ring, shared_rows, LANES), bf16),
            pltpu.VMEM((ring, wide, slab), bf16),
            pltpu.VMEM((ring, slab, part), bf16),
            pltpu.VMEM((ring, lines, slab), bf16),
            pltpu.VMEM((rim + total, channels), f32),
            pltpu.VMEM((rim + total, part), f32),
            pltpu.VMEM((ring, rows, channels), f32),
            pltpu.VMEM((ring, lines, rows), f32),
            pltpu.VMEM((part // 2, channels), f32),
            pltpu.VMEM((ring, rows, channels), bf16),
            pltpu.SemaphoreType.DMA((1 + 2 * ring,)),
        ],
        compiler_params=pltpu.CompilerParams(vmem_limit_bytes=60 * 1024 * 1024),
        cost_estimate=pl.CostEstimate(
            flops=2 * total * ring * slab * (wide + part),
            bytes_accessed=2 * total * ring * slab,
            transcendentals=0,
        ),
        name="layer",
    )(tokens, *columns, *payloads, *pieces, per_head, params, g_taps, g_shift)


def hold_kernel(gated, weight, held, sem):
    del gated
    copy = pltpu.make_async_copy(weight, held, sem)
    copy.start()
    copy.wait()


def hold(gated, weight):
    return pl.pallas_call(
        hold_kernel,
        in_specs=[HBM, HBM],
        out_specs=VMEM,
        out_shape=pltpu.VMEM(weight.shape, weight.dtype),
        scratch_shapes=[pltpu.SemaphoreType.DMA],
        compiler_params=pltpu.CompilerParams(vmem_limit_bytes=48 * 1024 * 1024),
        cost_estimate=pl.CostEstimate(
            flops=0, bytes_accessed=4 * weight.size, transcendentals=0
        ),
        name="hold",
    )(gated, weight)


def close_kernel(offsets, other, gain, weight, *refs):
    parts, (keep, give, inputs) = refs[:-3], refs[-3:]
    rows, width = parts[0].shape
    rows = rows // 2
    quarter = rows // 2
    columns = weight.shape[1] // 4
    me = lax.axis_index("seq")
    seat = lax.axis_index("mp")
    first = pl.multiple_of(((seat >> 1) ^ other) * rows, rows)
    square = jnp.zeros((rows, width), f32)
    for offset, part in zip(offsets, parts):
        value = part[pl.ds(first, rows)].astype(f32)
        square = square + value * value
        at = pl.multiple_of((me ^ offset) * width, width)
        inputs[:, pl.ds(at, width)] = (value * gain[:, pl.ds(at, width)]).astype(bf16)
    mean = jnp.sum(square, axis=1, keepdims=True) * (1.0 / (len(parts) * width))
    scale = lax.rsqrt(mean + norm_epsilon)
    for step in range(4):
        at = pl.ds(step * columns, columns)
        total = (matmul(inputs[...], weight[:, at]) * scale).astype(bf16)
        for core in range(2):

            @pl.when((seat & 1) == core)
            def _(core=core):
                for owner in range(2):
                    target = keep if owner == core else give
                    target[:, at] = total[owner * quarter : (owner + 1) * quarter]


def close(offsets, other, gain, weight, parts):
    rows, width = parts[0].shape
    shape = jax.ShapeDtypeStruct((rows // 4, weight.shape[1]), bf16)
    return pl.pallas_call(
        functools.partial(close_kernel, offsets, other),
        in_specs=[VMEM] * (2 + len(parts)),
        out_specs=[VMEM] * 2,
        out_shape=[shape, shape],
        scratch_shapes=[pltpu.VMEM((rows // 2, len(parts) * width), bf16)],
        compiler_params=pltpu.CompilerParams(vmem_limit_bytes=16 * 1024 * 1024),
        cost_estimate=pl.CostEstimate(
            flops=rows * weight.size, bytes_accessed=2 * weight.size, transcendentals=0
        ),
        name="close",
    )(gain, pltpu.with_memory_space_constraint(weight, pltpu.VMEM), *parts)


def tokens_travel(
    tokens,
    gate_weight,
    input_weight,
    group_weight,
    step_weight,
    step_bias,
    bucket_table,
    bucket_ids,
    decay_rate,
    conv_input,
    conv_input_bias,
    conv_group,
    conv_group_bias,
    skip_gain,
    norm_gain,
    out_weight,
):
    rows, depth = tokens.shape
    slab = gate_weight.shape[0]
    heads_here = step_bias.shape[0]
    head_size = gate_weight.shape[2]
    state_size = group_weight.shape[3]
    tap_count = conv_input.shape[0]
    ring = lax.axis_size("seq")
    seats = lax.axis_size("mp")
    me = lax.axis_index("seq")
    channels = heads_here * head_size // ring
    heads = channels // head_size
    swap = lambda size, bit: [(i, i ^ bit) for i in range(size)]
    column = lambda pairs: [(2 * a + w, 2 * b + w) for a, b in pairs for w in range(2)]

    payload = pack(
        tokens,
        group_weight.reshape(2 * slab, state_size),
        jnp.transpose(step_weight),
        bucket_ids.reshape(rows // LANES, LANES),
    )
    inner = (me >= 2) & (me < 6)
    outward = column([(1, 0), (2, 3)])
    middle = column([(1, 2), (2, 1)])
    near = lax.ppermute(payload, "seq", swap(ring, 2))
    mid = lax.ppermute(payload, "seq", middle)
    across_own = lax.ppermute(payload, "seq", swap(ring, 1))

    by_channel = lambda w: jnp.transpose(w, (1, 2, 0)).reshape(ring, channels, slab)
    trade = lambda w: lax.all_to_all(w, "seq", split_axis=0, concat_axis=0, tiled=True)
    cross = lambda item: lax.ppermute(item, "seq", swap(ring, 1))
    x_weight, gate = by_channel(input_weight), by_channel(gate_weight)
    per_head = jnp.concatenate([jnp.stack([step_bias, decay_rate]), bucket_table], axis=0)
    per_head = jnp.transpose(per_head).reshape(ring, heads, -1)
    per_head = jnp.pad(per_head, ((0, 0), (0, 8 - heads), (0, 0)))
    params = jnp.concatenate(
        [
            conv_input,
            conv_input_bias[None],
            jnp.broadcast_to(skip_gain[None, :, None], (1, heads_here, head_size)),
        ],
        axis=0,
    )
    params = jnp.moveaxis(params.reshape(params.shape[0], ring, channels), 1, 0)
    g_taps = conv_group.reshape(tap_count, 2 * state_size)
    g_shift = conv_group_bias.reshape(1, 2 * state_size)
    after = lambda value, *others: lax.optimization_barrier((value,) + others)[0]
    quarter = payload_rows(tokens)
    panels = depth // LANES

    def spread(*items):
        own = jnp.stack(
            [item[: panels * quarter].reshape(panels, quarter, LANES) for item in items]
        )
        beside = lax.ppermute(own, "mp", swap(seats, 1))
        across = lax.ppermute(own, "mp", swap(seats, 2))
        return own, beside, across, lax.ppermute(across, "mp", swap(seats, 1))

    near, mid, across_own, x_weight, per_head, params, g_taps, g_shift = lax.optimization_barrier(
        (near, mid, across_own, x_weight, per_head, params, g_taps, g_shift)
    )
    mid_far = lax.ppermute(near, "seq", middle)
    out_near = lax.ppermute(mid, "seq", outward)
    across_near = cross(near)
    x_weight = trade(x_weight)
    groups = [spread(near, across_own)]

    mid_far = after(mid_far, groups[0][1])
    out_far = lax.ppermute(mid_far, "seq", outward)
    second = jnp.where(inner, mid, out_near)
    groups.append(spread(second, across_near))
    gate = trade(after(gate, mid_far, x_weight))
    third = jnp.where(inner, mid_far, out_far)
    across_second = cross(after(second, across_near))
    third = after(third, groups[0][1], groups[0][3], groups[1][2], across_second)
    across_third = cross(third)
    groups.append(spread(third, across_second))
    across_third = after(across_third, groups[1][1], groups[1][3], groups[2][2])
    groups.append(spread(across_third))
    columns = [x_weight, gate]
    payloads = [payload, across_own, near, across_near, second, across_second, third, across_third]

    gated = layer(head_size, tokens, columns, payloads, groups, per_head, params, g_taps, g_shift)
    offsets = (6, 7, 5, 4, 3, 2, 1)
    parts = [lax.ppermute(gated[at], "seq", swap(ring, at)) for at in offsets] + [gated[0]]
    gain, weight = norm_gain.reshape(1, -1), out_weight.reshape(-1, depth)
    held = hold(gated[0][:ROW_PAD], weight)
    keep, give = close(offsets + (0,), 1, gain, held, parts)
    took = lax.ppermute(give, "mp", swap(seats, 1))
    send = (keep.astype(f32) + took.astype(f32)).astype(bf16)
    keep, give = close(offsets + (0,), 0, gain, held, parts)
    took = lax.ppermute(give, "mp", swap(seats, 1))
    took_far = lax.ppermute(send, "mp", swap(seats, 2))
    return (keep.astype(f32) + took.astype(f32) + took_far.astype(f32)).astype(bf16)


def on_device(*arrays):
    tokens, gate_weight, group_weight = arrays[0], arrays[1], arrays[3]
    ring = lax.axis_size("seq")
    channels = gate_weight.shape[1] * gate_weight.shape[2] // ring
    weights = 2 * gate_weight.size + group_weight.size + arrays[4].size
    fits = (
        tokens.size <= weights
        and channels % 128 == 0
        and gate_weight.shape[0] == 2 * group_weight.shape[3] == tokens.shape[0]
        and channels % gate_weight.shape[2] == 0
        and group_weight.shape[1] == 1
        and lax.axis_size("mp") == 4
        and ring == 8
    )
    return (tokens_travel if fits else weights_travel)(*arrays)


def solution(mesh):
    placed = (
        P("seq", None),
        P("seq", "mp", None),
        P("seq", "mp", None),
        P("seq", "mp", None, None),
        P("seq", "mp"),
        P("mp"),
        P(None, "mp"),
        P("seq"),
        P("mp"),
        P(None, "mp", None),
        P("mp", None),
        P(None, "mp", None, None),
        P("mp", None, None),
        P("mp"),
        P("mp", None),
        P("mp", None, None),
    )
    return jax.shard_map(
        on_device, mesh=mesh, in_specs=placed, out_specs=P(("seq", "mp"), None), check_vma=False
    )
```
